32 devices in a mesh: dp: 16 (over z, y, core), rows: 2 (over x).
Axes of the slice: x: 2, y: 2, z: 4, core: 2. Of those that a mesh axis runs over, the one named last changes fastest.
Arguments:
- image_in: bfloat16 [16, 8, 448, 128], P('dp', 'rows'), may hold values from -6 to 6
- noise_in: bfloat16 [16, 8, 448, 128], P('dp', 'rows'), may hold values from -6 to 6
- sigma_in: float32 [16], P('dp'), may hold values from 0.1 to 4
- embedding: bfloat16 [16, 512], P('dp'), may hold values from -6 to 6
- features: bfloat16 [16, 784, 256], P('dp', 'rows'), may hold values from -6 to 6
- norm1_gain: float32 [128], replicated, may hold values from 0.1 to 1.9
- norm1_bias: float32 [128], replicated, may hold values from -3 to 3
- conv1_w: bfloat16 [3, 3, 128, 256], replicated, may hold values from -0.1875 to 0.1875
- film_w: bfloat16 [512, 512], replicated, may hold values from -0.25 to 0.25
- film_b: float32 [512], replicated, may hold values from -2 to 2
- norm2_gain: float32 [256], replicated, may hold values from 0.1 to 1.9
- norm2_bias: float32 [256], replicated, may hold values from -3 to 3
- conv2_w: bfloat16 [3, 3, 256, 256], replicated, may hold values from -0.125 to 0.125
- skip_w: bfloat16 [128, 256], replicated, may hold values from -0.5 to 0.5
- down_w: bfloat16 [3, 3, 256, 256], replicated, may hold values from -0.125 to 0.125
- qkv_w: bfloat16 [256, 768], replicated, may hold values from -0.375 to 0.375
- proj_w: bfloat16 [256, 256], replicated, may hold values from -3 to 3
- down_cot: bfloat16 [16, 4, 224, 256], P('dp', 'rows'), may hold values from -6 to 6
- attn_cot: bfloat16 [16, 784, 256], P('dp', 'rows'), may hold values from -6 to 6
Outputs:
- block_out: bfloat16 [16, 4, 224, 256], P('dp', 'rows')
- attended: bfloat16 [16, 784, 256], P('dp', 'rows')
- image_grad: float32 [16, 8, 448, 128], P('dp', 'rows')
- features_grad: float32 [16, 784, 256], P('dp', 'rows')
- norm1_gain_grad: float32 [128], replicated
- norm1_bias_grad: float32 [128], replicated
- conv1_w_grad: float32 [3, 3, 128, 256], replicated
- film_w_grad: float32 [512, 512], replicated
- film_b_grad: float32 [512], replicated
- norm2_gain_grad: float32 [256], replicated
- norm2_bias_grad: float32 [256], replicated
- conv2_w_grad: float32 [3, 3, 256, 256], replicated
- skip_w_grad: float32 [128, 256], replicated
- down_w_grad: float32 [3, 3, 256, 256], replicated
- qkv_w_grad: float32 [256, 768], replicated
- proj_w_grad: float32 [256, 256], replicated
The draws below stay inside these ranges and needn't reach their ends.
All inputs are finite; a program needn't handle non-finite values.
Results may differ from the reference program's by a relative error of at most 0.011.
Values may be sent and summed in bfloat16 or wider, within the bound.
A program may use at most 128 MiB of HBM per device.

```python
import math
import jax
import jax.numpy as jnp
from jax import lax

C_IN = 128
C = 256
EMB = 512
G = 32
W = 448
H = 8
TOK = 784
SAMPLES = 16


def levels(stream_key, shape, cuts, least, largest):
    def one(position, parts):
        draws = jax.random.uniform(jax.random.fold_in(jax.random.fold_in(stream_key, 6), position), (parts,), jnp.float32, least / len(cuts), largest / len(cuts))
        return jnp.repeat(jnp.exp(draws), shape[position] // parts).reshape((-1,) + (1,) * (len(shape) - position - 1))

    factor_of = one(*cuts[0])
    for cut in cuts[1:]:
        factor_of = factor_of * one(*cut)
    return factor_of


def normal_values(key, dims, width, reach, pieces=(), dtype=jnp.bfloat16):
    array = width * jax.random.normal(key, dims, jnp.float32)
    if pieces:
        array = array * levels(key, dims, pieces, -0.22, 0.18)
    return jnp.clip(array, -reach, reach).astype(dtype)


def setup_inputs(seed: int = 0) -> dict:
    streams_of = jax.random.split(jax.random.key(seed), 20)
    image_in = normal_values(streams_of[0], (SAMPLES, H, W, C_IN), 1.0, 6.0, ((0, 16), (1, 2)))
    noise_in = normal_values(streams_of[1], (SAMPLES, H, W, C_IN), 1.0, 6.0, ((0, 16), (1, 2)))
    sigma_in = jnp.clip(jnp.exp(math.log(4.0) - 3.6888794 * jax.random.uniform(streams_of[2], (SAMPLES,), jnp.float32) ** levels(streams_of[2], (SAMPLES,), ((0, 16),), -0.2, 0.2)), 0.1, 4.0)
    embedding = normal_values(streams_of[3], (SAMPLES, EMB), 1.0, 6.0, ((0, 16),))
    features = normal_values(streams_of[4], (SAMPLES, TOK, C), 1.0, 6.0, ((0, 16), (1, 2)))
    norm1_gain = jnp.clip(1.0 + 0.18 * jax.random.normal(streams_of[5], (C_IN,), jnp.float32), 0.1, 1.9)
    norm1_bias = normal_values(streams_of[6], (C_IN,), 0.5, 3.0, (), jnp.float32)
    conv1_w = normal_values(streams_of[7], (3, 3, C_IN, C), (9 * C_IN) ** -0.5, 0.1875)
    film_w = normal_values(streams_of[8], (EMB, 2 * C), EMB ** -0.5, 0.25)
    film_b = normal_values(streams_of[9], (2 * C,), 0.3, 2.0, (), jnp.float32)
    norm2_gain = jnp.clip(1.0 + 0.18 * jax.random.normal(streams_of[10], (C,), jnp.float32), 0.1, 1.9)
    norm2_bias = normal_values(streams_of[11], (C,), 0.5, 3.0, (), jnp.float32)
    conv2_w = normal_values(streams_of[12], (3, 3, C, C), (9 * C) ** -0.5, 0.125)
    skip_w = normal_values(streams_of[13], (C_IN, C), C_IN ** -0.5, 0.5)
    down_w = normal_values(streams_of[14], (3, 3, C, C), (9 * C) ** -0.5, 0.125)
    qkv_w = normal_values(streams_of[15], (C, 3 * C), C ** -0.5, 0.375)
    proj_w = normal_values(streams_of[16], (C, C), 4 ** -0.5, 3.0)
    down_cot = normal_values(streams_of[17], (SAMPLES, H // 2, W // 2, C), 1.0, 6.0, ((0, 16), (1, 2)))
    attn_cot = normal_values(streams_of[18], (SAMPLES, TOK, C), 1.0, 6.0, ((0, 16), (1, 2)))
    return {"image_in": image_in, "noise_in": noise_in, "sigma_in": sigma_in, "embedding": embedding, "features": features, "norm1_gain": norm1_gain, "norm1_bias": norm1_bias, "conv1_w": conv1_w, "film_w": film_w, "film_b": film_b, "norm2_gain": norm2_gain, "norm2_bias": norm2_bias, "conv2_w": conv2_w, "skip_w": skip_w, "down_w": down_w, "qkv_w": qkv_w, "proj_w": proj_w, "down_cot": down_cot, "attn_cot": attn_cot}


EPSILON = 1e-05
SIGMA_DATA = 0.5
PRECISE = lax.Precision.HIGHEST
NUMBERS = ('NHWC', 'HWIO', 'NHWC')

@jax.custom_vjp
def low(v):
    return lax.optimization_barrier(v.astype(jnp.bfloat16)).astype(jnp.float32)

@jax.custom_vjp
def low_back(v):
    return v

def low_keep(v):
    return (low(v), None)

def low_pass(kept, grad):
    return (grad,)

def back_keep(v):
    return (v, None)

def back_low(kept, grad):
    return (low(grad),)
low.defvjp(low_keep, low_pass)
low_back.defvjp(back_keep, back_low)

def group_norm(field_in, gain_val, bias_val):
    split = field_in.reshape(field_in.shape[0], field_in.shape[1], G, field_in.shape[2] // G)
    mean_val = lax.optimization_barrier(jnp.mean(split, axis=(0, 1, 3)))
    square_mean = lax.optimization_barrier(jnp.mean(split * split, axis=(0, 1, 3)))
    inverse = lax.rsqrt(square_mean - mean_val * mean_val + EPSILON)
    normed = (split - mean_val[:, None]) * inverse[:, None]
    return normed.reshape(field_in.shape) * gain_val + bias_val

def conv_stride(field_in, weight, stride):
    return lax.conv_general_dilated(field_in[None], weight, (stride, stride), ((1, 1), (1, 1)), dimension_numbers=NUMBERS, precision=PRECISE)[0]

def sample_forward(params, image_val, feature_val, sigma_val, noise_val, embed_val):
    norm1_gain, norm1_bias, conv1_w, film_w, film_b, norm2_gain, norm2_bias, conv2_w, skip_w, down_w, qkv_w, proj_w = params
    channels = conv1_w.shape[3]
    scale_in = lax.rsqrt(SIGMA_DATA * SIGMA_DATA + sigma_val * sigma_val)
    shifted_in = scale_in * (image_val + sigma_val * noise_val)
    hidden_one = low(jax.nn.silu(group_norm(shifted_in, norm1_gain, norm1_bias)))
    conv_one = low_back(conv_stride(hidden_one, conv1_w, 1))
    film_out = jnp.dot(embed_val, film_w, precision=PRECISE) + film_b
    modulated = group_norm(conv_one, norm2_gain, norm2_bias) * (1.0 + film_out[:channels]) + film_out[channels:]
    hidden_two = low(jax.nn.silu(modulated))
    skip_out = jnp.einsum('hwc,cd->hwd', low(shifted_in), skip_w, precision=PRECISE)
    summed = low(low_back(conv_stride(hidden_two, conv2_w, 1) + skip_out))
    down_out = conv_stride(summed, down_w, 2)
    projected = jnp.dot(feature_val, qkv_w, precision=PRECISE)
    queries = low_back(low(projected[:, :channels]))
    keys_all = low_back(low(projected[:, channels:2 * channels]))
    values_all = low_back(low(projected[:, 2 * channels:]))
    scores = low_back(jnp.dot(queries, keys_all.T, precision=PRECISE) * channels ** (-0.5))
    weights = jax.nn.softmax(scores, axis=-1)
    mixed_out = low(low_back(jnp.dot(low(weights), values_all, precision=PRECISE)))
    attended = feature_val + jnp.dot(mixed_out, proj_w, precision=PRECISE)
    return (down_out, attended)

def reference(image_in, noise_in, sigma_in, embedding, features, norm1_gain, norm1_bias, conv1_w, film_w, film_b, norm2_gain, norm2_bias, conv2_w, skip_w, down_w, qkv_w, proj_w, down_cot, attn_cot):
    params = tuple((weight.astype(jnp.float32) for weight in (norm1_gain, norm1_bias, conv1_w, film_w, film_b, norm2_gain, norm2_bias, conv2_w, skip_w, down_w, qkv_w, proj_w)))

    def sample_step(totals, inputs):
        image_one, noise_one, sigma_one, embed_one, feature_one, down_one, attn_one = inputs

        def forward(weights, image_val, feature_val):
            return sample_forward(weights, image_val, feature_val, sigma_one, noise_one.astype(jnp.float32), embed_one.astype(jnp.float32))
        outputs, pullback = jax.vjp(forward, params, image_one.astype(jnp.float32), feature_one.astype(jnp.float32))
        param_grads, image_back, feature_back = pullback((down_one.astype(jnp.float32), attn_one.astype(jnp.float32)))
        totals = tuple((running + added for running, added in zip(totals, param_grads)))
        return (totals, (outputs[0].astype(jnp.bfloat16), outputs[1].astype(jnp.bfloat16), image_back, feature_back))
    starting = tuple((jnp.zeros_like(weight) for weight in params))
    totals, stacked = lax.scan(sample_step, starting, (image_in, noise_in, sigma_in, embedding, features, down_cot, attn_cot))
    return (stacked[0], stacked[1], stacked[2], stacked[3], totals[0], totals[1], totals[2], totals[3], totals[4], totals[5], totals[6], totals[7], totals[8], totals[9], totals[10], totals[11])
```

```python
import jax
import jax.numpy as jnp
from jax import lax
from jax.experimental import pallas as pl
from jax.experimental.pallas import tpu as pltpu
from jax.sharding import PartitionSpec as P

G = 32


EPSILON = 1e-05
SIGMA_DATA = 0.5
NUMBERS = ("NHWC", "HWIO", "NHWC")


def padded_2(block, sides, width):
    for axis, dim in sides:
        count = lax.axis_size(axis)
        forward = [(i, i + 1) for i in range(count - 1)]
        backward = [(target, source) for source, target in forward]
        low = lax.ppermute(
            lax.slice_in_dim(block, block.shape[dim] - width, None, axis=dim), axis, forward
        )
        high = lax.ppermute(lax.slice_in_dim(block, 0, width, axis=dim), axis, backward)
        block = jnp.concatenate([low, block, high], axis=dim)
    return block


def shifted(block, axis, distance):
    devices = range(lax.axis_size(axis))
    route = [(i - distance, i) for i in devices if i - distance in devices]
    return lax.ppermute(block, axis, route)


def pair_sums(left_val, right_val, groups):
    grouped = (left_val.shape[0], left_val.shape[1], groups, left_val.shape[2] // groups)
    split_left = left_val.reshape(grouped)
    return (
        jnp.sum(split_left, axis=(0, 1, 3)),
        jnp.sum(split_left * right_val.reshape(grouped), axis=(0, 1, 3)),
    )


def normalize(field_in, first_sum, square_sum, cell_count, groups):
    grouped = (field_in.shape[0], field_in.shape[1], groups, field_in.shape[2] // groups)
    mean_val = first_sum / cell_count
    inverse = lax.rsqrt(square_sum / cell_count - mean_val * mean_val + EPSILON)
    normed = (field_in.reshape(grouped) - mean_val[:, None]) * inverse[:, None]
    return (normed.reshape(field_in.shape), inverse)


def norm_back(hat_grad, normed, grad_sum, cross_sum, inverse, cell_count, groups):
    grouped = (hat_grad.shape[0], hat_grad.shape[1], groups, hat_grad.shape[2] // groups)
    result = (
        hat_grad.reshape(grouped)
        - (grad_sum / cell_count)[:, None]
        - normed.reshape(grouped) * (cross_sum / cell_count)[:, None]
    ) * inverse[:, None]
    return result.reshape(hat_grad.shape)


def silu_slope(pre_val):
    sigmoid = jax.nn.sigmoid(pre_val)
    return sigmoid * (1.0 + pre_val * (1.0 - sigmoid))


def conv_rows(padded, weight):
    return lax.conv_general_dilated(
        padded[None],
        weight,
        (1, 1),
        ((0, 0), (1, 1)),
        dimension_numbers=NUMBERS,
        preferred_element_type=jnp.float32,
    )[0]


def conv_back(grad_padded, weight):
    flipped = jnp.transpose(weight[::-1, ::-1], (0, 1, 3, 2))
    return conv_rows(grad_padded, flipped)


def tap_grad(widened, grad_val, stride):
    taps = lax.conv_general_dilated(
        widened[..., None],
        grad_val[:, :, None, :],
        (1, 1),
        ((0, 0), (0, 0)),
        rhs_dilation=(stride, stride),
        dimension_numbers=("HWNC", "HWIO", "NHWC"),
        preferred_element_type=jnp.float32,
    )
    return jnp.transpose(taps, (1, 2, 0, 3))


def widen(field_in):
    return jnp.pad(field_in, ((0, 0), (1, 1), (0, 0)))


MESH = pl.DeviceIdType.MESH


def flip(index, bit):
    return index + bit * (1 - 2 * ((index // bit) % 2))


class Side:
    def __init__(self, where, mine):
        self.where = where
        self.mine = mine


def sides(order, dp_size):
    d = lax.axis_index("dp")
    r = lax.axis_index("rows")
    found = []
    for name in order:
        if name == "rows":
            found.append(Side((d, 1 - r), r))
        else:
            found.append(Side((flip(d, name), r), (d // name) % 2))
    return found


def orders(dp_size):
    bits = []
    bit = 1
    while bit < dp_size:
        bits.append(bit)
        bit *= 2
    near = bits[:4] + ["rows"]
    return near, bits[4:]


def part(start, size):
    return pl.ds(pl.multiple_of(start, size), size)


class Total:
    def __init__(self, rows, halving, whole, own, kept, inbox, extra, result, send, recv):
        self.rows = rows
        self.halving = halving
        self.whole = whole
        self.own = own
        self.kept = kept
        self.inbox = inbox
        self.extra = extra
        self.result = result
        self.send = send
        self.recv = recv
        self.steps = len(halving)
        self.copy = None
        self.count = 0

    def size(self, step):
        return self.rows if step == 0 else self.rows >> step

    def begin(self, src, dst, where):
        k = self.count
        self.count += 1
        self.copy = pltpu.make_async_remote_copy(
            src_ref=src,
            dst_ref=dst,
            send_sem=self.send.at[k],
            recv_sem=self.recv.at[k],
            device_id=where,
            device_id_type=MESH,
        )
        self.copy.start()

    def start(self):
        side = self.halving[0]
        self.begin(self.own.at[1 - side.mine], self.inbox[0], side.where)
        self.stage = 0

    def offset(self, step):
        total = 0
        for t in range(1, step + 1):
            total = total + self.halving[t].mine * self.size(t)
        return total

    def region(self, step):
        lead = self.halving[0].mine
        if step == 0:
            return self.result.at[lead]
        return self.result.at[lead, part(self.offset(step), self.size(step))]

    def advance(self):
        stage = self.stage
        self.copy.wait()
        last = self.steps - 1
        if stage < self.steps:
            side = self.halving[stage]
            size = self.size(stage)
            got = self.inbox[stage]
            if stage == 0:
                have = self.own.at[side.mine]
            else:
                have = self.kept[stage - 1].at[part(side.mine * size, size)]
            if stage == last and not self.whole:
                dest = self.region(last)
            else:
                dest = self.kept[stage]
            add_rows(dest, have, got, size)
            if stage < last:
                nxt = self.halving[stage + 1]
                half = self.size(stage + 1)
                self.begin(
                    self.kept[stage].at[part((1 - nxt.mine) * half, half)],
                    self.inbox[stage + 1],
                    nxt.where,
                )
            elif self.whole:
                self.begin(self.kept[last], self.extra.at[0], self.whole[0].where)
            else:
                self.gather(last)
        elif stage < self.steps + len(self.whole):
            k = stage - self.steps
            size = self.size(last)
            final = k == len(self.whole) - 1
            have = self.kept[last + k]
            dest = self.region(last) if final else self.kept[last + k + 1]
            add_rows(dest, have, self.extra.at[k], size)
            if final:
                self.gather(last)
            else:
                self.begin(self.kept[last + k + 1], self.extra.at[k + 1], self.whole[k + 1].where)
        else:
            k = stage - self.steps - len(self.whole)
            if k < last:
                self.gather(last - 1 - k)
            else:
                self.copy = None
        self.stage = stage + 1

    def gather(self, step):
        mine = self.region(step)
        self.begin(mine, mine, self.halving[step].where)

    @property
    def events(self):
        return 2 * self.steps + len(self.whole)


def add_rows(dest, have, got, size):
    block = size
    while block > 160:
        block //= 2 if (block // 2) % 16 == 0 else 3
    if block == size:
        dest[...] = have[...] + got[...]
    else:

        @pl.loop(0, size // block)
        def _(i):
            here = part(i * block, block)
            dest[here] = have[here] + got[here]


def total_scratch(rows, steps, whole):
    kept = [pltpu.VMEM((rows >> k, 128), jnp.bfloat16) for k in range(0, steps)]
    kept += [pltpu.VMEM((rows >> (steps - 1), 128), jnp.bfloat16) for _ in range(whole)]
    inbox = [pltpu.VMEM((rows >> k, 128), jnp.bfloat16) for k in range(0, steps)]
    extra = pltpu.VMEM((max(whole, 1), rows >> (steps - 1), 128), jnp.bfloat16)
    events = 2 * steps + whole
    return [
        kept,
        inbox,
        extra,
        pltpu.SemaphoreType.DMA((events,)),
        pltpu.SemaphoreType.DMA((events,)),
    ]


GROUPS = (1024, 2304, 2304, 1280)


def totals_kernel(near, far, dp_size, *refs):
    own = refs[:4]
    out = refs[4:8]
    results, scratch, out_sem = refs[8], refs[9], refs[10]
    halving = sides(near, dp_size)
    whole = sides(far, dp_size)
    barrier = pltpu.get_barrier_semaphore()
    for side in halving + whole:
        pl.semaphore_signal(barrier, inc=1, device_id=side.where, device_id_type=MESH)
    pl.semaphore_wait(barrier, len(halving) + len(whole))
    groups = []
    for k, rows in enumerate(GROUPS):
        kept, inbox, extra, send, recv = scratch[k]
        groups.append(Total(rows, halving, whole, own[k], kept, inbox, extra, results[k], send, recv))
    for group in groups:
        group.start()
    for _ in range(groups[0].events):
        for group in groups:
            group.advance()
    for k in range(4):
        out[k][...] = results[k][...]


def sum_all(near, far, dp_size, parts):
    vmem = pl.BlockSpec(memory_space=pltpu.VMEM)
    return pl.pallas_call(
        lambda *refs: totals_kernel(near, far, dp_size, *refs),
        out_shape=[jax.ShapeDtypeStruct(p.shape, p.dtype) for p in parts],
        in_specs=[vmem] * 4,
        out_specs=[vmem] * 4,
        scratch_shapes=[
            [pltpu.VMEM(p.shape, p.dtype) for p in parts],
            [total_scratch(rows, len(near), len(far)) for rows in GROUPS],
            pltpu.SemaphoreType.DMA,
        ],
        compiler_params=pltpu.CompilerParams(
            collective_id=0, has_side_effects=True, vmem_limit_bytes=56 * 2**20
        ),
        name="sum_all",
    )(*parts)


def halves(rows):
    low = rows.astype(jnp.bfloat16)
    return jnp.stack([low[:, :128], low[:, 128:]])


def joined(parts):
    return jnp.concatenate([parts[0], parts[1]], axis=1).astype(jnp.float32)


def body(
    image_in,
    noise_in,
    sigma_in,
    embedding,
    features,
    norm1_gain,
    norm1_bias,
    conv1_w,
    film_w,
    film_b,
    norm2_gain,
    norm2_bias,
    conv2_w,
    skip_w,
    down_w,
    qkv_w,
    proj_w,
    down_cot,
    attn_cot,
):
    row_count, col_count, chans_in = (image_in.shape[1], image_in.shape[2], image_in.shape[3])
    channels = conv1_w.shape[3]
    groups = G
    all_rows = row_count * lax.axis_size("rows")
    count_one = all_rows * col_count * (chans_in // groups)
    count_two = all_rows * col_count * (channels // groups)
    contract_last = (((1,), (1,)), ((), ()))
    contract_first = (((0,), (0,)), ((), ()))
    sigma_one = sigma_in[0]
    scale_in = lax.rsqrt(SIGMA_DATA * SIGMA_DATA + sigma_one * sigma_one)
    shifted_in = scale_in * (
        image_in[0].astype(jnp.float32) + sigma_one * noise_in[0].astype(jnp.float32)
    )
    first_one, square_one = pair_sums(shifted_in, shifted_in, groups)
    first_one, square_one = lax.psum((first_one, square_one), "rows")
    hat_one, inverse_one = normalize(shifted_in, first_one, square_one, count_one, groups)
    pre_one = hat_one * norm1_gain + norm1_bias
    hidden_one = jax.nn.silu(pre_one).astype(jnp.bfloat16)
    padded_one = padded_2(hidden_one, (("rows", 0),), 1)
    conv_one = conv_rows(padded_one, conv1_w)
    film_out = jnp.dot(embedding, film_w, preferred_element_type=jnp.float32)[0] + film_b
    scale_mul = 1.0 + film_out[:channels]
    shift_add = film_out[channels:]
    first_two, square_two = pair_sums(conv_one, conv_one, groups)
    first_two, square_two = lax.psum((first_two, square_two), "rows")
    hat_two, inverse_two = normalize(conv_one, first_two, square_two, count_two, groups)
    normed_two = hat_two * norm2_gain + norm2_bias
    pre_two = normed_two * scale_mul + shift_add
    hidden_two = jax.nn.silu(pre_two).astype(jnp.bfloat16)
    padded_two = padded_2(hidden_two, (("rows", 0),), 1)
    low_in = shifted_in.astype(jnp.bfloat16).reshape(-1, chans_in)
    skip_out = jnp.dot(low_in, skip_w, preferred_element_type=jnp.float32).reshape(
        row_count, col_count, channels
    )
    summed = (conv_rows(padded_two, conv2_w) + skip_out).astype(jnp.bfloat16)
    above_row = shifted(summed[-1:], "rows", 1)
    extended = jnp.concatenate([above_row, summed], axis=0)
    down_out = lax.conv_general_dilated(
        extended[None],
        down_w,
        (2, 2),
        ((0, 0), (1, 1)),
        dimension_numbers=NUMBERS,
        preferred_element_type=jnp.float32,
    )
    block_out = down_out.astype(jnp.bfloat16)
    feature_rows = features[0]
    projected = jnp.dot(feature_rows, qkv_w, preferred_element_type=jnp.float32)
    queries = projected[:, :channels].astype(jnp.bfloat16)
    key_value = lax.all_gather(
        projected[:, channels:].astype(jnp.bfloat16), "rows", axis=0, tiled=True
    )
    keys_all = key_value[:, :channels]
    values_all = key_value[:, channels:]
    att_scale = channels ** (-0.5)
    scores = (
        lax.dot_general(queries, keys_all, contract_last, preferred_element_type=jnp.float32)
        * att_scale
    )
    largest = jnp.max(scores, axis=-1, keepdims=True)
    lse_rows = largest + jnp.log(jnp.sum(jnp.exp(scores - largest), axis=-1, keepdims=True))
    weights = jnp.exp(scores - lse_rows)
    mixed_out = jnp.dot(
        weights.astype(jnp.bfloat16), values_all, preferred_element_type=jnp.float32
    ).astype(jnp.bfloat16)
    attended = (
        feature_rows.astype(jnp.float32)
        + jnp.dot(mixed_out, proj_w, preferred_element_type=jnp.float32)
    ).astype(jnp.bfloat16)
    attn_grad = attn_cot[0]
    mixed_grad = lax.dot_general(
        attn_grad, proj_w, contract_last, preferred_element_type=jnp.float32
    ).astype(jnp.bfloat16)
    proj_grad = lax.dot_general(
        mixed_out, attn_grad, contract_first, preferred_element_type=jnp.float32
    )
    scores_again = (
        lax.dot_general(queries, keys_all, contract_last, preferred_element_type=jnp.float32)
        * att_scale
    )
    back_weights = jnp.exp(scores_again - lse_rows)
    prob_grad = lax.dot_general(
        mixed_grad, values_all, contract_last, preferred_element_type=jnp.float32
    )
    value_part = lax.dot_general(
        back_weights.astype(jnp.bfloat16),
        mixed_grad,
        contract_first,
        preferred_element_type=jnp.float32,
    )
    inner_sum = jnp.sum(back_weights * prob_grad, axis=-1, keepdims=True)
    score_grad = (back_weights * (prob_grad - inner_sum)).astype(jnp.bfloat16)
    query_grad = (
        jnp.dot(score_grad, keys_all, preferred_element_type=jnp.float32) * att_scale
    ).astype(jnp.bfloat16)
    key_part = (
        lax.dot_general(score_grad, queries, contract_first, preferred_element_type=jnp.float32)
        * att_scale
    )
    key_grad, value_grad = (
        lax.psum_scatter(key_part, "rows", scatter_dimension=0, tiled=True),
        lax.psum_scatter(value_part, "rows", scatter_dimension=0, tiled=True),
    )
    projected_grad = jnp.concatenate(
        [query_grad, key_grad.astype(jnp.bfloat16), value_grad.astype(jnp.bfloat16)], axis=1
    )
    qkv_grad = lax.dot_general(
        feature_rows, projected_grad, contract_first, preferred_element_type=jnp.float32
    )
    feature_grad = attn_grad.astype(jnp.float32) + lax.dot_general(
        projected_grad, qkv_w, contract_last, preferred_element_type=jnp.float32
    )
    attention_totals = (qkv_grad, proj_grad)
    down_grad_in = down_cot[0]
    down_grad = tap_grad(widen(extended)[:, :-1], down_grad_in, 2)
    flipped_down = jnp.transpose(down_w[::-1, ::-1], (0, 1, 3, 2))
    ext_grad = lax.conv_general_dilated(
        down_grad_in[None],
        flipped_down,
        (1, 1),
        ((2, 2), (1, 2)),
        lhs_dilation=(2, 2),
        dimension_numbers=NUMBERS,
        preferred_element_type=jnp.float32,
    )[0]
    from_below = shifted(ext_grad[:1], "rows", -1)
    summed_grad = ext_grad[1:].at[-1].add(from_below[0])
    low_grad = summed_grad.astype(jnp.bfloat16)
    flat_grad = low_grad.reshape(-1, channels)
    skip_grad = lax.dot_general(
        low_in, flat_grad, contract_first, preferred_element_type=jnp.float32
    )
    skip_back = lax.dot_general(
        flat_grad, skip_w, contract_last, preferred_element_type=jnp.float32
    ).reshape(row_count, col_count, chans_in)
    conv2_grad = tap_grad(widen(padded_two), low_grad, 1)
    grad_pad_two = padded_2(low_grad, (("rows", 0),), 1)
    hidden_two_grad = conv_back(grad_pad_two, conv2_w)
    pre_two_grad = hidden_two_grad * silu_slope(pre_two)
    shift_grad = jnp.sum(pre_two_grad, axis=(0, 1))
    scale_grad = jnp.sum(pre_two_grad * normed_two, axis=(0, 1))
    film_bias_grad = jnp.concatenate([scale_grad, shift_grad])
    film_grad = embedding[0].astype(jnp.float32)[:, None] * film_bias_grad[None, :]
    normed_grad = pre_two_grad * scale_mul
    gain2_grad = jnp.sum(normed_grad * hat_two, axis=(0, 1))
    bias2_grad = jnp.sum(normed_grad, axis=(0, 1))
    hat_two_grad = normed_grad * norm2_gain
    grad_sum_two, cross_two = pair_sums(hat_two_grad, hat_two, groups)
    grad_sum_two, cross_two = lax.psum((grad_sum_two, cross_two), "rows")
    conv_one_grad = norm_back(
        hat_two_grad, hat_two, grad_sum_two, cross_two, inverse_two, count_two, groups
    ).astype(jnp.bfloat16)
    conv1_grad = tap_grad(widen(padded_one), conv_one_grad, 1)
    grad_pad_one = padded_2(conv_one_grad, (("rows", 0),), 1)
    hidden_one_grad = conv_back(grad_pad_one, conv1_w)
    pre_one_grad = hidden_one_grad * silu_slope(pre_one)
    gain1_grad = jnp.sum(pre_one_grad * hat_one, axis=(0, 1))
    bias1_grad = jnp.sum(pre_one_grad, axis=(0, 1))
    hat_one_grad = pre_one_grad * norm1_gain
    grad_sum_one, cross_one = pair_sums(hat_one_grad, hat_one, groups)
    grad_sum_one, cross_one = lax.psum((grad_sum_one, cross_one), "rows")
    shifted_grad = (
        norm_back(hat_one_grad, hat_one, grad_sum_one, cross_one, inverse_one, count_one, groups)
        + skip_back
    )
    image_grad = (scale_in * shifted_grad)[None]
    small = lax.psum(
        (gain1_grad, bias1_grad, film_bias_grad, gain2_grad, bias2_grad), ("dp", "rows")
    )
    film_row = lax.psum(film_bias_grad, "rows")
    film_all = lax.all_gather(film_row, "dp")
    embed_all = lax.all_gather(embedding[0], "dp")
    film_total = lax.dot_general(
        embed_all.astype(jnp.float32),
        film_all,
        (((0,), (0,)), ((), ())),
        precision=lax.Precision.HIGHEST,
    )
    near, far = orders(lax.axis_size("dp"))
    sums = sum_all(
        near,
        far,
        lax.axis_size("dp"),
        [
            halves(
                jnp.concatenate(
                    [qkv_grad[:, :256], qkv_grad[:, 256:512], qkv_grad[:, 512:], proj_grad]
                )
            ),
            halves(conv2_grad.reshape(-1, 256)),
            halves(down_grad.reshape(-1, 256)),
            halves(jnp.concatenate([conv1_grad.reshape(-1, 256), skip_grad])),
        ],
    )
    att, conv2_sum, down_sum, first = (joined(p) for p in sums)
    totals = (
        small[0],
        small[1],
        first[:1152].reshape(conv1_grad.shape),
        film_total,
        small[2],
        small[3],
        small[4],
        conv2_sum.reshape(conv2_grad.shape),
        first[1152:],
        down_sum.reshape(down_grad.shape),
        jnp.concatenate([att[:256], att[256:512], att[512:768]], axis=1),
        att[768:],
    )
    return (
        block_out,
        attended[None],
        image_grad,
        feature_grad[None],
        totals[0],
        totals[1],
        totals[2],
        totals[3],
        totals[4],
        totals[5],
        totals[6],
        totals[7],
        totals[8],
        totals[9],
        totals[10],
        totals[11],
    )


def solution(mesh):
    placed = (
        P("dp", "rows", None, None),
        P("dp", "rows", None, None),
        P("dp"),
        P("dp", None),
        P("dp", "rows", None),
        P(),
        P(),
        P(),
        P(),
        P(),
        P(),
        P(),
        P(),
        P(),
        P(),
        P(),
        P(),
        P("dp", "rows", None, None),
        P("dp", "rows", None),
    )
    return jax.shard_map(
        body,
        mesh=mesh,
        in_specs=placed,
        out_specs=(
            P("dp", "rows", None, None),
            P("dp", "rows", None),
            P("dp", "rows", None, None),
            P("dp", "rows", None),
            P(),
            P(),
            P(),
            P(),
            P(),
            P(),
            P(),
            P(),
            P(),
            P(),
            P(),
            P(),
        ),
        check_vma=False,
    )
```

```python
import functools

import jax
import jax.numpy as jnp
from jax import lax
from jax.experimental import pallas as pl
from jax.experimental.pallas import tpu as pltpu
from jax.sharding import PartitionSpec as P

G = 32
EPSILON = 1e-05
SIGMA_DATA = 0.5
MESH = pl.DeviceIdType.MESH
ANY = pl.BlockSpec(memory_space=pl.ANY)
SMEM = pl.BlockSpec(memory_space=pltpu.SMEM)
VMEM_SPEC = pl.BlockSpec(memory_space=pltpu.VMEM)
BF = jnp.bfloat16
F32 = jnp.float32
TOKENS = 448


def flip(index, bit):
    return index + bit * (1 - 2 * ((index // bit) % 2))


class Side:
    def __init__(self, names):
        d = lax.axis_index("dp")
        r = lax.axis_index("rows")
        self.mine = []
        for name in names:
            self.mine.append(r if name == "rows" else (d // name) % 2)
        self.parts = 2 ** len(names)
        self.names = names
        self.position = (d, r)

    def partners(self):
        found = []
        for flips in range(1, self.parts):
            d, r = self.position
            index = 0
            for k, name in enumerate(self.names):
                other = (flips >> k) % 2
                side = self.mine[k]
                if other:
                    side = 1 - side
                    if name == "rows":
                        r = 1 - r
                    else:
                        d = flip(d, name)
                index = index * 2 + side
            found.append(((d, r), index))
        return found

    @property
    def index(self):
        index = 0
        for side in self.mine:
            index = index * 2 + side
        return index


def part(start, size):
    return pl.ds(pl.multiple_of(start, size), size)


class Total:
    def __init__(self, rows, stages, whole, own, kept, inbox, extra, result, send, recv):
        self.rows = rows
        self.stages = [Side(names) for names in stages]
        self.whole = [Side([name]) for name in whole]
        self.own = own
        self.kept = kept
        self.inbox = inbox
        self.extra = extra
        self.result = result
        self.send = send
        self.recv = recv
        self.sizes = sizes_of(rows, stages)
        self.steps = len(stages)
        self.copies = None
        self.count = 0

    def begin(self, src, dst, where):
        k = self.count
        self.count += 1
        copy = pltpu.make_async_remote_copy(
            src_ref=src,
            dst_ref=dst,
            send_sem=self.send.at[k],
            recv_sem=self.recv.at[k],
            device_id=where,
            device_id_type=MESH,
        )
        copy.start()
        self.copies.append(copy)

    def scatter(self, step):
        side = self.stages[step]
        size = self.sizes[step]
        for slot, (where, index) in enumerate(side.partners()):
            if step == 0:
                src = self.own.at[index]
            else:
                src = self.kept[step - 1].at[part(index * size, size)]
            self.begin(src, self.inbox[step].at[slot], where)

    def start(self):
        self.copies = []
        self.scatter(0)
        self.stage = 0

    def region(self, step):
        lead = self.stages[0].index
        if step == 0:
            return self.result.at[lead]
        offset = 0
        for t in range(1, step + 1):
            offset = offset + self.stages[t].index * self.sizes[t]
        return self.result.at[lead, part(offset, self.sizes[step])]

    def gather(self, step):
        mine = self.region(step)
        for where, _ in self.stages[step].partners():
            self.begin(mine, mine, where)

    def swap_whole(self, k):
        (where, _), = self.whole[k].partners()
        self.begin(self.kept[self.steps - 1 + k], self.extra.at[k], where)

    def advance(self):
        stage = self.stage
        last = self.steps - 1
        for copy in self.copies:
            copy.wait()
        self.copies = []
        if stage < self.steps:
            side = self.stages[stage]
            size = self.sizes[stage]
            if stage == 0:
                have = self.own.at[side.index]
            else:
                have = self.kept[stage - 1].at[part(side.index * size, size)]
            if stage == last and not self.whole:
                dest = self.region(last)
            else:
                dest = self.kept[stage]
            add_rows(dest, have, self.inbox[stage], side.parts - 1, size)
            if stage < last:
                self.scatter(stage + 1)
            elif self.whole:
                self.swap_whole(0)
            else:
                self.gather(last)
        elif stage < self.steps + len(self.whole):
            k = stage - self.steps
            final = k == len(self.whole) - 1
            dest = self.region(last) if final else self.kept[last + k + 1]
            add_rows(dest, self.kept[last + k], self.extra.at[pl.ds(k, 1)], 1, self.sizes[last])
            if final:
                self.gather(last)
            else:
                self.swap_whole(k + 1)
        else:
            k = stage - self.steps - len(self.whole)
            if k < last:
                self.gather(last - 1 - k)
            else:
                self.copies = None
        self.stage = stage + 1

    @property
    def busy(self):
        return self.copies is not None


def add_rows(dest, have, got, count, size):
    block = size
    while block > 160:
        block //= 2 if (block // 2) % 16 == 0 else 3

    def add(here):
        value = have[here].astype(jnp.float32)
        for slot in range(count):
            value = value + got[slot, here].astype(jnp.float32)
        dest[here] = value.astype(jnp.bfloat16)

    if block == size:
        add(pl.ds(0, size))
    else:

        @pl.loop(0, size // block)
        def _(i):
            add(part(i * block, block))


def sizes_of(rows, stages):
    sizes = [rows]
    for names in stages[1:]:
        sizes.append(sizes[-1] // 2 ** len(names))
    return sizes


def copies_of(stages, whole):
    return 2 * sum(2 ** len(names) - 1 for names in stages) + len(whole)


def total_scratch(rows, stages, whole):
    sizes = sizes_of(rows, stages)
    kept = [pltpu.VMEM((size, 128), jnp.bfloat16) for size in sizes + [sizes[-1]] * len(whole)]
    inbox = [
        pltpu.VMEM((2 ** len(names) - 1, size, 128), jnp.bfloat16)
        for names, size in zip(stages, sizes)
    ]
    extra = pltpu.VMEM((max(len(whole), 1), sizes[-1], 128), jnp.bfloat16)
    count = copies_of(stages, whole)
    return [
        kept,
        inbox,
        extra,
        pltpu.SemaphoreType.DMA((count,)),
        pltpu.SemaphoreType.DMA((count,)),
    ]


class Names:
    def __init__(self, pairs=()):
        vars(self).update(pairs)


class Once:
    def __init__(self, copy):
        self.copy = copy
        self.waited = False
        copy.start()

    def wait(self):
        if not self.waited:
            self.waited = True
            self.copy.wait()


def nn(left, right):
    return lax.dot_general(left, right, (((1,), (0,)), ((), ())), preferred_element_type=F32)


def nt(left, right):
    return lax.dot_general(left, right, (((1,), (1,)), ((), ())), preferred_element_type=F32)


def tn(left, right):
    return lax.dot_general(left, right, (((0,), (0,)), ((), ())), preferred_element_type=F32)


def fold(value):
    rows, lanes = value.shape
    return jnp.sum(value.reshape(rows // 8, 8, lanes), axis=0)


def one_row(value):
    return jnp.sum(value, axis=0, keepdims=True)


def group_sum(value, width):
    lanes = value.shape[1]
    lane = lax.broadcasted_iota(jnp.int32, value.shape, 1)
    step = 1
    while step < width:
        up = pltpu.roll(value, lanes - step, 1)
        down = pltpu.roll(value, step, 1)
        value = value + jnp.where((lane // step) % 2 == 0, up, down)
        step *= 2
    return value


def sigmoid(value):
    return 0.5 + 0.5 * jnp.tanh(0.5 * value)


def spread(row, staged, lanes):
    cells = row.shape[0]
    for b in range(3):
        for k in range(lanes // 128):
            at = b * lanes + k * 128
            row[:, at : at + 128] = staged[k, 7 + b : 7 + b + cells, :].astype(BF)


def put(staged, start, value):
    cells, lanes = value.shape
    for k in range(lanes // 128):
        staged[k, pl.ds(start, cells), :] = value[:, k * 128 : (k + 1) * 128]


def level_kernel(cfg, *refs):
    n_in = len(cfg.inputs)
    ins = Names(zip(cfg.inputs, refs[:n_in]))
    outs = Names(zip(cfg.outputs, refs[n_in : n_in + len(cfg.outputs)]))
    sc = Names(refs[n_in + len(cfg.outputs)])
    st = Names()
    rows, cols, chi, ch = cfg.rows, cfg.cols, cfg.chi, cfg.ch
    half = cols // 2
    r = lax.axis_index("rows")
    d = lax.axis_index("dp")
    across = (d, 1 - r)

    loads = Names()
    loading = []

    def load(name, dst):
        copy = Once(pltpu.make_async_copy(vars(ins)[name], dst, sc.load_sem.at[len(loading)]))
        loading.append(copy)
        setattr(loads, name, copy)

    stores = []

    def store(src, dst):
        copy = pltpu.make_async_copy(src, dst, sc.store_sem.at[len(stores)])
        copy.start()
        stores.append(copy)

    def swap_copy(k, src, dst):
        return pltpu.make_async_remote_copy(
            src_ref=src,
            dst_ref=dst,
            send_sem=sc.x_send.at[k],
            recv_sem=sc.x_recv.at[k],
            device_id=across,
            device_id_type=MESH,
        )

    swaps = []

    def swap(k, src, dst):
        copy = Once(swap_copy(k, src, dst))
        swaps.append(copy)
        return copy

    barrier = pltpu.get_barrier_semaphore()
    greeted = {}
    for stages in cfg.plans:
        for names in stages + [[name] for name in cfg.far]:
            side = Side(names)
            for flips, (where, _) in enumerate(side.partners(), 1):
                met = frozenset(n for k, n in enumerate(names) if (flips >> k) % 2)
                greeted[met] = where
    for where in greeted.values():
        pl.semaphore_signal(barrier, inc=1, device_id=where, device_id_type=MESH)

    sc.down_cot = sc.dc.at[1:3]
    for name in cfg.inputs[1:]:
        load(name, vars(sc)[name])

    for ref in (sc.stage_i, sc.stage_c, sc.stage_h):
        zeros = jnp.zeros((ref.shape[0], 8, 128), F32)
        ref[:, 0:8, :] = zeros
        ref[:, ref.shape[1] - 8 :, :] = zeros
    outer = 5 * r
    inner = 5 * (1 - r)
    edge = 4 - 3 * r
    sc.h1c[outer] = jnp.zeros((cols, 3 * chi), BF)
    sc.h2c[outer] = jnp.zeros((cols, 3 * ch), BF)
    sc.cg3[outer] = jnp.zeros((cols, 3 * ch), BF)
    sc.dc[3 * r] = jnp.zeros((half, ch), BF)

    @pl.when(r == 0)
    def _():
        sc.s3[0] = jnp.zeros((half, 3 * ch), BF)

    for ref in (sc.F, sc.GA):
        ref[1, 400:, :] = jnp.zeros((TOKENS - 400, ch), BF)
    pl.semaphore_wait(barrier, len(greeted))

    dc_swap = swap(0, ins.down_cot.at[1 - r], sc.dc.at[3 * r])

    sigma = jnp.full((1, chi), ins.sigma_in[0], F32)
    scale_in = lax.rsqrt(SIGMA_DATA * SIGMA_DATA + sigma * sigma)
    loads.image_in.wait()
    loads.noise_in.wait()
    piece = cols // 4

    def stats_one(i, carry):
        row, col = i // 4, i % 4
        here = part(col * piece, piece)
        value = scale_in * (
            sc.image_in[row, here].astype(F32) + sigma * sc.noise_in[row, here].astype(F32)
        )
        sc.xs[row, here] = value
        sc.image_in[row, here] = value.astype(BF)
        return carry[0] + fold(value), carry[1] + fold(value * value)

    zero8 = jnp.zeros((8, chi), F32)
    sum_a, sum_b = lax.fori_loop(0, rows * 4, stats_one, (zero8, zero8))
    low_in = sc.image_in

    def send_stats(k, top, bottom):
        lanes = top.shape[1]
        sc.st_out[k, 0:1, 0:lanes] = top
        sc.st_out[k, 1:2, 0:lanes] = bottom
        copy = swap(1 + k, sc.st_out.at[k], sc.st_in.at[k])
        return copy

    def both_stats(k, copy, lanes):
        copy.wait()
        total = sc.st_out[k, :, 0:lanes] + sc.st_in[k, :, 0:lanes]
        return total[0:1], total[1:2]

    swap_one = send_stats(0, one_row(sum_a), one_row(sum_b))

    dw = sc.down_w
    loads.down_cot.wait()
    loads.down_w.wait()

    def shifted_cot(m):
        staged = sc.stage_h
        put(staged, 8, sc.dc[m].astype(F32))
        right = [staged[k, 9 : 9 + half, :].astype(BF) for k in range(ch // 128)]
        return sc.dc[m], jnp.concatenate(right, axis=1)

    def dw_tap(a, b):
        return dw[a, b * ch : (b + 1) * ch, :]

    def even_row(m):
        here, right = shifted_cot(m)
        return nt(here, dw_tap(1, 1)), nt(here, dw_tap(1, 2)) + nt(right, dw_tap(1, 0))

    def odd_row(m):
        here, right = shifted_cot(m)
        even = nt(here, dw_tap(2, 1))
        odd = nt(here, dw_tap(2, 2)) + nt(right, dw_tap(2, 0))
        here, right = shifted_cot(m + 1)
        even += nt(here, dw_tap(0, 1))
        odd += nt(here, dw_tap(0, 2)) + nt(right, dw_tap(0, 0))
        return even, odd

    def put_row(l, pair):
        staged = sc.stage_c
        for k in range(ch // 128):
            for odd in range(2):
                value = pair[odd][:, k * 128 : (k + 1) * 128]
                staged[k, pl.ds(8 + odd, half, stride=2), :] = value
        spread(sc.sg3.at[l], staged, ch)

    def summed_grad_own():
        @pl.loop(0, 2)
        def _(k):
            put_row(1 + 2 * k, even_row(1 + k))

        put_row(2, odd_row(1))

    def summed_grad_edge():
        dc_swap.wait()
        put_row(4, odd_row(2))

        @pl.when(r == 0)
        def _():
            put_row(5, even_row(3))
            sc.sg3[0] = jnp.zeros((cols, 3 * ch), BF)

        @pl.when(r == 1)
        def _():
            put_row(0, odd_row(0))
            sc.sg3[5] = jnp.zeros((cols, 3 * ch), BF)

    gain1 = lambda: sc.norm1_gain[...]
    bias1 = lambda: sc.norm1_bias[...]
    count1 = float(2 * rows * cols * (chi // G))
    count2 = float(2 * rows * cols * (ch // G))

    def moments(first, second, width, count):
        mean = group_sum(first, width) / count
        return mean, lax.rsqrt(group_sum(second, width) / count - mean * mean + EPSILON)

    st.sums2 = (0.0, 0.0)
    st.sums4 = (zero8, zero8)

    def fill_halo(row, staged, lanes):
        put(staged, 8, row[:, lanes : 2 * lanes].astype(F32))
        for k in range(lanes // 128):
            at = k * 128
            row[:, at : at + 128] = staged[k, 7 : 7 + cols, :].astype(BF)
            row[:, 2 * lanes + at : 2 * lanes + at + 128] = staged[k, 9 : 9 + cols, :].astype(BF)

    def hidden_one():
        loads.norm1_gain.wait()
        loads.norm1_bias.wait()
        first, second = both_stats(0, swap_one, chi)
        mean, inverse = moments(first, second, chi // G, count1)
        st.mean1, st.inv1 = mean, inverse

        def row_of(l):
            staged = sc.stage_i

            @pl.loop(0, 4)
            def _(c):
                here = part(c * piece, piece)
                pre = (sc.xs[l - 1, here] - mean) * inverse * gain1() + bias1()
                put(staged, pl.multiple_of(8 + c * piece, 8), pre * sigmoid(pre))

            spread(sc.h1c.at[l], staged, chi)

        row_of(edge)
        mid = sc.h1c.at[edge, :, chi : 2 * chi]
        st.h1 = swap(5, mid, sc.h1c.at[outer, :, chi : 2 * chi])

        @pl.loop(0, 3)
        def _(i):
            row_of(1 + i + r)

    def conv_pair(source, weight, base, lanes):
        acc = None
        for a in range(3):
            left = source[pl.ds(base - 1 + a, 2)].reshape(2 * cols, 3 * lanes)
            term = nn(left, weight[a])
            acc = term if acc is None else acc + term
        return acc

    near_pair = 1 + 2 * r
    edge_pair = 3 - 2 * r

    def conv_one(base):
        loads.conv1_w.wait()
        acc = conv_pair(sc.h1c, sc.conv1_w, base, chi)
        sc.c1[pl.ds(base - 1, 2)] = acc.reshape(2, cols, ch)
        sums = fold(acc), fold(acc * acc)
        st.sums2 = tuple(x + y for x, y in zip(st.sums2, sums))

    def halo_one():
        st.h1.wait()
        fill_halo(sc.h1c.at[inner], sc.stage_i, chi)

    def stats_two():
        first, second = st.sums2
        st.swap2 = send_stats(1, one_row(first), one_row(second))

    def back_pair(source, weight, base, lanes):
        acc = None
        for a in range(3):
            for b in range(3):
                left = source[pl.ds(base - 1 + a, 2), :, b * ch : (b + 1) * ch]
                term = nt(
                    left.reshape(2 * cols, ch), weight[2 - a, (2 - b) * lanes : (3 - b) * lanes, :]
                )
                acc = term if acc is None else acc + term
        return acc

    def hidden_two_grad(base):
        loads.conv2_w.wait()
        acc = back_pair(sc.sg3, sc.conv2_w, base, ch)
        sc.g2[pl.ds(base - 1, 2)] = acc.reshape(2, cols, ch)

    def grad_rows():
        return sc.sg3[1:5, :, ch : 2 * ch].reshape(rows * cols, ch)

    conv2_at = [(1, 0), (2, 0), (3, 0)]
    down_at = [(4, 0), (5, 0), (6, 0)]
    conv1_at = [(7, 0), (7, 3 * chi), (8, 0)]
    skip_at = (8, 3 * chi)

    def put_grad(place, value):
        group, start = place
        low = value.astype(BF)
        size = low.shape[0]
        sc.own[group][0, start : start + size, :] = low[:, :128]
        sc.own[group][1, start : start + size, :] = low[:, 128:]

    def skip_back():
        loads.skip_w.wait()
        sc.skb[...] = nt(grad_rows(), sc.skip_w[...]).reshape(rows, cols, chi)

    def skip_grad():
        put_grad(skip_at, tn(low_in[...].reshape(rows * cols, chi), grad_rows()))

    def film():
        for copy in (
            loads.embedding,
            loads.film_w,
            loads.film_b,
            loads.norm2_gain,
            loads.norm2_bias,
        ):
            copy.wait()
        row = nn(sc.embedding[...], sc.film_w[...]) + sc.film_b[...]
        scale = 1.0 + row[:, :ch]
        shift = row[:, ch:]
        gain, bias = sc.norm2_gain[...], sc.norm2_bias[...]
        st.scale = scale
        st.pre_gain = gain * scale
        st.pre_bias = bias * scale + shift

    def hidden_two():
        first, second = both_stats(1, st.swap2, ch)
        mean, inverse = moments(first, second, ch // G, count2)
        st.inv2 = inverse
        step = cols // 8

        def row_of(l, carry):
            staged = sc.stage_c

            def cells(c, carry):
                here = part(c * step, step)
                hat = (sc.c1[l - 1, here] - mean) * inverse
                sc.c1[l - 1, here] = hat
                pre = hat * st.pre_gain + st.pre_bias
                gate = sigmoid(pre)
                value = pre * gate
                put(staged, pl.multiple_of(8 + c * step, 8), value)
                grad = sc.g2[l - 1, here] * (gate + value * (1.0 - gate))
                sc.g2[l - 1, here] = grad
                return carry[0] + fold(grad), carry[1] + fold(grad * hat)

            carry = lax.fori_loop(0, 8, cells, carry)
            spread(sc.h2c.at[l], staged, ch)
            return carry

        zero = jnp.zeros((8, ch), F32)
        carry = lax.fori_loop(0, rows, lambda i, carry: row_of(1 + i, carry), (zero, zero))
        st.swap3 = send_stats(2, one_row(carry[0]), one_row(carry[1]))
        mid = sc.h2c.at[edge, :, ch : 2 * ch]
        st.h2 = swap(6, mid, sc.h2c.at[outer, :, ch : 2 * ch])

    def halo_two():
        st.h2.wait()
        fill_halo(sc.h2c.at[inner], sc.stage_c, ch)

    def conv2_grad(a):
        left = sc.h2c[1:5].reshape(rows * cols, 3 * ch)
        right = sc.sg3[2 - a : 6 - a, :, ch : 2 * ch].reshape(rows * cols, ch)
        put_grad(conv2_at[a], tn(left, right))

    def odd_shift(row):
        staged = sc.stage_h
        put(staged, 8, row[:, 2 * ch :].astype(F32))
        for k in range(ch // 128):
            row[:, k * 128 : (k + 1) * 128] = staged[k, 7 : 7 + half, :].astype(BF)

    def summed(base):
        acc = conv_pair(sc.h2c, sc.conv2_w, base, ch)
        low = low_in[pl.ds(base - 1, 2)].reshape(2 * cols, chi)
        acc = (acc + nn(low, sc.skip_w[...])).reshape(2, cols, ch)
        for k in range(2):
            staged = sc.stage_c
            put(staged, 8, acc[k])
            row = sc.s3.at[base + k]
            for i in range(ch // 128):
                for odd in range(2):
                    at = (1 + odd) * ch + i * 128
                    value = staged[i, pl.ds(8 + odd, half, stride=2), :]
                    row[:, at : at + 128] = value.astype(BF)
            odd_shift(row)

    def summed_swap():
        copy = swap_copy(7, sc.s3.at[4, :, ch:], sc.s3.at[0, :, ch:])
        st.s3 = copy

        @pl.when(r == 0)
        def _():
            copy.start()

    def halo_summed():
        copy = st.s3

        @pl.when(r == 0)
        def _():
            copy.wait_send()

        @pl.when(r == 1)
        def _():
            copy.wait_recv()
            odd_shift(sc.s3.at[0])

    def down(k):
        acc = None
        for a in range(3):
            term = nn(sc.s3[2 * k + a], dw[a])
            acc = term if acc is None else acc + term
        sc.block[k] = acc.astype(BF)

    def down_grad(a):
        first, cot = ((2, 2), (1, 1), (2, 1))[a]
        value = tn(sc.s3[first], sc.dc[cot]) + tn(sc.s3[first + 2], sc.dc[cot + 1])
        put_grad(down_at[a], value)

    def conv_one_grad():
        first, second = both_stats(2, st.swap3, ch)
        st.A, st.B = first, second
        factor = st.pre_gain
        m1 = group_sum(first * factor, ch // G) / count2
        m2 = group_sum(second * factor, ch // G) / count2
        inverse = st.inv2
        step = cols // 8

        def row_of(l):
            staged = sc.stage_c

            @pl.loop(0, 8)
            def _(c):
                here = part(c * step, step)
                value = (
                    sc.g2[l - 1, here] * factor - m1 - sc.c1[l - 1, here] * m2
                ) * inverse
                put(staged, pl.multiple_of(8 + c * step, 8), value)

            spread(sc.cg3.at[l], staged, ch)

        row_of(edge)
        mid = sc.cg3.at[edge, :, ch : 2 * ch]
        st.cg = swap(8, mid, sc.cg3.at[outer, :, ch : 2 * ch])

        @pl.loop(0, 3)
        def _(i):
            row_of(1 + i + r)

    def halo_grad():
        st.cg.wait()
        fill_halo(sc.cg3.at[inner], sc.stage_c, ch)

    def conv1_grad(a):
        right = sc.cg3[1:5, :, ch : 2 * ch].reshape(rows * cols, ch)
        left = sc.h1c[a : a + 4].reshape(rows * cols, 3 * chi)
        put_grad(conv1_at[a], tn(left, right))

    def hidden_one_grad(base):
        acc = back_pair(sc.cg3, sc.conv1_w, base, chi)
        sc.h1g[pl.ds(base - 1, 2)] = acc.reshape(2, cols, chi)
        mean, inverse = st.mean1, st.inv1

        def cells(i, carry):
            row, col = base - 1 + i // 4, i % 4
            here = part(col * piece, piece)
            hat = (sc.xs[row, here] - mean) * inverse
            sc.xs[row, here] = hat
            pre = hat * gain1() + bias1()
            gate = sigmoid(pre)
            grad = sc.h1g[row, here] * (gate + pre * gate * (1.0 - gate))
            sc.h1g[row, here] = grad
            return carry[0] + fold(grad), carry[1] + fold(grad * hat)

        st.sums4 = lax.fori_loop(0, 8, cells, st.sums4)

    def stats_four():
        first, second = st.sums4
        st.swap4 = send_stats(3, one_row(first), one_row(second))

    def image_grad():
        first, second = both_stats(3, st.swap4, chi)
        pk = sc.packet.at[d]
        values = (
            sc.embedding[...].astype(F32),
            st.A,
            st.B,
            st.scale * st.A,
            st.scale * st.B,
            first,
            second,
            jnp.zeros((1, 256), F32),
        )
        at = 0
        for value in values:
            for k in range(value.shape[1] // 128):
                pk[at : at + 1, :] = value[:, k * 128 : (k + 1) * 128]
                at += 1
        packet_start()
        m1 = group_sum(first * gain1(), chi // G) / count1
        m2 = group_sum(second * gain1(), chi // G) / count1

        @pl.loop(0, rows * 4)
        def _(i):
            row, col = i // 4, i % 4
            here = part(col * piece, piece)
            value = (
                sc.h1g[row, here] * gain1() - m1 - sc.xs[row, here] * m2
            ) * st.inv1 + sc.skb[row, here]
            sc.h1g[row, here] = scale_in * value

        store(sc.h1g, outs.image_grad)

    bits = [Side([bit]).partners()[0][0] for bit in cfg.bits]

    def packet_copy(k):
        size = cfg.bits[k]
        mine = sc.packet.at[pl.ds((d // size) * size, size)]
        return pltpu.make_async_remote_copy(
            src_ref=mine,
            dst_ref=mine,
            send_sem=sc.pk_send.at[k],
            recv_sem=sc.pk_recv.at[k],
            device_id=bits[k],
            device_id_type=MESH,
        )

    pk_state = [0]

    def packet_start():
        packet_copy(0).start()

    def packet_step():
        k = pk_state[0]
        packet_copy(k).wait()
        pk_state[0] = k + 1
        if k + 1 < len(cfg.bits):
            packet_copy(k + 1).start()

    tokens = cfg.tokens

    def tokens_in():
        loads.features.wait()
        loads.attn_cot.wait()
        for src, dst in ((sc.features, sc.F), (sc.attn_cot, sc.GA)):
            pad = jnp.zeros((TOKENS - tokens, ch), F32)
            dst[0] = jnp.concatenate([src[...].astype(F32), pad], axis=0).astype(BF)

    def send_tokens(ref, k):
        where = pl.ds(0, 208) if k % 2 == 0 else pl.ds(208, 192)
        return swap(9 + k, ref.at[0, where], ref.at[1, where])

    def project(k):
        loads.qkv_w.wait()
        loads.proj_w.wait()
        value = nn(sc.F[k], sc.qkv_w[...])
        for i, dst in enumerate((sc.Q, sc.K, sc.V)):
            dst[k] = value[:, i * ch : (i + 1) * ch].astype(BF)
        sc.MG[k] = nt(sc.GA[k], sc.proj_w[...]).astype(BF)

    att_scale = ch ** (-0.5)

    def flat(ref):
        return ref[...].reshape(2 * TOKENS, ch)

    def scores():
        sc.S[...] = nt(flat(sc.K), flat(sc.Q))
        sc.D[...] = nt(flat(sc.V), flat(sc.MG))

    def softmax(first, last):
        row = lax.broadcasted_iota(jnp.int32, (TOKENS, 128), 0)
        real = row < tokens

        @pl.loop(first, last)
        def _(c):
            here = part(c * 128, 128)
            both = [pl.ds(0, TOKENS), pl.ds(TOKENS, TOKENS)]
            value = [jnp.where(real, sc.S[keys, here] * att_scale, -1e30) for keys in both]
            most = jnp.max(jnp.maximum(value[0], value[1]), axis=0, keepdims=True)
            value = [jnp.exp(v - most) for v in value]
            scale = 1.0 / jnp.sum(value[0] + value[1], axis=0, keepdims=True)
            prob = [v * scale for v in value]
            for keys, v in zip(both, prob):
                sc.PR[keys, here] = v.astype(BF)
            back = [sc.D[keys, here] for keys in both]
            total = jnp.sum(prob[0] * back[0] + prob[1] * back[1], axis=0, keepdims=True)
            for keys, v, b in zip(both, prob, back):
                sc.DS[keys, here] = (v * (b - total)).astype(BF)

    def attend():
        mixed = tn(sc.PR[:, 0:512], flat(sc.V))[:TOKENS].astype(BF)
        out = sc.F[0].astype(F32) + nn(mixed, sc.proj_w[...])
        sc.att[...] = out[:tokens].astype(BF)
        put_grad((0, 3 * ch), tn(mixed, sc.GA[0]))
        store(sc.att, outs.attended)

    def attention_back():
        pg = sc.PG
        pg[:, 0:ch] = (tn(sc.DS[:, 0:512], flat(sc.K))[:TOKENS] * att_scale).astype(BF)
        pg[:, ch : 2 * ch] = (nn(sc.DS[0:TOKENS], flat(sc.Q)) * att_scale).astype(BF)
        pg[:, 2 * ch :] = nn(sc.PR[0:TOKENS], flat(sc.MG)).astype(BF)

    def attention_grads():
        pg = sc.PG
        grad = tn(sc.F[0], pg[...])
        for i in range(3):
            put_grad((0, i * ch), grad[:, i * ch : (i + 1) * ch])
        out = sc.GA[0].astype(F32) + nt(pg[...], sc.qkv_w[...])
        sc.fg[...] = out[:tokens]
        store(sc.fg, outs.features_grad)

    groups = []
    for k, size in enumerate(cfg.groups):
        kept, inbox, extra, send, recv = sc.sums[k]
        groups.append(
            Total(
                size,
                cfg.plans[k],
                cfg.far,
                sc.own[k],
                kept,
                inbox,
                extra,
                sc.result[k],
                send,
                recv,
            )
        )

    def adv(*which):
        for k in which:
            if groups[k].count == 0:
                groups[k].start()
            elif groups[k].busy:
                groups[k].advance()
                if not groups[k].busy:
                    store(sc.result[k], vars(outs)["sum%d" % k])

    summed_grad_own()
    tokens_in()
    summed_grad_edge()
    hidden_two_grad(near_pair)
    hidden_one()
    conv_one(near_pair)
    film()
    hidden_two_grad(edge_pair)
    skip_back()
    skip_grad()
    st.tok = [send_tokens(sc.F, 0)]
    halo_one()
    conv_one(edge_pair)
    stats_two()
    st.tok += [send_tokens(sc.F, 1), send_tokens(sc.GA, 2), send_tokens(sc.GA, 3)]
    hidden_two()
    conv2_grad(0)
    adv(1)
    conv2_grad(1)
    adv(2)
    conv2_grad(2)
    adv(3)
    adv(1)
    summed(near_pair)
    adv(2)
    adv(3)
    conv_one_grad()
    adv(1)
    conv1_grad(0)
    conv1_grad(1)
    adv(7)
    conv1_grad(2)
    adv(8)
    halo_two()
    summed(edge_pair)
    summed_swap()
    adv(3)
    adv(2)
    adv(7)
    adv(8)
    down_grad(0)
    adv(4)
    down_grad(1)
    adv(5)
    down_grad(2)
    adv(6)
    for copy in st.tok:
        copy.wait()
    project(0)
    project(1)
    adv(1)
    adv(4)
    adv(5)
    adv(3)
    adv(6)
    scores()
    softmax(0, 7)
    adv(8)
    adv(2)
    adv(1)
    adv(7)
    adv(5)
    attend()
    attention_back()
    attention_grads()
    adv(0)
    adv(4)
    adv(2)
    adv(6)
    adv(1)
    adv(8)
    adv(3)
    hidden_one_grad(near_pair)
    adv(0)
    adv(7)
    halo_grad()
    hidden_one_grad(edge_pair)
    stats_four()
    adv(2)
    adv(4)
    adv(3)
    adv(5)
    adv(6)
    down(1)
    halo_summed()
    down(0)
    store(sc.block, outs.block_out)
    adv(1)
    adv(8)
    image_grad()
    adv(3)
    adv(0)
    adv(7)
    adv(5)
    adv(8)
    packet_step()
    adv(2)
    adv(4)
    adv(1)
    adv(5)
    adv(8)
    adv(6)
    packet_step()
    adv(1)
    adv(3)
    adv(2)
    adv(0)
    adv(7)
    adv(4)
    packet_step()
    adv(2)
    adv(6)
    adv(3)
    adv(5)
    adv(8)
    adv(6)
    packet_step()
    adv(7)
    adv(0)
    adv(4)
    adv(3)
    adv(5)
    adv(8)
    adv(3)
    adv(5)
    adv(7)
    adv(0)
    adv(7)
    adv(8)
    adv(4)
    adv(0)
    adv(8)
    adv(4)

    while any(group.busy for group in groups):
        adv(*range(len(groups)))
    while pk_state[0] < len(cfg.bits):
        packet_step()
    store(sc.packet, outs.packet)
    for copy in stores + swaps:
        copy.wait()
    for copy in loading:
        copy.wait()


class Config:
    pass


def finish_kernel(cfg, *refs):
    n_in = len(cfg.finish_in)
    ins = Names(zip(cfg.finish_in, refs[:n_in]))
    n_out = len(cfg.finish_out)
    outs = Names(zip(cfg.finish_out, refs[n_in : n_in + n_out]))
    sc = Names(refs[n_in + n_out])
    ch, chi = cfg.ch, cfg.chi
    copies = []

    def begin(src, dst):
        copy = pltpu.make_async_copy(src, dst, sc.sem.at[len(copies)])
        copy.start()
        copies.append(copy)
        return copy

    order = cfg.done_order
    got = [begin(vars(ins)["sum%d" % k], sc.low[k]) for k in order]
    through = [
        begin(ins.image_grad, sc.image_grad),
        begin(ins.features_grad, sc.features_grad),
        begin(ins.block_out, sc.block_out),
        begin(ins.attended, sc.attended),
    ]
    passed = (
        (sc.image_grad, outs.image_grad),
        (sc.features_grad, outs.features_grad),
        (sc.block_out, outs.block_out),
        (sc.attended, outs.attended),
    )
    waits = []

    def packet_rows(k):
        return ins.packet[pl.ds(k, cfg.dp, stride=16), :]

    def wide_rows(k):
        return jnp.concatenate([packet_rows(k), packet_rows(k + 1)], axis=1)

    first, second = wide_rows(4), wide_rows(6)
    scale_grad = ins.norm2_gain[...] * second + ins.norm2_bias[...] * first
    film = jnp.concatenate([scale_grad, first], axis=1)
    embed = jnp.concatenate([wide_rows(0), wide_rows(2)], axis=1)
    outs.film_w[...] = lax.dot_general(
        embed,
        film,
        (((0,), (0,)), ((), ())),
        precision=lax.Precision.HIGHEST,
        preferred_element_type=F32,
    )
    outs.film_b[...] = jnp.sum(film, axis=0, keepdims=True)
    outs.gain2[...] = jnp.sum(wide_rows(10), axis=0, keepdims=True)
    outs.bias2[...] = jnp.sum(wide_rows(8), axis=0, keepdims=True)
    outs.gain1[...] = jnp.sum(packet_rows(13), axis=0, keepdims=True)
    outs.bias1[...] = jnp.sum(packet_rows(12), axis=0, keepdims=True)

    def widen(low, wide, size):
        step = 128

        @pl.loop(0, size // step)
        def _(i):
            here = part(i * step, step)
            wide[here, 0:128] = low[0, here, :].astype(F32)
            wide[here, 128:256] = low[1, here, :].astype(F32)

    places = {}
    for at, group in enumerate((1, 2, 3)):
        places[group] = [(0, 3 * ch, outs.conv2.at[pl.ds(at * 3 * ch, 3 * ch)])]
    for at, group in enumerate((4, 5, 6)):
        places[group] = [(0, 3 * ch, outs.down.at[pl.ds(at * 3 * ch, 3 * ch)])]
    places[7] = [(0, 6 * chi, outs.conv1.at[pl.ds(0, 6 * chi)])]
    places[8] = [(0, 3 * chi, outs.conv1.at[pl.ds(6 * chi, 3 * chi)]), (3 * chi, chi, outs.skip)]
    for k, copy in zip(order, got):
        copy.wait()
        if k == 0:
            for i in range(4):
                wide = sc.wide[0] if i < 3 else sc.wide_p
                at = i * ch if i < 3 else 0
                for j in range(2):
                    value = sc.low[0][j, i * ch : (i + 1) * ch, :].astype(F32)
                    wide[:, at + j * 128 : at + (j + 1) * 128] = value
            waits.append(begin(sc.wide[0], outs.qkv))
            waits.append(begin(sc.wide_p, outs.proj))
        else:
            widen(sc.low[k], sc.wide[k], cfg.groups[k])
            for start, size, dst in places[k]:
                waits.append(begin(sc.wide[k].at[pl.ds(start, size)], dst))
    for (src, dst), copy in zip(passed, through):
        copy.wait()
        waits.append(begin(src, dst))
    for copy in waits:
        copy.wait()


def body(
    image_in,
    noise_in,
    sigma_in,
    embedding,
    features,
    norm1_gain,
    norm1_bias,
    conv1_w,
    film_w,
    film_b,
    norm2_gain,
    norm2_bias,
    conv2_w,
    skip_w,
    down_w,
    qkv_w,
    proj_w,
    down_cot,
    attn_cot,
):
    cfg = Config()
    cfg.rows, cfg.cols, cfg.chi = image_in.shape[1:]
    cfg.ch = conv1_w.shape[3]
    cfg.tokens = features.shape[1]
    cfg.dp = lax.axis_size("dp")
    cfg.bits = [2**k for k in range(cfg.dp.bit_length() - 1)]
    cfg.far = cfg.bits[4:]
    rows, cols, chi, ch, dp = cfg.rows, cfg.cols, cfg.chi, cfg.ch, cfg.dp
    half = cols // 2
    cfg.groups = [4 * ch] + [3 * ch] * 6 + [6 * chi, 4 * chi]
    cfg.plans = [
        [[1], ["rows", 2], [4, 8]],
        [[1], [2], [4, 8], ["rows"]],
        [[1], [2], [4, 8], ["rows"]],
        [[1], [4], [2], [8], ["rows"]],
        [[1], [4], ["rows", 2], [8]],
        [[1], [2], [4, 8], ["rows"]],
        [[1], ["rows", 2], [4, 8]],
        [[1], [4], ["rows", 2], [8]],
        [[1], [2], [4], [8], ["rows"]],
    ]
    cfg.done_order = (1, 2, 6, 3, 5, 7, 0, 8, 4)
    args = dict(
        sigma_in=sigma_in,
        image_in=image_in[0],
        noise_in=noise_in[0],
        down_cot=down_cot[0],
        norm1_gain=norm1_gain.reshape(1, chi),
        norm1_bias=norm1_bias.reshape(1, chi),
        down_w=down_w.reshape(3, 3 * ch, ch),
        conv1_w=conv1_w.reshape(3, 3 * chi, ch),
        conv2_w=conv2_w.reshape(3, 3 * ch, ch),
        features=features[0],
        attn_cot=attn_cot[0],
        skip_w=skip_w,
        embedding=embedding,
        film_w=film_w,
        film_b=film_b.reshape(1, 2 * ch),
        norm2_gain=norm2_gain.reshape(1, ch),
        norm2_bias=norm2_bias.reshape(1, ch),
        qkv_w=qkv_w,
        proj_w=proj_w,
    )
    cfg.inputs = tuple(args)
    shape = jax.ShapeDtypeStruct
    out_shapes = dict(
        block_out=shape((2, half, ch), BF),
        attended=shape((cfg.tokens, ch), BF),
        image_grad=shape((rows, cols, chi), F32),
        features_grad=shape((cfg.tokens, ch), F32),
        packet=shape((dp, 16, 128), F32),
    )
    for k, size in enumerate(cfg.groups):
        out_shapes["sum%d" % k] = shape((2, size, 128), BF)
    cfg.outputs = tuple(out_shapes)
    vm = pltpu.VMEM
    scratch = {
        name: vm(value.shape, value.dtype)
        for name, value in args.items()
        if value is not sigma_in and value is not args["down_cot"]
    }
    scratch.update(
        dc=vm((4, half, ch), BF),
        xs=vm((rows, cols, chi), F32),
        stage_i=vm((chi // 128, cols + 16, 128), F32),
        stage_c=vm((ch // 128, cols + 16, 128), F32),
        stage_h=vm((ch // 128, half + 16, 128), F32),
        h1c=vm((rows + 2, cols, 3 * chi), BF),
        h2c=vm((rows + 2, cols, 3 * ch), BF),
        sg3=vm((rows + 2, cols, 3 * ch), BF),
        cg3=vm((rows + 2, cols, 3 * ch), BF),
        s3=vm((rows + 1, half, 3 * ch), BF),
        c1=vm((rows, cols, ch), F32),
        g2=vm((rows, cols, ch), F32),
        h1g=vm((rows, cols, chi), F32),
        skb=vm((rows, cols, chi), F32),
        block=vm((2, half, ch), BF),
        st_out=vm((4, 8, ch), F32),
        st_in=vm((4, 8, ch), F32),
        packet=vm((dp, 16, 128), F32),
        F=vm((2, TOKENS, ch), BF),
        GA=vm((2, TOKENS, ch), BF),
        Q=vm((2, TOKENS, ch), BF),
        K=vm((2, TOKENS, ch), BF),
        V=vm((2, TOKENS, ch), BF),
        MG=vm((2, TOKENS, ch), BF),
        S=vm((2 * TOKENS, 2 * TOKENS), F32),
        D=vm((2 * TOKENS, 2 * TOKENS), F32),
        PR=vm((2 * TOKENS, 2 * TOKENS), BF),
        DS=vm((2 * TOKENS, 2 * TOKENS), BF),
        PG=vm((TOKENS, 3 * ch), BF),
        att=vm((cfg.tokens, ch), BF),
        fg=vm((cfg.tokens, ch), F32),
        own=[vm((2, size, 128), BF) for size in cfg.groups],
        result=[vm((2, size, 128), BF) for size in cfg.groups],
        sums=[total_scratch(*plan, cfg.far) for plan in zip(cfg.groups, cfg.plans)],
        load_sem=pltpu.SemaphoreType.DMA((len(args),)),
        store_sem=pltpu.SemaphoreType.DMA((len(out_shapes),)),
        x_send=pltpu.SemaphoreType.DMA((13,)),
        x_recv=pltpu.SemaphoreType.DMA((13,)),
        pk_send=pltpu.SemaphoreType.DMA((len(cfg.bits),)),
        pk_recv=pltpu.SemaphoreType.DMA((len(cfg.bits),)),
    )
    made = pl.pallas_call(
        functools.partial(level_kernel, cfg),
        out_shape=list(out_shapes.values()),
        in_specs=[SMEM] + [ANY] * (len(args) - 1),
        out_specs=[ANY] * len(out_shapes),
        scratch_shapes=[scratch],
        compiler_params=pltpu.CompilerParams(
            collective_id=0, has_side_effects=True, vmem_limit_bytes=62 * 2**20
        ),
        name="level",
    )(*args.values())
    made = dict(zip(cfg.outputs, made))

    small = dict(
        packet=made["packet"].reshape(dp * 16, 128),
        norm2_gain=args["norm2_gain"],
        norm2_bias=args["norm2_bias"],
    )
    big = {name: value for name, value in made.items() if name not in small}
    cfg.finish_in = tuple(small) + tuple(big)
    finals = dict(
        block_out=out_shapes["block_out"],
        attended=out_shapes["attended"],
        image_grad=out_shapes["image_grad"],
        features_grad=out_shapes["features_grad"],
        conv1=shape((9 * chi, ch), F32),
        conv2=shape((9 * ch, ch), F32),
        skip=shape((chi, ch), F32),
        down=shape((9 * ch, ch), F32),
        qkv=shape((ch, 3 * ch), F32),
        proj=shape((ch, ch), F32),
    )
    finals_small = dict(
        gain1=shape((1, chi), F32),
        bias1=shape((1, chi), F32),
        film_w=shape((2 * ch, 2 * ch), F32),
        film_b=shape((1, 2 * ch), F32),
        gain2=shape((1, ch), F32),
        bias2=shape((1, ch), F32),
    )
    cfg.finish_out = tuple(finals_small) + tuple(finals)
    finish_scratch = dict(
        low=[vm((2, size, 128), BF) for size in cfg.groups],
        wide=[vm((ch, 3 * ch), F32)] + [vm((size, ch), F32) for size in cfg.groups[1:]],
        wide_p=vm((ch, ch), F32),
        image_grad=vm((rows, cols, chi), F32),
        features_grad=vm((cfg.tokens, ch), F32),
        block_out=vm((2, half, ch), BF),
        attended=vm((cfg.tokens, ch), BF),
        sem=pltpu.SemaphoreType.DMA((32,)),
    )
    done = pl.pallas_call(
        functools.partial(finish_kernel, cfg),
        out_shape=list(finals_small.values()) + list(finals.values()),
        in_specs=[VMEM_SPEC] * len(small) + [ANY] * len(big),
        out_specs=[VMEM_SPEC] * len(finals_small) + [ANY] * len(finals),
        scratch_shapes=[finish_scratch],
        compiler_params=pltpu.CompilerParams(vmem_limit_bytes=56 * 2**20),
        name="finish",
    )(*small.values(), *big.values())
    done = Names(zip(cfg.finish_out, done))
    return (
        done.block_out[None],
        done.attended[None],
        done.image_grad[None],
        done.features_grad[None],
        done.gain1.reshape(chi),
        done.bias1.reshape(chi),
        done.conv1.reshape(conv1_w.shape),
        done.film_w,
        done.film_b.reshape(2 * ch),
        done.gain2.reshape(ch),
        done.bias2.reshape(ch),
        done.conv2.reshape(conv2_w.shape),
        done.skip,
        done.down.reshape(down_w.shape),
        done.qkv,
        done.proj,
    )


def solution(mesh):
    placed = (
        P("dp", "rows", None, None),
        P("dp", "rows", None, None),
        P("dp"),
        P("dp", None),
        P("dp", "rows", None),
        P(),
        P(),
        P(),
        P(),
        P(),
        P(),
        P(),
        P(),
        P(),
        P(),
        P(),
        P(),
        P("dp", "rows", None, None),
        P("dp", "rows", None),
    )
    return jax.shard_map(
        body,
        mesh=mesh,
        in_specs=placed,
        out_specs=(
            P("dp", "rows", None, None),
            P("dp", "rows", None),
            P("dp", "rows", None, None),
            P("dp", "rows", None),
            P(),
            P(),
            P(),
            P(),
            P(),
            P(),
            P(),
            P(),
            P(),
            P(),
            P(),
            P(),
        ),
        check_vma=False,
    )
```

```python
import functools

import jax
import jax.numpy as jnp
from jax import lax
from jax.experimental import pallas as pl
from jax.experimental.pallas import tpu as pltpu
from jax.sharding import PartitionSpec as P

G = 32
EPSILON = 1e-05
SIGMA_DATA = 0.5
MESH = pl.DeviceIdType.MESH
ANY = pl.BlockSpec(memory_space=pl.ANY)
SMEM = pl.BlockSpec(memory_space=pltpu.SMEM)
BF = jnp.bfloat16
F32 = jnp.float32
TOKENS = 448
KEYS = 400


def flip(index, bit):
    return index + bit * (1 - 2 * ((index // bit) % 2))


class Side:
    def __init__(self, names):
        d = lax.axis_index("dp")
        r = lax.axis_index("rows")
        self.mine = []
        for name in names:
            self.mine.append(r if name == "rows" else (d // name) % 2)
        self.parts = 2 ** len(names)
        self.names = names
        self.position = (d, r)

    def partners(self):
        found = []
        for flips in range(1, self.parts):
            d, r = self.position
            index = 0
            for k, name in enumerate(self.names):
                other = (flips >> k) % 2
                side = self.mine[k]
                if other:
                    side = 1 - side
                    if name == "rows":
                        r = 1 - r
                    else:
                        d = flip(d, name)
                index = index * 2 + side
            found.append(((d, r), index))
        return found

    @property
    def index(self):
        index = 0
        for side in self.mine:
            index = index * 2 + side
        return index


def part(start, size):
    return pl.ds(pl.multiple_of(start, size), size)


class Total:
    def __init__(self, rows, stages, whole, own, kept, inbox, extra, result, send, recv):
        self.rows = rows
        self.stages = [Side(names) for names in stages]
        self.whole = [Side([name]) for name in whole]
        self.own = own
        self.kept = kept
        self.inbox = inbox
        self.extra = extra
        self.result = result
        self.send = send
        self.recv = recv
        self.sizes = sizes_of(rows, stages)
        self.steps = len(stages)
        self.copies = None
        self.count = 0

    def begin(self, src, dst, where):
        k = self.count
        self.count += 1
        copy = pltpu.make_async_remote_copy(
            src_ref=src,
            dst_ref=dst,
            send_sem=self.send.at[k],
            recv_sem=self.recv.at[k],
            device_id=where,
            device_id_type=MESH,
        )
        copy.start()
        self.copies.append(copy)

    def scatter(self, step):
        side = self.stages[step]
        size = self.sizes[step]
        for slot, (where, index) in enumerate(side.partners()):
            if step == 0:
                src = self.own.at[index]
            else:
                src = self.kept[step - 1].at[part(index * size, size)]
            self.begin(src, self.inbox[step].at[slot], where)

    def start(self):
        self.copies = []
        self.scatter(0)
        self.stage = 0

    def region(self, step):
        lead = self.stages[0].index
        if step == 0:
            return self.result.at[lead]
        offset = 0
        for t in range(1, step + 1):
            offset = offset + self.stages[t].index * self.sizes[t]
        return self.result.at[lead, part(offset, self.sizes[step])]

    def gather(self, step):
        mine = self.region(step)
        for where, _ in self.stages[step].partners():
            self.begin(mine, mine, where)

    def swap_whole(self, k):
        (where, _), = self.whole[k].partners()
        self.begin(self.kept[self.steps - 1 + k], self.extra.at[k], where)

    def advance(self):
        stage = self.stage
        last = self.steps - 1
        for copy in self.copies:
            copy.wait()
        self.copies = []
        if stage < self.steps:
            side = self.stages[stage]
            size = self.sizes[stage]
            if stage == 0:
                have = self.own.at[side.index]
            else:
                have = self.kept[stage - 1].at[part(side.index * size, size)]
            if stage == last and not self.whole:
                dest = self.region(last)
            else:
                dest = self.kept[stage]
            add_rows(dest, have, self.inbox[stage], side.parts - 1, size)
            if stage < last:
                self.scatter(stage + 1)
            elif self.whole:
                self.swap_whole(0)
            else:
                self.gather(last)
        elif stage < self.steps + len(self.whole):
            k = stage - self.steps
            final = k == len(self.whole) - 1
            dest = self.region(last) if final else self.kept[last + k + 1]
            add_rows(dest, self.kept[last + k], self.extra.at[pl.ds(k, 1)], 1, self.sizes[last])
            if final:
                self.gather(last)
            else:
                self.swap_whole(k + 1)
        else:
            k = stage - self.steps - len(self.whole)
            if k < last:
                self.gather(last - 1 - k)
            else:
                self.copies = None
        self.stage = stage + 1

    @property
    def busy(self):
        return self.copies is not None


def add_rows(dest, have, got, count, size):
    block = size
    while block > 400:
        block //= 2 if (block // 2) % 16 == 0 else 3

    def add(here):
        value = have[here].astype(jnp.float32)
        for slot in range(count):
            value = value + got[slot, here].astype(jnp.float32)
        dest[here] = value.astype(jnp.bfloat16)

    if block == size:
        add(pl.ds(0, size))
    else:

        @pl.loop(0, size // block)
        def _(i):
            add(part(i * block, block))


def sizes_of(rows, stages):
    sizes = [rows]
    for names in stages[1:]:
        sizes.append(sizes[-1] // 2 ** len(names))
    return sizes


def copies_of(stages, whole):
    return 2 * sum(2 ** len(names) - 1 for names in stages) + len(whole)


def total_scratch(rows, stages, whole):
    sizes = sizes_of(rows, stages)
    kept = [pltpu.VMEM((size, 128), jnp.bfloat16) for size in sizes + [sizes[-1]] * len(whole)]
    inbox = [
        pltpu.VMEM((2 ** len(names) - 1, size, 128), jnp.bfloat16)
        for names, size in zip(stages, sizes)
    ]
    extra = pltpu.VMEM((max(len(whole), 1), sizes[-1], 128), jnp.bfloat16)
    count = copies_of(stages, whole)
    return [
        kept,
        inbox,
        extra,
        pltpu.SemaphoreType.DMA((count,)),
        pltpu.SemaphoreType.DMA((count,)),
    ]


class Names:
    def __init__(self, pairs=()):
        vars(self).update(pairs)


class Once:
    def __init__(self, copy):
        self.copy = copy
        self.waited = False
        copy.start()

    def wait(self):
        if not self.waited:
            self.waited = True
            self.copy.wait()


def nn(left, right):
    return lax.dot_general(left, right, (((1,), (0,)), ((), ())), preferred_element_type=F32)


def nt(left, right):
    return lax.dot_general(left, right, (((1,), (1,)), ((), ())), preferred_element_type=F32)


def tn(left, right):
    return lax.dot_general(left, right, (((0,), (0,)), ((), ())), preferred_element_type=F32)


def fold(value):
    rows, lanes = value.shape
    return jnp.sum(value.reshape(rows // 8, 8, lanes), axis=0)


def one_row(value):
    return jnp.sum(value, axis=0, keepdims=True)


def group_sum(value, width):
    lanes = value.shape[1]
    lane = lax.broadcasted_iota(jnp.int32, value.shape, 1)
    step = 1
    while step < width:
        up = pltpu.roll(value, lanes - step, 1)
        down = pltpu.roll(value, step, 1)
        value = value + jnp.where((lane // step) % 2 == 0, up, down)
        step *= 2
    return value


def sigmoid(value):
    return 0.5 + 0.5 * jnp.tanh(0.5 * value)


def spread(row, staged, lanes):
    cells = row.shape[0]
    for b in range(3):
        for k in range(lanes // 128):
            at = b * lanes + k * 128
            row[:, at : at + 128] = staged[k, 7 + b : 7 + b + cells, :].astype(BF)


def put(staged, start, value):
    cells, lanes = value.shape
    for k in range(lanes // 128):
        staged[k, pl.ds(start, cells), :] = value[:, k * 128 : (k + 1) * 128]


def level_kernel(cfg, *refs):
    n_in = len(cfg.inputs)
    ins = Names(zip(cfg.inputs, refs[:n_in]))
    outs = Names(zip(cfg.outputs, refs[n_in : n_in + len(cfg.outputs)]))
    sc = Names(refs[n_in + len(cfg.outputs)])
    st = Names()
    rows, cols, chi, ch = cfg.rows, cfg.cols, cfg.chi, cfg.ch
    half = cols // 2
    r = lax.axis_index("rows")
    d = lax.axis_index("dp")
    across = (d, 1 - r)

    loads = Names()
    loading = []

    def load(name, dst):
        copy = Once(pltpu.make_async_copy(vars(ins)[name], dst, sc.load_sem.at[len(loading)]))
        loading.append(copy)
        setattr(loads, name, copy)

    stores = []

    def store(src, dst):
        copy = pltpu.make_async_copy(src, dst, sc.store_sem.at[len(stores)])
        copy.start()
        stores.append(copy)

    def swap_copy(k, src, dst):
        return pltpu.make_async_remote_copy(
            src_ref=src,
            dst_ref=dst,
            send_sem=sc.x_send.at[k],
            recv_sem=sc.x_recv.at[k],
            device_id=across,
            device_id_type=MESH,
        )

    swaps = []

    def swap(k, src, dst):
        copy = Once(swap_copy(k, src, dst))
        swaps.append(copy)
        return copy

    barrier = pltpu.get_barrier_semaphore()
    greeted = {}
    for stages in cfg.plans:
        for names in stages + [[name] for name in cfg.far]:
            side = Side(names)
            for flips, (where, _) in enumerate(side.partners(), 1):
                met = frozenset(n for k, n in enumerate(names) if (flips >> k) % 2)
                greeted[met] = where
    for where in greeted.values():
        pl.semaphore_signal(barrier, inc=1, device_id=where, device_id_type=MESH)

    sc.down_cot = sc.dc.at[1:3]
    names = cfg.inputs[1:]
    for name in names[:4]:
        load(name, vars(sc)[name])

    sigma = jnp.full((1, chi), ins.sigma_in[0], F32)
    scale_in = lax.rsqrt(SIGMA_DATA * SIGMA_DATA + sigma * sigma)
    loads.image_in.wait()
    loads.noise_in.wait()
    for name in names[4:]:
        load(name, vars(sc)[name])
    piece = cols // 4

    def stats_one(i, carry):
        row, col = i // 4, i % 4
        here = part(col * piece, piece)
        value = scale_in * (
            sc.image_in[row, here].astype(F32) + sigma * sc.noise_in[row, here].astype(F32)
        )
        sc.xs[row, here] = value
        sc.image_in[row, here] = value.astype(BF)
        return carry[0] + fold(value), carry[1] + fold(value * value)

    zero8 = jnp.zeros((8, chi), F32)
    sum_a, sum_b = lax.fori_loop(0, rows * 4, stats_one, (zero8, zero8))
    low_in = sc.image_in

    def send_stats(k, top, bottom):
        lanes = top.shape[1]
        sc.st_out[k, 0:1, 0:lanes] = top
        sc.st_out[k, 1:2, 0:lanes] = bottom
        copy = swap(1 + k, sc.st_out.at[k], sc.st_in.at[k])
        return copy

    def both_stats(k, copy, lanes):
        copy.wait()
        total = sc.st_out[k, :, 0:lanes] + sc.st_in[k, :, 0:lanes]
        return total[0:1], total[1:2]

    pl.semaphore_wait(barrier, len(greeted))
    swap_one = send_stats(0, one_row(sum_a), one_row(sum_b))

    edge = 4 - 3 * r
    rows_one = [swap(6, low_in.at[edge - 1], sc.xh.at[0])]

    def send_next_row():
        rows_one.append(swap(8, low_in.at[2 - r], sc.xh.at[1]))

    dc_swap = swap(0, ins.down_cot.at[1 - r], sc.dc.at[3 * r])
    dc_more = swap_copy(5, ins.down_cot.at[1], sc.dc.at[4])

    def down_cot_more():
        @pl.when(r == 1)
        def _():
            dc_more.start()

    for ref in (sc.stage_i, sc.stage_o, sc.stage_c, sc.stage_h):
        zeros = jnp.zeros((ref.shape[0], 8, 128), F32)
        ref[:, 0:8, :] = zeros
        ref[:, ref.shape[1] - 8 :, :] = zeros
    outer = 5 * r
    inner = 5 * (1 - r)
    sc.h1c[outer + 1] = jnp.zeros((cols, 3 * chi), BF)
    sc.h2c[outer] = jnp.zeros((cols, 3 * ch), BF)
    sc.cg[outer] = jnp.zeros((cols, ch), BF)
    sc.sg3[outer + 1] = jnp.zeros((cols, 3 * ch), BF)
    sc.dc[3 * r] = jnp.zeros((half, ch), BF)
    for ref in (sc.F, sc.GA):
        ref[1, 400:, :] = jnp.zeros((TOKENS - 400, ch), BF)

    @pl.when(r == 0)
    def _():
        sc.s3[0] = jnp.zeros((half, 3 * ch), BF)

    dw = sc.down_w
    loads.down_cot.wait()
    loads.down_w.wait()

    def shifted_cot(m):
        staged = sc.stage_h
        put(staged, 8, sc.dc[m].astype(F32))
        right = [staged[k, 9 : 9 + half, :].astype(BF) for k in range(ch // 128)]
        return sc.dc[m], jnp.concatenate(right, axis=1)

    def dw_tap(a, b):
        return dw[a, b * ch : (b + 1) * ch, :]

    def even_row(m):
        here, right = shifted_cot(m)
        return nt(here, dw_tap(1, 1)), nt(here, dw_tap(1, 2)) + nt(right, dw_tap(1, 0))

    def odd_row(m):
        here, right = shifted_cot(m)
        even = nt(here, dw_tap(2, 1))
        odd = nt(here, dw_tap(2, 2)) + nt(right, dw_tap(2, 0))
        here, right = shifted_cot(m + 1)
        even += nt(here, dw_tap(0, 1))
        odd += nt(here, dw_tap(0, 2)) + nt(right, dw_tap(0, 0))
        return even, odd

    def put_row(l, pair):
        staged = sc.stage_c
        for k in range(ch // 128):
            for odd in range(2):
                value = pair[odd][:, k * 128 : (k + 1) * 128]
                staged[k, pl.ds(8 + odd, half, stride=2), :] = value
        spread(sc.sg3.at[l + 1], staged, ch)

    def summed_grad_own():
        @pl.loop(0, 2)
        def _(k):
            put_row(1 + 2 * k, even_row(1 + k))

        put_row(2, odd_row(1))

        @pl.when(r == 1)
        def _():
            put_row(4, odd_row(2))

    def summed_grad_edge():
        dc_swap.wait()

        @pl.when(r == 0)
        def _():
            put_row(4, odd_row(2))
            put_row(5, even_row(3))

        @pl.when(r == 1)
        def _():
            put_row(0, odd_row(0))

    def summed_grad_more():
        @pl.when(r == 0)
        def _():
            dc_more.wait_recv()
            put_row(6, odd_row(3))

        @pl.when(r == 1)
        def _():
            dc_more.wait_send()
            put_row(-1, even_row(0))

    gain1 = lambda: sc.norm1_gain[...]
    bias1 = lambda: sc.norm1_bias[...]
    count1 = float(2 * rows * cols * (chi // G))
    count2 = float(2 * rows * cols * (ch // G))

    def moments(first, second, width, count):
        mean = group_sum(first, width) / count
        return mean, lax.rsqrt(group_sum(second, width) / count - mean * mean + EPSILON)

    st.sums2 = (0.0, 0.0)
    st.tok = []
    st.sums4 = (zero8, zero8)

    def row_one(place, values):
        mean, inverse = st.mean1, st.inv1

        @pl.loop(0, 4)
        def _(c):
            here = part(c * piece, piece)
            pre = (values[here].astype(F32) - mean) * inverse * gain1() + bias1()
            put(sc.stage_i, pl.multiple_of(8 + c * piece, 8), pre * sigmoid(pre))

        spread(sc.h1c.at[place], sc.stage_i, chi)

    def hidden_one():
        loads.norm1_gain.wait()
        loads.norm1_bias.wait()
        first, second = both_stats(0, swap_one, chi)
        st.mean1, st.inv1 = moments(first, second, chi // G, count1)

        @pl.loop(0, rows)
        def _(i):
            row_one(2 + i, sc.xs.at[i])

    def hidden_one_halo(k):
        rows_one[k].wait()
        row_one(inner + 1 if k == 0 else 7 * (1 - r), sc.xh.at[k])

    near_pair = 1 + 2 * r
    edge_pair = 3 - 2 * r

    def conv_rows(source, weight, base, count, lanes):
        left = [
            source[pl.ds(base - 1 + a, count)].reshape(count * cols, 3 * lanes) for a in range(3)
        ]
        return nn(jnp.concatenate(left, axis=1), weight[...].reshape(9 * lanes, ch))

    def conv_one(base):
        loads.conv1_w.wait()
        acc = conv_rows(sc.h1c, sc.conv1_w, base + 1, 2, chi)
        sc.c1[pl.ds(base - 1, 2)] = acc.reshape(2, cols, ch)
        sums = fold(acc), fold(acc * acc)
        st.sums2 = tuple(x + y for x, y in zip(st.sums2, sums))

    def conv_one_halo():
        sc.c1[rows] = conv_rows(sc.h1c, sc.conv1_w, inner + 1, 1, chi)

    def stats_two():
        first, second = st.sums2
        st.swap2 = send_stats(1, one_row(first), one_row(second))

    def back_pair(source, weight, base, lanes):
        return back_rows(source, weight, base, 2, lanes)

    def back_rows(source, weight, base, count, lanes):
        acc = None
        for a in range(3):
            for b in range(3):
                left = source[pl.ds(base - 1 + a, count), :, b * ch : (b + 1) * ch]
                term = nt(
                    left.reshape(count * cols, ch), weight[2 - a, (2 - b) * lanes : (3 - b) * lanes, :]
                )
                acc = term if acc is None else acc + term
        return acc

    def hidden_two_grad(base):
        loads.conv2_w.wait()
        acc = back_pair(sc.sg3, sc.conv2_w, base + 1, ch)
        sc.g2[pl.ds(base - 1, 2)] = acc.reshape(2, cols, ch)

    def hidden_two_grad_halo():
        sc.g2[rows] = back_rows(sc.sg3, sc.conv2_w, inner + 1, 1, ch)

    def grad_rows():
        return sc.sg3[2:6, :, ch : 2 * ch].reshape(rows * cols, ch)

    down_at = [(4, 0), (5, 0), (6, 0)]
    conv1_at = [(7, 0), (7, 3 * chi), (8, 0)]
    skip_at = (8, 3 * chi)

    def put_grad(place, value):
        group, start = place
        low = value.astype(BF)
        size = low.shape[0]
        sc.own[group][0, start : start + size, :] = low[:, :128]
        sc.own[group][1, start : start + size, :] = low[:, 128:]

    def skip_back():
        loads.skip_w.wait()
        sc.skb[...] = nt(grad_rows(), sc.skip_w[...]).reshape(rows, cols, chi)

    def skip_grad():
        put_grad(skip_at, tn(low_in[...].reshape(rows * cols, chi), grad_rows()))

    def film():
        for copy in (
            loads.embedding,
            loads.film_w,
            loads.film_b,
            loads.norm2_gain,
            loads.norm2_bias,
        ):
            copy.wait()
        row = nn(sc.embedding[...], sc.film_w[...]) + sc.film_b[...]
        scale = 1.0 + row[:, :ch]
        shift = row[:, ch:]
        gain, bias = sc.norm2_gain[...], sc.norm2_bias[...]
        st.scale = scale
        st.pre_gain = gain * scale
        st.pre_bias = bias * scale + shift

    def hidden_two():
        first, second = both_stats(1, st.swap2, ch)
        mean, inverse = moments(first, second, ch // G, count2)
        st.mean2, st.inv2 = mean, inverse
        step = cols // 8

        def row_of(l, carry):
            staged = sc.stage_c

            def cells(c, carry):
                here = part(c * step, step)
                hat = (sc.c1[l - 1, here] - mean) * inverse
                sc.c1[l - 1, here] = hat
                pre = hat * st.pre_gain + st.pre_bias
                gate = sigmoid(pre)
                value = pre * gate
                put(staged, pl.multiple_of(8 + c * step, 8), value)
                grad = sc.g2[l - 1, here] * (gate + value * (1.0 - gate))
                sc.g2[l - 1, here] = grad
                return carry[0] + fold(grad), carry[1] + fold(grad * hat)

            carry = lax.fori_loop(0, 8, cells, carry)
            spread(sc.h2c.at[l], staged, ch)
            return carry

        zero = jnp.zeros((8, ch), F32)
        carry = lax.fori_loop(0, rows, lambda i, carry: row_of(1 + i, carry), (zero, zero))
        st.swap3 = send_stats(2, one_row(carry[0]), one_row(carry[1]))

    def hidden_two_halo():
        step = cols // 8

        @pl.loop(0, 8)
        def _(c):
            here = part(c * step, step)
            hat = (sc.c1[rows, here] - st.mean2) * st.inv2
            sc.c1[rows, here] = hat
            pre = hat * st.pre_gain + st.pre_bias
            put(sc.stage_c, pl.multiple_of(8 + c * step, 8), pre * sigmoid(pre))

        spread(sc.h2c.at[inner], sc.stage_c, ch)

    def conv2_grad(b):
        left = sc.h2c[1:5, :, b * ch : (b + 1) * ch].reshape(rows * cols, ch)
        right = [
            sc.sg3[3 - a : 7 - a, :, ch : 2 * ch].reshape(rows * cols, ch) for a in range(3)
        ]
        grad = tn(left, jnp.concatenate(right, axis=1))
        for a in range(3):
            put_grad((1 + b, a * ch), grad[:, a * ch : (a + 1) * ch])

    def odd_shift(row):
        staged = sc.stage_h
        put(staged, 8, row[:, 2 * ch :].astype(F32))
        for k in range(ch // 128):
            row[:, k * 128 : (k + 1) * 128] = staged[k, 7 : 7 + half, :].astype(BF)

    def summed(base):
        acc = conv_rows(sc.h2c, sc.conv2_w, base, 2, ch)
        low = low_in[pl.ds(base - 1, 2)].reshape(2 * cols, chi)
        acc = (acc + nn(low, sc.skip_w[...])).reshape(2, cols, ch)
        for k in range(2):
            staged = sc.stage_c
            put(staged, 8, acc[k])
            row = sc.s3.at[base + k]
            for i in range(ch // 128):
                for odd in range(2):
                    at = (1 + odd) * ch + i * 128
                    value = staged[i, pl.ds(8 + odd, half, stride=2), :]
                    row[:, at : at + 128] = value.astype(BF)
            odd_shift(row)

    def summed_swap():
        copy = swap_copy(7, sc.s3.at[4, :, ch:], sc.s3.at[0, :, ch:])
        st.s3 = copy

        @pl.when(r == 0)
        def _():
            copy.start()

    def halo_summed():
        copy = st.s3

        @pl.when(r == 0)
        def _():
            copy.wait_send()

        @pl.when(r == 1)
        def _():
            copy.wait_recv()
            odd_shift(sc.s3.at[0])

    def down(k):
        acc = None
        for a in range(3):
            term = nn(sc.s3[2 * k + a], dw[a])
            acc = term if acc is None else acc + term
        sc.block[k] = acc.astype(BF)

    def down_grad(a):
        first, cot = ((2, 2), (1, 1), (2, 1))[a]
        value = tn(sc.s3[first], sc.dc[cot]) + tn(sc.s3[first + 2], sc.dc[cot + 1])
        put_grad(down_at[a], value)

    def back_two(grad, hat):
        return (grad * st.pre_gain - st.m1 - hat * st.m2) * st.inv2

    def conv_one_grad():
        first, second = both_stats(2, st.swap3, ch)
        st.A, st.B = first, second
        st.m1 = group_sum(first * st.pre_gain, ch // G) / count2
        st.m2 = group_sum(second * st.pre_gain, ch // G) / count2
        step = cols // 4

        @pl.loop(0, rows * 4)
        def _(i):
            row, here = i // 4, part(i % 4 * step, step)
            sc.cg[1 + row, here] = back_two(sc.g2[row, here], sc.c1[row, here]).astype(BF)

    def conv_one_grad_halo():
        step = cols // 4

        @pl.loop(0, 4)
        def _(c):
            here = part(c * step, step)
            hat = sc.c1[rows, here]
            pre = hat * st.pre_gain + st.pre_bias
            gate = sigmoid(pre)
            grad = sc.g2[rows, here] * (gate + pre * gate * (1.0 - gate))
            sc.cg[inner, here] = back_two(grad, hat).astype(BF)

    def conv1_grad():
        left = sc.h1c[2:6].reshape(rows * cols, 3 * chi)
        right = [sc.cg[2 - a : 6 - a].reshape(rows * cols, ch) for a in range(3)]
        grad = tn(left, jnp.concatenate(right, axis=1))
        for a in range(3):
            put_grad(conv1_at[a], grad[:, a * ch : (a + 1) * ch])

    def hidden_one_grad(base):
        acc = None
        for a in range(3):
            left = sc.cg[pl.ds(base - 1 + a, 2)].reshape(2 * cols, ch)
            term = nt(left, sc.conv1_w[2 - a])
            acc = term if acc is None else acc + term
        acc = acc.reshape(2, cols, 3 * chi)
        for i in range(2):
            put(sc.stage_i, 8, acc[i, :, 0:chi])
            put(sc.stage_o, 8, acc[i, :, 2 * chi :])
            right = sc.stage_i[0, 9 : 9 + cols, :]
            left = sc.stage_o[0, 7 : 7 + cols, :]
            sc.h1g[base - 1 + i] = acc[i, :, chi : 2 * chi] + right + left

    def pre_one_grad(base):
        mean, inverse = st.mean1, st.inv1

        def cells(i, carry):
            row, col = base - 1 + i // 4, i % 4
            here = part(col * piece, piece)
            hat = (sc.xs[row, here] - mean) * inverse
            sc.xs[row, here] = hat
            pre = hat * gain1() + bias1()
            gate = sigmoid(pre)
            grad = sc.h1g[row, here] * (gate + pre * gate * (1.0 - gate))
            sc.h1g[row, here] = grad
            return carry[0] + fold(grad), carry[1] + fold(grad * hat)

        st.sums4 = lax.fori_loop(0, 8, cells, st.sums4)

    def stats_four():
        first, second = st.sums4
        st.swap4 = send_stats(3, one_row(first), one_row(second))

    def packet_begin():
        first, second = both_stats(3, st.swap4, chi)
        st.C, st.D = first, second
        pk = sc.packet.at[d]
        values = (
            sc.embedding[...].astype(F32),
            st.A,
            st.B,
            st.scale * st.A,
            st.scale * st.B,
            first,
            second,
            jnp.zeros((1, 256), F32),
        )
        at = 0
        for value in values:
            for k in range(value.shape[1] // 128):
                pk[at : at + 1, :] = value[:, k * 128 : (k + 1) * 128]
                at += 1
        packet_start()

    def image_grad():
        first, second = st.C, st.D
        m1 = group_sum(first * gain1(), chi // G) / count1
        m2 = group_sum(second * gain1(), chi // G) / count1

        @pl.loop(0, rows * 4)
        def _(i):
            row, col = i // 4, i % 4
            here = part(col * piece, piece)
            value = (
                sc.h1g[row, here] * gain1() - m1 - sc.xs[row, here] * m2
            ) * st.inv1 + sc.skb[row, here]
            sc.h1g[row, here] = scale_in * value

        store(sc.h1g, outs.image_grad)

    bits = [Side([bit]).partners()[0][0] for bit in cfg.bits]

    def packet_copy(k):
        size = cfg.bits[k]
        mine = sc.packet.at[pl.ds((d // size) * size, size)]
        return pltpu.make_async_remote_copy(
            src_ref=mine,
            dst_ref=mine,
            send_sem=sc.pk_send.at[k],
            recv_sem=sc.pk_recv.at[k],
            device_id=bits[k],
            device_id_type=MESH,
        )

    pk_state = [0]

    def packet_start():
        packet_copy(0).start()

    def packet_step():
        k = pk_state[0]
        packet_copy(k).wait()
        pk_state[0] = k + 1
        if k + 1 < len(cfg.bits):
            packet_copy(k + 1).start()

    tokens = cfg.tokens

    def tokens_in():
        loads.features.wait()
        loads.attn_cot.wait()
        for src, dst in ((sc.features, sc.F), (sc.attn_cot, sc.GA)):
            pad = jnp.zeros((TOKENS - tokens, ch), F32)
            dst[0] = jnp.concatenate([src[...].astype(F32), pad], axis=0).astype(BF)

    def send_tokens(ref, k):
        where = pl.ds(0, 208) if k % 2 == 0 else pl.ds(208, 192)
        return swap(9 + k, ref.at[0, where], ref.at[1, where])

    def project(k):
        loads.qkv_w.wait()
        loads.proj_w.wait()
        value = nn(sc.F[k], sc.qkv_w[...])
        for i, dst in enumerate((sc.Q, sc.K, sc.V)):
            dst[k] = value[: dst.shape[1], i * ch : (i + 1) * ch].astype(BF)
        sc.MG[k] = nt(sc.GA[k], sc.proj_w[...]).astype(BF)

    att_scale = ch ** (-0.5)

    def flat(ref):
        return ref[...].reshape(2 * ref.shape[1], ch)

    def scores():
        sc.S[...] = nt(flat(sc.K), flat(sc.Q))

    def prob_grads():
        sc.D[...] = nt(flat(sc.V), flat(sc.MG))

    def softmax(first, last):
        row = lax.broadcasted_iota(jnp.int32, (KEYS, 128), 0)
        real = row < tokens

        @pl.loop(first, last)
        def _(c):
            here = part(c * 128, 128)
            both = [pl.ds(0, KEYS), pl.ds(KEYS, KEYS)]
            value = [jnp.where(real, sc.S[keys, here] * att_scale, -1e30) for keys in both]
            most = jnp.max(jnp.maximum(value[0], value[1]), axis=0, keepdims=True)
            value = [jnp.exp(v - most) for v in value]
            scale = 1.0 / jnp.sum(value[0] + value[1], axis=0, keepdims=True)
            prob = [v * scale for v in value]
            for keys, v in zip(both, prob):
                sc.PR[keys, here] = v.astype(BF)
            back = [sc.D[keys, here] for keys in both]
            total = jnp.sum(prob[0] * back[0] + prob[1] * back[1], axis=0, keepdims=True)
            for keys, v, b in zip(both, prob, back):
                sc.DS[keys, here] = (v * (b - total)).astype(BF)

    def attend():
        mixed = tn(sc.PR[:, 0:512], flat(sc.V))[:KEYS].astype(BF)
        out = sc.F[0, :KEYS].astype(F32) + nn(mixed, sc.proj_w[...])
        sc.att[...] = out[:tokens].astype(BF)
        put_grad((0, 3 * ch), tn(mixed, sc.GA[0, :KEYS]))
        store(sc.att, outs.attended)

    def attention_back():
        pg = sc.PG
        pg[:, 0:ch] = (tn(sc.DS[:, 0:512], flat(sc.K))[:KEYS] * att_scale).astype(BF)
        pg[:, ch : 2 * ch] = (nn(sc.DS[0:KEYS], flat(sc.Q)) * att_scale).astype(BF)
        pg[:, 2 * ch :] = nn(sc.PR[0:KEYS], flat(sc.MG)).astype(BF)

    def attention_grads():
        pg = sc.PG
        grad = tn(sc.F[0, :KEYS], pg[...])
        for i in range(3):
            put_grad((0, i * ch), grad[:, i * ch : (i + 1) * ch])
        out = sc.GA[0, :KEYS].astype(F32) + nt(pg[...], sc.qkv_w[...])
        sc.fg[...] = out[:tokens]
        store(sc.fg, outs.features_grad)

    groups = []
    for k, size in enumerate(cfg.groups):
        kept, inbox, extra, send, recv = sc.sums[k]
        groups.append(
            Total(
                size,
                cfg.plans[k],
                cfg.far,
                sc.own[k],
                kept,
                inbox,
                extra,
                sc.result[k],
                send,
                recv,
            )
        )

    def adv(*which):
        for k in which:
            if groups[k].count == 0:
                groups[k].start()
            elif groups[k].busy:
                groups[k].advance()
                if not groups[k].busy:
                    store(sc.result[k], vars(outs)["sum%d" % k])

    summed_grad_own()
    hidden_two_grad(near_pair)
    hidden_one()
    conv_one(near_pair)
    hidden_one_halo(0)
    conv_one(edge_pair)
    stats_two()
    summed_grad_edge()
    film()
    tokens_in()
    project(0)
    send_next_row()
    st.tok.append(send_tokens(sc.GA, 3))
    st.tok.append(send_tokens(sc.F, 0))
    skip_back()
    skip_grad()
    hidden_two_grad(edge_pair)
    hidden_two()
    st.tok.append(send_tokens(sc.F, 1))
    conv2_grad(0)
    adv(1)
    conv2_grad(1)
    adv(2)
    st.tok.append(send_tokens(sc.GA, 2))
    hidden_one_halo(1)
    adv(1)
    conv_one_halo()
    adv(2)
    hidden_two_halo()
    conv2_grad(2)
    adv(3)
    conv_one_grad()
    down_cot_more()
    summed(near_pair)
    adv(3)
    summed(edge_pair)
    down_grad(0)
    adv(4)
    summed_swap()
    for copy in st.tok:
        copy.wait()
    project(1)
    prob_grads()
    adv(1)
    adv(4)
    scores()
    down(1)
    adv(2)
    adv(3)
    down_grad(1)
    adv(5)
    down_grad(2)
    adv(6)
    softmax(0, 2)
    adv(5)
    softmax(2, 4)
    adv(6)
    adv(1)
    adv(2)
    softmax(4, 6)
    adv(4)
    softmax(6, 7)
    adv(3)
    attend()
    attention_back()
    adv(6)
    halo_summed()
    down(0)
    store(sc.block, outs.block_out)
    attention_grads()
    adv(0)
    summed_grad_more()
    adv(1)
    adv(5)
    hidden_two_grad_halo()
    adv(2)
    adv(4)
    adv(0)
    conv_one_grad_halo()
    adv(3)
    conv1_grad()
    adv(7)
    adv(8)
    adv(6)
    hidden_one_grad(edge_pair)
    adv(5)
    adv(1)
    adv(7)
    adv(8)
    adv(2)
    adv(4)
    hidden_one_grad(near_pair)
    adv(1)
    pre_one_grad(near_pair)
    adv(0)
    pre_one_grad(edge_pair)
    stats_four()
    adv(3)
    adv(6)
    adv(7)
    adv(5)
    adv(4)
    packet_begin()
    image_grad()
    adv(8)
    adv(2)
    packet_step()
    adv(3)
    adv(0)
    adv(6)
    adv(5)
    adv(7)
    packet_step()
    adv(8)
    adv(4)
    adv(5)
    adv(0)
    adv(2)
    adv(3)
    packet_step()
    adv(2)
    adv(7)
    adv(3)
    adv(6)
    adv(8)
    adv(4)
    adv(0)
    adv(4)
    adv(0)
    adv(7)
    packet_step()
    adv(6)
    adv(7)
    adv(8)
    adv(6)
    adv(8)

    while any(group.busy for group in groups):
        adv(*range(len(groups)))
    while pk_state[0] < len(cfg.bits):
        packet_step()
    store(sc.packet, outs.packet)
    for copy in stores + swaps:
        copy.wait()
    for copy in loading:
        copy.wait()


class Config:
    pass


def finish_kernel(cfg, *refs):
    n_in = len(cfg.finish_in)
    ins = Names(zip(cfg.finish_in, refs[:n_in]))
    n_out = len(cfg.finish_out)
    outs = Names(zip(cfg.finish_out, refs[n_in : n_in + n_out]))
    sc = Names(refs[n_in + n_out])
    ch, chi = cfg.ch, cfg.chi
    copies = []

    def begin(src, dst):
        copy = pltpu.make_async_copy(src, dst, sc.sem.at[len(copies)])
        copy.start()
        copies.append(copy)
        return copy

    small = [
        begin(ins.packet, sc.packet),
        begin(ins.norm2_gain, sc.norm2_gain),
        begin(ins.norm2_bias, sc.norm2_bias),
    ]
    order = cfg.done_order
    got = [begin(vars(ins)["sum%d" % k], sc.low[k]) for k in order]
    through = [
        begin(ins.image_grad, sc.image_grad),
        begin(ins.features_grad, sc.features_grad),
        begin(ins.block_out, sc.block_out),
        begin(ins.attended, sc.attended),
    ]
    passed = (
        (sc.image_grad, outs.image_grad),
        (sc.features_grad, outs.features_grad),
        (sc.block_out, outs.block_out),
        (sc.attended, outs.attended),
    )
    waits = []

    def packet_rows(k):
        return sc.packet[pl.ds(k, cfg.dp, stride=16), :]

    def wide_rows(k):
        return jnp.concatenate([packet_rows(k), packet_rows(k + 1)], axis=1)

    def total(value):
        return jnp.sum(value, axis=0, keepdims=True)

    def widen(low, wide, size):
        step = 256

        @pl.loop(0, size // step)
        def _(i):
            here = part(i * step, step)
            wide[here, 0:128] = low[0, here, :].astype(F32)
            wide[here, 128:256] = low[1, here, :].astype(F32)

    def places(k):
        if 1 <= k <= 3:
            for a in range(3):
                yield a * ch, ch, outs.conv2.at[pl.ds((3 * a + k - 1) * ch, ch)]
        elif k <= 6:
            yield 0, 3 * ch, outs.down.at[pl.ds((k - 4) * 3 * ch, 3 * ch)]
        elif k == 7:
            yield 0, 6 * chi, outs.conv1.at[pl.ds(0, 6 * chi)]
        else:
            yield 0, 3 * chi, outs.conv1.at[pl.ds(6 * chi, 3 * chi)]
            yield 3 * chi, chi, outs.skip

    def film():
        for copy in small:
            copy.wait()
        first, second = wide_rows(4), wide_rows(6)
        scale_grad = sc.norm2_gain[...] * second + sc.norm2_bias[...] * first
        rows = jnp.concatenate([scale_grad, first], axis=1)
        embed = jnp.concatenate([wide_rows(0), wide_rows(2)], axis=1)
        sc.film_w[...] = lax.dot_general(
            embed,
            rows,
            (((0,), (0,)), ((), ())),
            precision=lax.Precision.HIGHEST,
            preferred_element_type=F32,
        )
        sc.film_b[...] = total(rows)
        sc.gain2[...] = total(wide_rows(10))
        sc.bias2[...] = total(wide_rows(8))
        sc.gain1[...] = total(packet_rows(13))
        sc.bias1[...] = total(packet_rows(12))
        for src, dst in (
            (sc.film_w, outs.film_w),
            (sc.film_b, outs.film_b),
            (sc.gain2, outs.gain2),
            (sc.bias2, outs.bias2),
            (sc.gain1, outs.gain1),
            (sc.bias1, outs.bias1),
        ):
            waits.append(begin(src, dst))

    for turn, (k, copy) in enumerate(zip(order, got)):
        if turn == 1:
            film()
        copy.wait()
        if k == 0:
            for i in range(4):
                wide = sc.wide[0] if i < 3 else sc.wide_p
                at = i * ch if i < 3 else 0
                for j in range(2):
                    value = sc.low[0][j, i * ch : (i + 1) * ch, :].astype(F32)
                    wide[:, at + j * 128 : at + (j + 1) * 128] = value
            waits.append(begin(sc.wide[0], outs.qkv))
            waits.append(begin(sc.wide_p, outs.proj))
        else:
            widen(sc.low[k], sc.wide[k], cfg.groups[k])
            for start, size, dst in places(k):
                waits.append(begin(sc.wide[k].at[pl.ds(start, size)], dst))
    for (src, dst), copy in zip(passed, through):
        copy.wait()
        waits.append(begin(src, dst))
    for copy in waits:
        copy.wait()


def body(
    image_in,
    noise_in,
    sigma_in,
    embedding,
    features,
    norm1_gain,
    norm1_bias,
    conv1_w,
    film_w,
    film_b,
    norm2_gain,
    norm2_bias,
    conv2_w,
    skip_w,
    down_w,
    qkv_w,
    proj_w,
    down_cot,
    attn_cot,
):
    cfg = Config()
    cfg.rows, cfg.cols, cfg.chi = image_in.shape[1:]
    cfg.ch = conv1_w.shape[3]
    cfg.tokens = features.shape[1]
    cfg.dp = lax.axis_size("dp")
    cfg.bits = [2**k for k in range(cfg.dp.bit_length() - 1)]
    cfg.far = cfg.bits[4:]
    rows, cols, chi, ch, dp = cfg.rows, cfg.cols, cfg.chi, cfg.ch, cfg.dp
    half = cols // 2
    cfg.groups = [4 * ch] + [3 * ch] * 6 + [6 * chi, 4 * chi]
    cfg.plans = [
        [[1], ["rows", 2], [4, 8]],
        [[1], ["rows", 2], [4, 8]],
        [[1], ["rows"], [2], [4, 8]],
        [[1], [2], [4], [8, "rows"]],
        [[1], [4], ["rows", 2], [8]],
        [[1], ["rows", 2], [4, 8]],
        [[1], [4], ["rows", 2], [8]],
        [[1], ["rows", 2], [4, 8]],
        [[1], ["rows", 2], [4, 8]],
    ]
    cfg.done_order = (1, 5, 2, 3, 4, 0, 7, 6, 8)
    args = dict(
        sigma_in=sigma_in,
        image_in=image_in[0],
        noise_in=noise_in[0],
        norm1_gain=norm1_gain.reshape(1, chi),
        norm1_bias=norm1_bias.reshape(1, chi),
        down_cot=down_cot[0],
        down_w=down_w.reshape(3, 3 * ch, ch),
        conv1_w=conv1_w.reshape(3, 3 * chi, ch),
        conv2_w=conv2_w.reshape(3, 3 * ch, ch),
        skip_w=skip_w,
        features=features[0],
        attn_cot=attn_cot[0],
        embedding=embedding,
        film_w=film_w,
        film_b=film_b.reshape(1, 2 * ch),
        norm2_gain=norm2_gain.reshape(1, ch),
        norm2_bias=norm2_bias.reshape(1, ch),
        qkv_w=qkv_w,
        proj_w=proj_w,
    )
    cfg.inputs = tuple(args)
    shape = jax.ShapeDtypeStruct
    out_shapes = dict(
        block_out=shape((2, half, ch), BF),
        attended=shape((cfg.tokens, ch), BF),
        image_grad=shape((rows, cols, chi), F32),
        features_grad=shape((cfg.tokens, ch), F32),
        packet=shape((dp, 16, 128), F32),
    )
    for k, size in enumerate(cfg.groups):
        out_shapes["sum%d" % k] = shape((2, size, 128), BF)
    cfg.outputs = tuple(out_shapes)
    vm = pltpu.VMEM
    scratch = {
        name: vm(value.shape, value.dtype)
        for name, value in args.items()
        if value is not sigma_in and value is not args["down_cot"]
    }
    scratch.update(
        dc=vm((5, half, ch), BF),
        xh=vm((2, cols, chi), BF),
        xs=vm((rows, cols, chi), F32),
        stage_i=vm((chi // 128, cols + 16, 128), F32),
        stage_o=vm((chi // 128, cols + 16, 128), F32),
        stage_c=vm((ch // 128, cols + 16, 128), F32),
        stage_h=vm((ch // 128, half + 16, 128), F32),
        h1c=vm((rows + 4, cols, 3 * chi), BF),
        h2c=vm((rows + 2, cols, 3 * ch), BF),
        sg3=vm((rows + 4, cols, 3 * ch), BF),
        cg=vm((rows + 2, cols, ch), BF),
        s3=vm((rows + 1, half, 3 * ch), BF),
        c1=vm((rows + 1, cols, ch), F32),
        g2=vm((rows + 1, cols, ch), F32),
        h1g=vm((rows, cols, chi), F32),
        skb=vm((rows, cols, chi), F32),
        block=vm((2, half, ch), BF),
        st_out=vm((4, 8, ch), F32),
        st_in=vm((4, 8, ch), F32),
        packet=vm((dp, 16, 128), F32),
        F=vm((2, TOKENS, ch), BF),
        GA=vm((2, TOKENS, ch), BF),
        Q=vm((2, TOKENS, ch), BF),
        K=vm((2, KEYS, ch), BF),
        V=vm((2, KEYS, ch), BF),
        MG=vm((2, TOKENS, ch), BF),
        S=vm((2 * KEYS, 2 * TOKENS), F32),
        D=vm((2 * KEYS, 2 * TOKENS), F32),
        PR=vm((2 * KEYS, 2 * TOKENS), BF),
        DS=vm((2 * KEYS, 2 * TOKENS), BF),
        PG=vm((KEYS, 3 * ch), BF),
        att=vm((cfg.tokens, ch), BF),
        fg=vm((cfg.tokens, ch), F32),
        own=[vm((2, size, 128), BF) for size in cfg.groups],
        result=[vm((2, size, 128), BF) for size in cfg.groups],
        sums=[total_scratch(*plan, cfg.far) for plan in zip(cfg.groups, cfg.plans)],
        load_sem=pltpu.SemaphoreType.DMA((len(args),)),
        store_sem=pltpu.SemaphoreType.DMA((len(out_shapes),)),
        x_send=pltpu.SemaphoreType.DMA((13,)),
        x_recv=pltpu.SemaphoreType.DMA((13,)),
        pk_send=pltpu.SemaphoreType.DMA((len(cfg.bits),)),
        pk_recv=pltpu.SemaphoreType.DMA((len(cfg.bits),)),
    )
    made = pl.pallas_call(
        functools.partial(level_kernel, cfg),
        out_shape=list(out_shapes.values()),
        in_specs=[SMEM] + [ANY] * (len(args) - 1),
        out_specs=[ANY] * len(out_shapes),
        scratch_shapes=[scratch],
        compiler_params=pltpu.CompilerParams(
            collective_id=0, has_side_effects=True, vmem_limit_bytes=62 * 2**20
        ),
        name="level",
    )(*args.values())
    made = dict(zip(cfg.outputs, made))

    small = dict(
        packet=made["packet"].reshape(dp * 16, 128),
        norm2_gain=args["norm2_gain"],
        norm2_bias=args["norm2_bias"],
    )
    big = {name: value for name, value in made.items() if name not in small}
    cfg.finish_in = tuple(small) + tuple(big)
    finals = dict(
        block_out=out_shapes["block_out"],
        attended=out_shapes["attended"],
        image_grad=out_shapes["image_grad"],
        features_grad=out_shapes["features_grad"],
        conv1=shape((9 * chi, ch), F32),
        conv2=shape((9 * ch, ch), F32),
        skip=shape((chi, ch), F32),
        down=shape((9 * ch, ch), F32),
        qkv=shape((ch, 3 * ch), F32),
        proj=shape((ch, ch), F32),
    )
    finals.update(
        gain1=shape((1, chi), F32),
        bias1=shape((1, chi), F32),
        film_w=shape((2 * ch, 2 * ch), F32),
        film_b=shape((1, 2 * ch), F32),
        gain2=shape((1, ch), F32),
        bias2=shape((1, ch), F32),
    )
    cfg.finish_out = tuple(finals)
    finish_scratch = dict(
        low=[vm((2, size, 128), BF) for size in cfg.groups],
        wide=[vm((ch, 3 * ch), F32)] + [vm((size, ch), F32) for size in cfg.groups[1:]],
        wide_p=vm((ch, ch), F32),
        image_grad=vm((rows, cols, chi), F32),
        features_grad=vm((cfg.tokens, ch), F32),
        block_out=vm((2, half, ch), BF),
        attended=vm((cfg.tokens, ch), BF),
        packet=vm((dp * 16, 128), F32),
        norm2_gain=vm((1, ch), F32),
        norm2_bias=vm((1, ch), F32),
        gain1=vm((1, chi), F32),
        bias1=vm((1, chi), F32),
        film_w=vm((2 * ch, 2 * ch), F32),
        film_b=vm((1, 2 * ch), F32),
        gain2=vm((1, ch), F32),
        bias2=vm((1, ch), F32),
        sem=pltpu.SemaphoreType.DMA((48,)),
    )
    done = pl.pallas_call(
        functools.partial(finish_kernel, cfg),
        out_shape=list(finals.values()),
        in_specs=[ANY] * len(cfg.finish_in),
        out_specs=[ANY] * len(finals),
        scratch_shapes=[finish_scratch],
        compiler_params=pltpu.CompilerParams(vmem_limit_bytes=56 * 2**20),
        name="finish",
    )(*small.values(), *big.values())
    done = Names(zip(cfg.finish_out, done))
    return (
        done.block_out[None],
        done.attended[None],
        done.image_grad[None],
        done.features_grad[None],
        done.gain1.reshape(chi),
        done.bias1.reshape(chi),
        done.conv1.reshape(conv1_w.shape),
        done.film_w,
        done.film_b.reshape(2 * ch),
        done.gain2.reshape(ch),
        done.bias2.reshape(ch),
        done.conv2.reshape(conv2_w.shape),
        done.skip,
        done.down.reshape(down_w.shape),
        done.qkv,
        done.proj,
    )


def solution(mesh):
    placed = (
        P("dp", "rows", None, None),
        P("dp", "rows", None, None),
        P("dp"),
        P("dp", None),
        P("dp", "rows", None),
        P(),
        P(),
        P(),
        P(),
        P(),
        P(),
        P(),
        P(),
        P(),
        P(),
        P(),
        P(),
        P("dp", "rows", None, None),
        P("dp", "rows", None),
    )
    return jax.shard_map(
        body,
        mesh=mesh,
        in_specs=placed,
        out_specs=(
            P("dp", "rows", None, None),
            P("dp", "rows", None),
            P("dp", "rows", None, None),
            P("dp", "rows", None),
            P(),
            P(),
            P(),
            P(),
            P(),
            P(),
            P(),
            P(),
            P(),
            P(),
            P(),
            P(),
        ),
        check_vma=False,
    )
```

```python
import functools

import jax
import jax.numpy as jnp
from jax import lax
from jax.experimental import pallas as pl
from jax.experimental.pallas import tpu as pltpu
from jax.sharding import PartitionSpec as P

G = 32
EPSILON = 1e-05
SIGMA_DATA = 0.5
MESH = pl.DeviceIdType.MESH
ANY = pl.BlockSpec(memory_space=pl.ANY)
SMEM = pl.BlockSpec(memory_space=pltpu.SMEM)
BF = jnp.bfloat16
F32 = jnp.float32
TOKENS = 448
KEYS = 400


def flip(index, bit):
    return index + bit * (1 - 2 * ((index // bit) % 2))


class Side:
    def __init__(self, names):
        d = lax.axis_index("dp")
        r = lax.axis_index("rows")
        self.mine = []
        for name in names:
            self.mine.append(r if name == "rows" else (d // name) % 2)
        self.parts = 2 ** len(names)
        self.names = names
        self.position = (d, r)

    def partners(self):
        found = []
        for flips in range(1, self.parts):
            d, r = self.position
            index = 0
            for k, name in enumerate(self.names):
                other = (flips >> k) % 2
                side = self.mine[k]
                if other:
                    side = 1 - side
                    if name == "rows":
                        r = 1 - r
                    else:
                        d = flip(d, name)
                index = index * 2 + side
            found.append(((d, r), index))
        return found

    @property
    def index(self):
        index = 0
        for side in self.mine:
            index = index * 2 + side
        return index


def part(start, size):
    return pl.ds(pl.multiple_of(start, size), size)


class Total:
    def __init__(self, rows, stages, whole, own, kept, inbox, extra, result, send, recv):
        self.rows = rows
        self.stages = [Side(names) for names in stages]
        self.whole = [Side([name]) for name in whole]
        self.own = own
        self.kept = kept
        self.inbox = inbox
        self.extra = extra
        self.result = result
        self.send = send
        self.recv = recv
        self.sizes = sizes_of(rows, stages)
        self.steps = len(stages)
        self.copies = None
        self.count = 0

    def begin(self, src, dst, where):
        k = self.count
        self.count += 1
        copy = pltpu.make_async_remote_copy(
            src_ref=src,
            dst_ref=dst,
            send_sem=self.send.at[k],
            recv_sem=self.recv.at[k],
            device_id=where,
            device_id_type=MESH,
        )
        copy.start()
        self.copies.append(copy)

    def scatter(self, step):
        side = self.stages[step]
        size = self.sizes[step]
        for slot, (where, index) in enumerate(side.partners()):
            if step == 0:
                src = self.own.at[index]
            else:
                src = self.kept[step - 1].at[part(index * size, size)]
            self.begin(src, self.inbox[step].at[slot], where)

    def start(self):
        self.copies = []
        self.scatter(0)
        self.stage = 0

    def region(self, step):
        lead = self.stages[0].index
        if step == 0:
            return self.result.at[lead]
        offset = 0
        for t in range(1, step + 1):
            offset = offset + self.stages[t].index * self.sizes[t]
        return self.result.at[lead, part(offset, self.sizes[step])]

    def gather(self, step):
        mine = self.region(step)
        for where, _ in self.stages[step].partners():
            self.begin(mine, mine, where)

    def swap_whole(self, k):
        (where, _), = self.whole[k].partners()
        self.begin(self.kept[self.steps - 1 + k], self.extra.at[k], where)

    def advance(self):
        stage = self.stage
        last = self.steps - 1
        for copy in self.copies:
            copy.wait()
        self.copies = []
        if stage < self.steps:
            side = self.stages[stage]
            size = self.sizes[stage]
            if stage == 0:
                have = self.own.at[side.index]
            else:
                have = self.kept[stage - 1].at[part(side.index * size, size)]
            if stage == last and not self.whole:
                dest = self.region(last)
            else:
                dest = self.kept[stage]
            add_rows(dest, have, self.inbox[stage], side.parts - 1, size)
            if stage < last:
                self.scatter(stage + 1)
            elif self.whole:
                self.swap_whole(0)
            else:
                self.gather(last)
        elif stage < self.steps + len(self.whole):
            k = stage - self.steps
            final = k == len(self.whole) - 1
            dest = self.region(last) if final else self.kept[last + k + 1]
            add_rows(dest, self.kept[last + k], self.extra.at[pl.ds(k, 1)], 1, self.sizes[last])
            if final:
                self.gather(last)
            else:
                self.swap_whole(k + 1)
        else:
            k = stage - self.steps - len(self.whole)
            if k < last:
                self.gather(last - 1 - k)
            else:
                self.copies = None
        self.stage = stage + 1

    @property
    def busy(self):
        return self.copies is not None


def add_rows(dest, have, got, count, size):
    block = size
    while block > 400:
        block //= 2 if (block // 2) % 16 == 0 else 3

    def add(here):
        value = have[here].astype(jnp.float32)
        for slot in range(count):
            value = value + got[slot, here].astype(jnp.float32)
        dest[here] = value.astype(jnp.bfloat16)

    if block == size:
        add(pl.ds(0, size))
    else:

        @pl.loop(0, size // block)
        def _(i):
            add(part(i * block, block))


def sizes_of(rows, stages):
    sizes = [rows]
    for names in stages[1:]:
        sizes.append(sizes[-1] // 2 ** len(names))
    return sizes


def copies_of(stages, whole):
    return 2 * sum(2 ** len(names) - 1 for names in stages) + len(whole)


def total_scratch(rows, stages, whole):
    sizes = sizes_of(rows, stages)
    kept = [pltpu.VMEM((size, 128), jnp.bfloat16) for size in sizes + [sizes[-1]] * len(whole)]
    inbox = [
        pltpu.VMEM((2 ** len(names) - 1, size, 128), jnp.bfloat16)
        for names, size in zip(stages, sizes)
    ]
    extra = pltpu.VMEM((max(len(whole), 1), sizes[-1], 128), jnp.bfloat16)
    count = copies_of(stages, whole)
    return [
        kept,
        inbox,
        extra,
        pltpu.SemaphoreType.DMA((count,)),
        pltpu.SemaphoreType.DMA((count,)),
    ]


class Names:
    def __init__(self, pairs=()):
        vars(self).update(pairs)


class Once:
    def __init__(self, copy):
        self.copy = copy
        self.waited = False
        copy.start()

    def wait(self):
        if not self.waited:
            self.waited = True
            self.copy.wait()


def nn(left, right):
    return lax.dot_general(left, right, (((1,), (0,)), ((), ())), preferred_element_type=F32)


def nt(left, right):
    return lax.dot_general(left, right, (((1,), (1,)), ((), ())), preferred_element_type=F32)


def tn(left, right):
    return lax.dot_general(left, right, (((0,), (0,)), ((), ())), preferred_element_type=F32)


def fold(value):
    rows, lanes = value.shape
    return jnp.sum(value.reshape(rows // 8, 8, lanes), axis=0)


def one_row(value):
    return jnp.sum(value, axis=0, keepdims=True)


def group_sum(value, width):
    lanes = value.shape[1]
    lane = lax.broadcasted_iota(jnp.int32, value.shape, 1)
    step = 1
    while step < width:
        up = pltpu.roll(value, lanes - step, 1)
        down = pltpu.roll(value, step, 1)
        value = value + jnp.where((lane // step) % 2 == 0, up, down)
        step *= 2
    return value


def sigmoid(value):
    return 0.5 + 0.5 * jnp.tanh(0.5 * value)


def spread(row, staged, lanes):
    cells = row.shape[0]
    for b in range(3):
        for k in range(lanes // 128):
            at = b * lanes + k * 128
            row[:, at : at + 128] = staged[k, 7 + b : 7 + b + cells, :].astype(BF)


def put(staged, start, value):
    cells, lanes = value.shape
    for k in range(lanes // 128):
        staged[k, pl.ds(start, cells), :] = value[:, k * 128 : (k + 1) * 128]


def level_kernel(cfg, *refs):
    n_in = len(cfg.inputs)
    ins = Names(zip(cfg.inputs, refs[:n_in]))
    outs = Names(zip(cfg.outputs, refs[n_in : n_in + len(cfg.outputs)]))
    sc = Names(refs[n_in + len(cfg.outputs)])
    st = Names()
    rows, cols, chi, ch = cfg.rows, cfg.cols, cfg.chi, cfg.ch
    half = cols // 2
    r = lax.axis_index("rows")
    d = lax.axis_index("dp")
    across = (d, 1 - r)

    loads = Names()
    loading = []

    def load(name, dst):
        copy = Once(pltpu.make_async_copy(vars(ins)[name], dst, sc.load_sem.at[len(loading)]))
        loading.append(copy)
        setattr(loads, name, copy)

    stores = []

    def store(src, dst):
        copy = pltpu.make_async_copy(src, dst, sc.store_sem.at[len(stores)])
        copy.start()
        stores.append(copy)

    def swap_copy(k, src, dst):
        return pltpu.make_async_remote_copy(
            src_ref=src,
            dst_ref=dst,
            send_sem=sc.x_send.at[k],
            recv_sem=sc.x_recv.at[k],
            device_id=across,
            device_id_type=MESH,
        )

    swaps = []

    def swap(k, src, dst):
        copy = Once(swap_copy(k, src, dst))
        swaps.append(copy)
        return copy

    barrier = pltpu.get_barrier_semaphore()
    greeted = {}
    for stages in cfg.plans:
        for names in stages + [[name] for name in cfg.far]:
            side = Side(names)
            for flips, (where, _) in enumerate(side.partners(), 1):
                met = frozenset(n for k, n in enumerate(names) if (flips >> k) % 2)
                greeted[met] = where
    for where in greeted.values():
        pl.semaphore_signal(barrier, inc=1, device_id=where, device_id_type=MESH)

    sc.down_cot = sc.dc.at[1:3]
    names = cfg.inputs[1:]
    for name in names[:4]:
        load(name, vars(sc)[name])

    sigma = jnp.full((1, chi), ins.sigma_in[0], F32)
    scale_in = lax.rsqrt(SIGMA_DATA * SIGMA_DATA + sigma * sigma)
    loads.image_in.wait()
    loads.noise_in.wait()
    for name in names[4:]:
        load(name, vars(sc)[name])
    piece = cols // 4

    def stats_one(i, carry):
        row, col = i // 2, i % 2
        here = part(col * half, half)
        value = scale_in * (
            sc.image_in[row, here].astype(F32) + sigma * sc.noise_in[row, here].astype(F32)
        )
        sc.xs[row, here] = value
        sc.image_in[row, here] = value.astype(BF)
        return carry[0] + fold(value), carry[1] + fold(value * value)

    zero8 = jnp.zeros((8, chi), F32)
    sum_a, sum_b = lax.fori_loop(0, rows * 2, stats_one, (zero8, zero8))
    low_in = sc.image_in

    def send_stats(k, top, bottom):
        lanes = top.shape[1]
        sc.st_out[k, 0:1, 0:lanes] = top
        sc.st_out[k, 1:2, 0:lanes] = bottom
        copy = swap(1 + k, sc.st_out.at[k], sc.st_in.at[k])
        return copy

    def both_stats(k, copy, lanes):
        copy.wait()
        total = sc.st_out[k, :, 0:lanes] + sc.st_in[k, :, 0:lanes]
        return total[0:1], total[1:2]

    pl.semaphore_wait(barrier, len(greeted))
    swap_one = send_stats(0, one_row(sum_a), one_row(sum_b))

    edge = 4 - 3 * r
    rows_one = [swap(6, low_in.at[edge - 1], sc.xh.at[0])]

    def send_next_row():
        rows_one.append(swap(8, low_in.at[2 - r], sc.xh.at[1]))

    dc_swap = swap(0, ins.down_cot.at[1 - r], sc.dc.at[3 * r])
    dc_more = swap_copy(5, ins.down_cot.at[1], sc.dc.at[4])

    def down_cot_more():
        @pl.when(r == 1)
        def _():
            dc_more.start()

    for ref in (sc.stage_i, sc.stage_o, sc.stage_c, sc.stage_h):
        zeros = jnp.zeros((ref.shape[0], 8, 128), F32)
        ref[:, 0:8, :] = zeros
        ref[:, ref.shape[1] - 8 :, :] = zeros
    outer = 5 * r
    inner = 5 * (1 - r)
    sc.h1c[outer + 1] = jnp.zeros((cols, 3 * chi), BF)
    sc.h2c[outer] = jnp.zeros((cols, 3 * ch), BF)
    sc.cg[outer] = jnp.zeros((cols, ch), BF)
    sc.sg3[outer + 1] = jnp.zeros((cols, 3 * ch), BF)
    sc.dc[3 * r] = jnp.zeros((half, ch), BF)
    for ref in (sc.F, sc.GA):
        ref[1, 400:, :] = jnp.zeros((TOKENS - 400, ch), BF)

    @pl.when(r == 0)
    def _():
        sc.s3[0] = jnp.zeros((half, 3 * ch), BF)

    dw = sc.down_w
    loads.down_cot.wait()
    loads.down_w.wait()

    def shifted_cot(m):
        staged = sc.stage_h
        put(staged, 8, sc.dc[m].astype(F32))
        right = [staged[k, 9 : 9 + half, :].astype(BF) for k in range(ch // 128)]
        return sc.dc[m], jnp.concatenate(right, axis=1)

    def dw_tap(a, b):
        return dw[a, b * ch : (b + 1) * ch, :]

    def even_row(m):
        here, right = shifted_cot(m)
        return nt(here, dw_tap(1, 1)), nt(here, dw_tap(1, 2)) + nt(right, dw_tap(1, 0))

    def odd_row(m):
        here, right = shifted_cot(m)
        even = nt(here, dw_tap(2, 1))
        odd = nt(here, dw_tap(2, 2)) + nt(right, dw_tap(2, 0))
        here, right = shifted_cot(m + 1)
        even += nt(here, dw_tap(0, 1))
        odd += nt(here, dw_tap(0, 2)) + nt(right, dw_tap(0, 0))
        return even, odd

    def put_row(l, pair):
        staged = sc.stage_c
        for k in range(ch // 128):
            for odd in range(2):
                value = pair[odd][:, k * 128 : (k + 1) * 128]
                staged[k, pl.ds(8 + odd, half, stride=2), :] = value
        spread(sc.sg3.at[l + 1], staged, ch)

    def summed_grad_own():
        @pl.loop(0, 2)
        def _(k):
            put_row(1 + 2 * k, even_row(1 + k))

        put_row(2, odd_row(1))

        @pl.when(r == 1)
        def _():
            put_row(4, odd_row(2))

    def summed_grad_edge():
        dc_swap.wait()

        @pl.when(r == 0)
        def _():
            put_row(4, odd_row(2))
            put_row(5, even_row(3))

        @pl.when(r == 1)
        def _():
            put_row(0, odd_row(0))

    def summed_grad_more():
        @pl.when(r == 0)
        def _():
            dc_more.wait_recv()
            put_row(6, odd_row(3))

        @pl.when(r == 1)
        def _():
            dc_more.wait_send()
            put_row(-1, even_row(0))

    gain1 = lambda: sc.norm1_gain[...]
    bias1 = lambda: sc.norm1_bias[...]
    count1 = float(2 * rows * cols * (chi // G))
    count2 = float(2 * rows * cols * (ch // G))

    def moments(first, second, width, count):
        mean = group_sum(first, width) / count
        return mean, lax.rsqrt(group_sum(second, width) / count - mean * mean + EPSILON)

    st.sums2 = (0.0, 0.0)
    st.tok = []
    st.sums4 = (zero8, zero8)

    def row_one(place, values):
        mean, inverse = st.mean1, st.inv1

        @pl.loop(0, 4)
        def _(c):
            here = part(c * piece, piece)
            pre = (values[here].astype(F32) - mean) * inverse * gain1() + bias1()
            put(sc.stage_i, pl.multiple_of(8 + c * piece, 8), pre * sigmoid(pre))

        spread(sc.h1c.at[place], sc.stage_i, chi)

    def hidden_one():
        loads.norm1_gain.wait()
        loads.norm1_bias.wait()
        first, second = both_stats(0, swap_one, chi)
        st.mean1, st.inv1 = moments(first, second, chi // G, count1)

        @pl.loop(0, rows)
        def _(i):
            row_one(2 + i, sc.xs.at[i])

    def hidden_one_halo(k):
        rows_one[k].wait()
        row_one(inner + 1 if k == 0 else 7 * (1 - r), sc.xh.at[k])

    near_pair = 1 + 2 * r
    edge_pair = 3 - 2 * r

    def conv_rows(source, weight, base, count, lanes):
        left = [
            source[pl.ds(base - 1 + a, count)].reshape(count * cols, 3 * lanes) for a in range(3)
        ]
        return nn(jnp.concatenate(left, axis=1), weight[...].reshape(9 * lanes, ch))

    def conv_one(base):
        loads.conv1_w.wait()
        acc = conv_rows(sc.h1c, sc.conv1_w, base + 1, 2, chi)
        sc.c1[pl.ds(base - 1, 2)] = acc.reshape(2, cols, ch)
        sums = fold(acc), fold(acc * acc)
        st.sums2 = tuple(x + y for x, y in zip(st.sums2, sums))

    def conv_one_halo():
        sc.c1[rows] = conv_rows(sc.h1c, sc.conv1_w, inner + 1, 1, chi)

    def stats_two():
        first, second = st.sums2
        st.swap2 = send_stats(1, one_row(first), one_row(second))

    def back_pair(source, weight, base, lanes):
        return back_rows(source, weight, base, 2, lanes)

    def back_rows(source, weight, base, count, lanes):
        acc = None
        for a in range(3):
            for b in range(3):
                left = source[pl.ds(base - 1 + a, count), :, b * ch : (b + 1) * ch]
                term = nt(
                    left.reshape(count * cols, ch), weight[2 - a, (2 - b) * lanes : (3 - b) * lanes, :]
                )
                acc = term if acc is None else acc + term
        return acc

    def hidden_two_grad(base):
        loads.conv2_w.wait()
        acc = back_pair(sc.sg3, sc.conv2_w, base + 1, ch)
        sc.g2[pl.ds(base - 1, 2)] = acc.reshape(2, cols, ch)

    def hidden_two_grad_halo():
        sc.g2[rows] = back_rows(sc.sg3, sc.conv2_w, inner + 1, 1, ch)

    def grad_rows():
        return sc.sg3[2:6, :, ch : 2 * ch].reshape(rows * cols, ch)

    down_at = [(4, 0), (5, 0), (6, 0)]
    conv1_at = [(7, 0), (7, 3 * chi), (8, 0)]
    skip_at = (8, 3 * chi)

    def put_grad(place, value):
        group, start = place
        low = value.astype(BF)
        size = low.shape[0]
        sc.own[group][0, start : start + size, :] = low[:, :128]
        sc.own[group][1, start : start + size, :] = low[:, 128:]

    def skip_back():
        loads.skip_w.wait()
        sc.skb[...] = nt(grad_rows(), sc.skip_w[...]).reshape(rows, cols, chi)

    def skip_grad():
        put_grad(skip_at, tn(low_in[...].reshape(rows * cols, chi), grad_rows()))

    def film():
        for copy in (
            loads.embedding,
            loads.film_w,
            loads.film_b,
            loads.norm2_gain,
            loads.norm2_bias,
        ):
            copy.wait()
        row = nn(sc.embedding[...], sc.film_w[...]) + sc.film_b[...]
        scale = 1.0 + row[:, :ch]
        shift = row[:, ch:]
        gain, bias = sc.norm2_gain[...], sc.norm2_bias[...]
        st.scale = scale
        st.pre_gain = gain * scale
        st.pre_bias = bias * scale + shift

    def hidden_two():
        first, second = both_stats(1, st.swap2, ch)
        mean, inverse = moments(first, second, ch // G, count2)
        st.mean2, st.inv2 = mean, inverse
        step = cols // 8

        def row_of(l, carry):
            staged = sc.stage_c

            def cells(c, carry):
                here = part(c * step, step)
                hat = (sc.c1[l - 1, here] - mean) * inverse
                sc.c1[l - 1, here] = hat
                pre = hat * st.pre_gain + st.pre_bias
                gate = sigmoid(pre)
                value = pre * gate
                put(staged, pl.multiple_of(8 + c * step, 8), value)
                grad = sc.g2[l - 1, here] * (gate + value * (1.0 - gate))
                sc.g2[l - 1, here] = grad
                return carry[0] + fold(grad), carry[1] + fold(grad * hat)

            carry = lax.fori_loop(0, 8, cells, carry)
            spread(sc.h2c.at[l], staged, ch)
            return carry

        zero = jnp.zeros((8, ch), F32)
        carry = lax.fori_loop(0, rows, lambda i, carry: row_of(1 + i, carry), (zero, zero))
        st.swap3 = send_stats(2, one_row(carry[0]), one_row(carry[1]))

    def hidden_two_halo():
        step = cols // 8

        @pl.loop(0, 8)
        def _(c):
            here = part(c * step, step)
            hat = (sc.c1[rows, here] - st.mean2) * st.inv2
            sc.c1[rows, here] = hat
            pre = hat * st.pre_gain + st.pre_bias
            put(sc.stage_c, pl.multiple_of(8 + c * step, 8), pre * sigmoid(pre))

        spread(sc.h2c.at[inner], sc.stage_c, ch)

    def conv2_grad(b):
        left = sc.h2c[1:5, :, b * ch : (b + 1) * ch].reshape(rows * cols, ch)
        right = [
            sc.sg3[3 - a : 7 - a, :, ch : 2 * ch].reshape(rows * cols, ch) for a in range(3)
        ]
        grad = tn(left, jnp.concatenate(right, axis=1))
        for a in range(3):
            put_grad((1 + b, a * ch), grad[:, a * ch : (a + 1) * ch])

    def odd_shift(row):
        staged = sc.stage_h
        put(staged, 8, row[:, 2 * ch :].astype(F32))
        for k in range(ch // 128):
            row[:, k * 128 : (k + 1) * 128] = staged[k, 7 : 7 + half, :].astype(BF)

    def summed(base):
        loads.skip_w.wait()
        loads.conv2_w.wait()
        acc = conv_rows(sc.h2c, sc.conv2_w, base, 2, ch)
        low = low_in[pl.ds(base - 1, 2)].reshape(2 * cols, chi)
        acc = (acc + nn(low, sc.skip_w[...])).reshape(2, cols, ch)
        for k in range(2):
            staged = sc.stage_c
            put(staged, 8, acc[k])
            row = sc.s3.at[base + k]
            for i in range(ch // 128):
                for odd in range(2):
                    at = (1 + odd) * ch + i * 128
                    value = staged[i, pl.ds(8 + odd, half, stride=2), :]
                    row[:, at : at + 128] = value.astype(BF)
            odd_shift(row)

    def summed_swap():
        copy = swap_copy(7, sc.s3.at[4, :, ch:], sc.s3.at[0, :, ch:])
        st.s3 = copy

        @pl.when(r == 0)
        def _():
            copy.start()

    def halo_summed():
        copy = st.s3

        @pl.when(r == 0)
        def _():
            copy.wait_send()

        @pl.when(r == 1)
        def _():
            copy.wait_recv()
            odd_shift(sc.s3.at[0])

    def down(k):
        acc = None
        for a in range(3):
            term = nn(sc.s3[2 * k + a], dw[a])
            acc = term if acc is None else acc + term
        sc.block[k] = acc.astype(BF)

    def down_grad(a):
        first, cot = ((2, 2), (1, 1), (2, 1))[a]
        value = tn(sc.s3[first], sc.dc[cot]) + tn(sc.s3[first + 2], sc.dc[cot + 1])
        put_grad(down_at[a], value)

    def back_two(grad, hat):
        return (grad * st.pre_gain - st.m1 - hat * st.m2) * st.inv2

    def conv_one_grad():
        first, second = both_stats(2, st.swap3, ch)
        st.A, st.B = first, second
        st.m1 = group_sum(first * st.pre_gain, ch // G) / count2
        st.m2 = group_sum(second * st.pre_gain, ch // G) / count2
        step = cols // 4

        @pl.loop(0, rows * 4)
        def _(i):
            row, here = i // 4, part(i % 4 * step, step)
            sc.cg[1 + row, here] = back_two(sc.g2[row, here], sc.c1[row, here]).astype(BF)

    def conv_one_grad_halo():
        step = cols // 4

        @pl.loop(0, 4)
        def _(c):
            here = part(c * step, step)
            hat = sc.c1[rows, here]
            pre = hat * st.pre_gain + st.pre_bias
            gate = sigmoid(pre)
            grad = sc.g2[rows, here] * (gate + pre * gate * (1.0 - gate))
            sc.cg[inner, here] = back_two(grad, hat).astype(BF)

    def conv1_grad():
        left = sc.h1c[2:6].reshape(rows * cols, 3 * chi)
        right = [sc.cg[2 - a : 6 - a].reshape(rows * cols, ch) for a in range(3)]
        grad = tn(left, jnp.concatenate(right, axis=1))
        for a in range(3):
            put_grad(conv1_at[a], grad[:, a * ch : (a + 1) * ch])

    def hidden_one_grad(base):
        acc = None
        for a in range(3):
            left = sc.cg[pl.ds(base - 1 + a, 2)].reshape(2 * cols, ch)
            term = nt(left, sc.conv1_w[2 - a])
            acc = term if acc is None else acc + term
        acc = acc.reshape(2, cols, 3 * chi)
        for i in range(2):
            put(sc.stage_i, 8, acc[i, :, 0:chi])
            put(sc.stage_o, 8, acc[i, :, 2 * chi :])
            right = sc.stage_i[0, 9 : 9 + cols, :]
            left = sc.stage_o[0, 7 : 7 + cols, :]
            sc.h1g[base - 1 + i] = acc[i, :, chi : 2 * chi] + right + left

    def pre_one_grad(base):
        mean, inverse = st.mean1, st.inv1

        def cells(i, carry):
            row, col = base - 1 + i // 4, i % 4
            here = part(col * piece, piece)
            hat = (sc.xs[row, here] - mean) * inverse
            sc.xs[row, here] = hat
            pre = hat * gain1() + bias1()
            gate = sigmoid(pre)
            grad = sc.h1g[row, here] * (gate + pre * gate * (1.0 - gate))
            sc.h1g[row, here] = grad
            return carry[0] + fold(grad), carry[1] + fold(grad * hat)

        st.sums4 = lax.fori_loop(0, 8, cells, st.sums4)

    def stats_four():
        first, second = st.sums4
        st.swap4 = send_stats(3, one_row(first), one_row(second))

    def packet_begin():
        first, second = both_stats(3, st.swap4, chi)
        st.C, st.D = first, second
        pk = sc.packet.at[d]
        values = (
            sc.embedding[...].astype(F32),
            st.A,
            st.B,
            st.scale * st.A,
            st.scale * st.B,
            first,
            second,
            jnp.zeros((1, 256), F32),
        )
        at = 0
        for value in values:
            for k in range(value.shape[1] // 128):
                pk[at : at + 1, :] = value[:, k * 128 : (k + 1) * 128]
                at += 1
        packet_start()

    def image_grad():
        first, second = st.C, st.D
        m1 = group_sum(first * gain1(), chi // G) / count1
        m2 = group_sum(second * gain1(), chi // G) / count1

        @pl.loop(0, rows * 4)
        def _(i):
            row, col = i // 4, i % 4
            here = part(col * piece, piece)
            value = (
                sc.h1g[row, here] * gain1() - m1 - sc.xs[row, here] * m2
            ) * st.inv1 + sc.skb[row, here]
            sc.h1g[row, here] = scale_in * value

        store(sc.h1g, outs.image_grad)

    bits = [Side([bit]).partners()[0][0] for bit in cfg.bits]

    def packet_copy(k):
        size = cfg.bits[k]
        mine = sc.packet.at[pl.ds((d // size) * size, size)]
        return pltpu.make_async_remote_copy(
            src_ref=mine,
            dst_ref=mine,
            send_sem=sc.pk_send.at[k],
            recv_sem=sc.pk_recv.at[k],
            device_id=bits[k],
            device_id_type=MESH,
        )

    pk_state = [0]

    def packet_start():
        packet_copy(0).start()

    def packet_step():
        k = pk_state[0]
        packet_copy(k).wait()
        pk_state[0] = k + 1
        if k + 1 < len(cfg.bits):
            packet_copy(k + 1).start()

    tokens = cfg.tokens

    def tokens_in():
        loads.features.wait()
        loads.attn_cot.wait()
        for src, dst in ((sc.features, sc.F), (sc.attn_cot, sc.GA)):
            pad = jnp.zeros((TOKENS - tokens, ch), F32)
            dst[0] = jnp.concatenate([src[...].astype(F32), pad], axis=0).astype(BF)

    def send_tokens(ref, k):
        where = pl.ds(0, 208) if k % 2 == 0 else pl.ds(208, 192)
        return swap(9 + k, ref.at[0, where], ref.at[1, where])

    att_scale = ch ** (-0.5)

    def project(k):
        loads.qkv_w.wait()
        loads.proj_w.wait()
        value = nn(sc.F[k], sc.qkv_w[...])
        scaled = value[:, :ch] * att_scale
        sc.Q[k] = scaled.astype(BF)
        sc.K[k] = value[:KEYS, ch : 2 * ch].astype(BF)
        sc.V[k] = value[:KEYS, 2 * ch :].astype(BF)
        sc.MG[k] = nt(sc.GA[k], sc.proj_w[...]).astype(BF)


    def flat(ref):
        return ref[...].reshape(2 * ref.shape[1], ch)

    def scores():
        sc.S[...] = nt(flat(sc.K), flat(sc.Q))

    def prob_grads():
        sc.D[...] = nt(flat(sc.V), flat(sc.MG))

    def softmax(first, last):
        row = lax.broadcasted_iota(jnp.int32, (KEYS, 128), 0)
        real = row < tokens

        @pl.loop(first, last)
        def _(c):
            here = part(c * 128, 128)
            both = [pl.ds(0, KEYS), pl.ds(KEYS, KEYS)]
            value = [jnp.where(real, sc.S[keys, here], -1e30) for keys in both]
            most = jnp.max(jnp.maximum(value[0], value[1]), axis=0, keepdims=True)
            value = [jnp.exp(v - most) for v in value]
            scale = 1.0 / jnp.sum(value[0] + value[1], axis=0, keepdims=True)
            prob = [v * scale for v in value]
            for keys, v in zip(both, prob):
                sc.PR[keys, here] = v.astype(BF)
            back = [sc.D[keys, here] for keys in both]
            total = jnp.sum(prob[0] * back[0] + prob[1] * back[1], axis=0, keepdims=True)
            for keys, v, b in zip(both, prob, back):
                sc.DS[keys, here] = (v * (b - total)).astype(BF)

    def attend():
        mixed = tn(sc.PR[:, 0:512], flat(sc.V))[:KEYS].astype(BF)
        sc.MX[...] = mixed
        put_grad((0, 3 * ch), tn(mixed, sc.GA[0, :KEYS]))

    def attended():
        out = sc.F[0, :KEYS].astype(F32) + nn(sc.MX[...], sc.proj_w[...])
        sc.att[...] = out[:tokens].astype(BF)
        store(sc.att, outs.attended)

    def attention_back():
        pg = sc.PG
        pg[:, 0:ch] = (tn(sc.DS[:, 0:512], flat(sc.K))[:KEYS] * att_scale).astype(BF)
        pg[:, ch : 2 * ch] = nn(sc.DS[0:KEYS], flat(sc.Q)).astype(BF)
        pg[:, 2 * ch :] = nn(sc.PR[0:KEYS], flat(sc.MG)).astype(BF)

    def attention_grads():
        pg = sc.PG
        grad = tn(sc.F[0, :KEYS], pg[...])
        for i in range(3):
            put_grad((0, i * ch), grad[:, i * ch : (i + 1) * ch])

    def features_grad():
        pg = sc.PG
        out = sc.GA[0, :KEYS].astype(F32) + nt(pg[...], sc.qkv_w[...])
        sc.fg[...] = out[:tokens]
        store(sc.fg, outs.features_grad)

    groups = []
    for k, size in enumerate(cfg.groups):
        kept, inbox, extra, send, recv = sc.sums[k]
        groups.append(
            Total(
                size,
                cfg.plans[k],
                cfg.far,
                sc.own[k],
                kept,
                inbox,
                extra,
                sc.result[k],
                send,
                recv,
            )
        )

    def adv(*which):
        for k in which:
            if groups[k].count == 0:
                groups[k].start()
            elif groups[k].busy:
                groups[k].advance()
                if not groups[k].busy:
                    store(sc.result[k], vars(outs)["sum%d" % k])

    summed_grad_own()
    tokens_in()
    hidden_two_grad(near_pair)
    hidden_one()
    down_cot_more()
    hidden_one_halo(0)
    conv_one(near_pair)
    st.tok.append(send_tokens(sc.F, 1))
    film()
    project(0)
    conv_one(edge_pair)
    stats_two()
    send_next_row()
    st.tok.append(send_tokens(sc.GA, 3))
    st.tok.append(send_tokens(sc.F, 0))
    st.tok.append(send_tokens(sc.GA, 2))
    summed_grad_edge()
    skip_grad()
    hidden_two_grad(edge_pair)
    summed_grad_more()
    hidden_two_grad_halo()
    hidden_two()
    conv2_grad(0)
    adv(1)
    conv2_grad(2)
    adv(3)
    hidden_one_halo(1)
    adv(1)
    conv_one_halo()
    adv(3)
    hidden_two_halo()
    summed(near_pair)
    summed(edge_pair)
    adv(1)
    summed_swap()
    down_grad(0)
    adv(4)
    for copy in st.tok:
        copy.wait()
    project(1)
    down_grad(1)
    adv(5)
    scores()
    adv(4)
    adv(3)
    conv_one_grad()
    adv(5)
    adv(1)
    hidden_one_grad(near_pair)
    down_grad(2)
    adv(6)
    conv_one_grad_halo()
    conv1_grad()
    adv(7)
    adv(8)
    adv(4)
    adv(6)
    adv(3)
    hidden_one_grad(edge_pair)
    adv(7)
    adv(8)
    adv(5)
    prob_grads()
    softmax(0, 2)
    adv(4)
    adv(1)
    softmax(2, 4)
    adv(6)
    softmax(4, 6)
    softmax(6, 7)
    adv(3)
    attend()
    adv(8)
    adv(7)
    attention_back()
    adv(5)
    adv(4)
    attention_grads()
    adv(0)
    attended()
    adv(1)
    conv2_grad(1)
    adv(2)
    adv(6)
    adv(0)
    features_grad()
    adv(8)
    down(1)
    adv(2)
    adv(3)
    pre_one_grad(near_pair)
    adv(5)
    adv(7)
    pre_one_grad(edge_pair)
    stats_four()
    adv(3)
    skip_back()
    adv(1)
    adv(4)
    halo_summed()
    down(0)
    store(sc.block, outs.block_out)
    adv(6)
    adv(8)
    adv(0)
    adv(5)
    adv(7)
    adv(4)
    packet_begin()
    image_grad()
    adv(2)
    adv(6)
    packet_step()
    adv(1)
    adv(0)
    adv(7)
    adv(1)
    adv(8)
    adv(5)
    adv(8)
    adv(2)
    adv(6)
    adv(4)
    packet_step()
    adv(0)
    adv(4)
    adv(7)
    adv(2)
    packet_step()
    adv(5)
    adv(6)
    adv(5)
    adv(6)
    adv(7)
    adv(0)
    adv(7)
    adv(0)
    adv(2)
    packet_step()
    adv(2)

    while any(group.busy for group in groups):
        adv(*range(len(groups)))
    while pk_state[0] < len(cfg.bits):
        packet_step()
    store(sc.packet, outs.packet)
    for copy in stores + swaps:
        copy.wait()
    for copy in loading:
        copy.wait()


class Config:
    pass


def finish_kernel(cfg, *refs):
    n_in = len(cfg.finish_in)
    ins = Names(zip(cfg.finish_in, refs[:n_in]))
    n_out = len(cfg.finish_out)
    outs = Names(zip(cfg.finish_out, refs[n_in : n_in + n_out]))
    sc = Names(refs[n_in + n_out])
    ch, chi = cfg.ch, cfg.chi
    copies = []

    def begin(src, dst):
        copy = pltpu.make_async_copy(src, dst, sc.sem.at[len(copies)])
        copy.start()
        copies.append(copy)
        return copy

    small = [
        begin(ins.packet, sc.packet),
        begin(ins.norm2_gain, sc.norm2_gain),
        begin(ins.norm2_bias, sc.norm2_bias),
    ]
    order = cfg.done_order
    got = [begin(vars(ins)["sum%d" % k], sc.low[k]) for k in order]
    through = [
        begin(ins.image_grad, sc.image_grad),
        begin(ins.features_grad, sc.features_grad),
        begin(ins.block_out, sc.block_out),
        begin(ins.attended, sc.attended),
    ]
    passed = (
        (sc.image_grad, outs.image_grad),
        (sc.features_grad, outs.features_grad),
        (sc.block_out, outs.block_out),
        (sc.attended, outs.attended),
    )
    waits = []

    def packet_rows(k):
        return sc.packet[pl.ds(k, cfg.dp, stride=16), :]

    def wide_rows(k):
        return jnp.concatenate([packet_rows(k), packet_rows(k + 1)], axis=1)

    def total(value):
        return jnp.sum(value, axis=0, keepdims=True)

    def widen(low, wide, size):
        step = 256

        @pl.loop(0, size // step)
        def _(i):
            here = part(i * step, step)
            wide[here, 0:128] = low[0, here, :].astype(F32)
            wide[here, 128:256] = low[1, here, :].astype(F32)

    def places(k):
        if 1 <= k <= 3:
            for a in range(3):
                yield a * ch, ch, outs.conv2.at[pl.ds((3 * a + k - 1) * ch, ch)]
        elif k <= 6:
            yield 0, 3 * ch, outs.down.at[pl.ds((k - 4) * 3 * ch, 3 * ch)]
        elif k == 7:
            yield 0, 6 * chi, outs.conv1.at[pl.ds(0, 6 * chi)]
        else:
            yield 0, 3 * chi, outs.conv1.at[pl.ds(6 * chi, 3 * chi)]
            yield 3 * chi, chi, outs.skip

    def film():
        for copy in small:
            copy.wait()
        first, second = wide_rows(4), wide_rows(6)
        scale_grad = sc.norm2_gain[...] * second + sc.norm2_bias[...] * first
        rows = jnp.concatenate([scale_grad, first], axis=1)
        embed = jnp.concatenate([wide_rows(0), wide_rows(2)], axis=1)
        sc.film_w[...] = lax.dot_general(
            embed,
            rows,
            (((0,), (0,)), ((), ())),
            precision=lax.Precision.HIGHEST,
            preferred_element_type=F32,
        )
        sc.film_b[...] = total(rows)
        sc.gain2[...] = total(wide_rows(10))
        sc.bias2[...] = total(wide_rows(8))
        sc.gain1[...] = total(packet_rows(13))
        sc.bias1[...] = total(packet_rows(12))
        for src, dst in (
            (sc.film_w, outs.film_w),
            (sc.film_b, outs.film_b),
            (sc.gain2, outs.gain2),
            (sc.bias2, outs.bias2),
            (sc.gain1, outs.gain1),
            (sc.bias1, outs.bias1),
        ):
            waits.append(begin(src, dst))

    for turn, (k, copy) in enumerate(zip(order, got)):
        if turn == 1:
            film()
        copy.wait()
        if k == 0:
            for i in range(4):
                wide = sc.wide[0] if i < 3 else sc.wide_p
                at = i * ch if i < 3 else 0
                for j in range(2):
                    value = sc.low[0][j, i * ch : (i + 1) * ch, :].astype(F32)
                    wide[:, at + j * 128 : at + (j + 1) * 128] = value
            waits.append(begin(sc.wide[0], outs.qkv))
            waits.append(begin(sc.wide_p, outs.proj))
        else:
            widen(sc.low[k], sc.wide[k], cfg.groups[k])
            for start, size, dst in places(k):
                waits.append(begin(sc.wide[k].at[pl.ds(start, size)], dst))
    for (src, dst), copy in zip(passed, through):
        copy.wait()
        waits.append(begin(src, dst))
    for copy in waits:
        copy.wait()


def body(
    image_in,
    noise_in,
    sigma_in,
    embedding,
    features,
    norm1_gain,
    norm1_bias,
    conv1_w,
    film_w,
    film_b,
    norm2_gain,
    norm2_bias,
    conv2_w,
    skip_w,
    down_w,
    qkv_w,
    proj_w,
    down_cot,
    attn_cot,
):
    cfg = Config()
    cfg.rows, cfg.cols, cfg.chi = image_in.shape[1:]
    cfg.ch = conv1_w.shape[3]
    cfg.tokens = features.shape[1]
    cfg.dp = lax.axis_size("dp")
    cfg.bits = [2**k for k in range(cfg.dp.bit_length() - 1)]
    cfg.far = cfg.bits[4:]
    rows, cols, chi, ch, dp = cfg.rows, cfg.cols, cfg.chi, cfg.ch, cfg.dp
    half = cols // 2
    cfg.groups = [4 * ch] + [3 * ch] * 6 + [6 * chi, 4 * chi]
    cfg.plans = [
        [[1], ["rows", 2], [4, 8]],
        [[1], [2], [4], ["rows", 8]],
        [[1], ["rows", 2], [4, 8]],
        [[1], ["rows", 2], [4, 8]],
        [[1], [2], [4], [8, "rows"]],
        [[1], ["rows"], [2], [4, 8]],
        [[1], [2], ["rows", 4], [8]],
        [[1], [4], ["rows", 2], [8]],
        [[1], ["rows", 2], [4, 8]],
    ]
    cfg.done_order = (3, 1, 8, 4, 5, 6, 7, 0, 2)
    args = dict(
        sigma_in=sigma_in,
        image_in=image_in[0],
        noise_in=noise_in[0],
        norm1_gain=norm1_gain.reshape(1, chi),
        norm1_bias=norm1_bias.reshape(1, chi),
        down_cot=down_cot[0],
        down_w=down_w.reshape(3, 3 * ch, ch),
        conv1_w=conv1_w.reshape(3, 3 * chi, ch),
        conv2_w=conv2_w.reshape(3, 3 * ch, ch),
        skip_w=skip_w,
        features=features[0],
        attn_cot=attn_cot[0],
        embedding=embedding,
        film_w=film_w,
        film_b=film_b.reshape(1, 2 * ch),
        norm2_gain=norm2_gain.reshape(1, ch),
        norm2_bias=norm2_bias.reshape(1, ch),
        qkv_w=qkv_w,
        proj_w=proj_w,
    )
    cfg.inputs = tuple(args)
    shape = jax.ShapeDtypeStruct
    out_shapes = dict(
        block_out=shape((2, half, ch), BF),
        attended=shape((cfg.tokens, ch), BF),
        image_grad=shape((rows, cols, chi), F32),
        features_grad=shape((cfg.tokens, ch), F32),
        packet=shape((dp, 16, 128), F32),
    )
    for k, size in enumerate(cfg.groups):
        out_shapes["sum%d" % k] = shape((2, size, 128), BF)
    cfg.outputs = tuple(out_shapes)
    vm = pltpu.VMEM
    scratch = {
        name: vm(value.shape, value.dtype)
        for name, value in args.items()
        if value is not sigma_in and value is not args["down_cot"]
    }
    scratch.update(
        dc=vm((5, half, ch), BF),
        xh=vm((2, cols, chi), BF),
        xs=vm((rows, cols, chi), F32),
        stage_i=vm((chi // 128, cols + 16, 128), F32),
        stage_o=vm((chi // 128, cols + 16, 128), F32),
        stage_c=vm((ch // 128, cols + 16, 128), F32),
        stage_h=vm((ch // 128, half + 16, 128), F32),
        h1c=vm((rows + 4, cols, 3 * chi), BF),
        h2c=vm((rows + 2, cols, 3 * ch), BF),
        sg3=vm((rows + 4, cols, 3 * ch), BF),
        cg=vm((rows + 2, cols, ch), BF),
        s3=vm((rows + 1, half, 3 * ch), BF),
        c1=vm((rows + 1, cols, ch), F32),
        g2=vm((rows + 1, cols, ch), F32),
        h1g=vm((rows, cols, chi), F32),
        skb=vm((rows, cols, chi), F32),
        block=vm((2, half, ch), BF),
        st_out=vm((4, 8, ch), F32),
        st_in=vm((4, 8, ch), F32),
        packet=vm((dp, 16, 128), F32),
        F=vm((2, TOKENS, ch), BF),
        GA=vm((2, TOKENS, ch), BF),
        Q=vm((2, TOKENS, ch), BF),
        K=vm((2, KEYS, ch), BF),
        V=vm((2, KEYS, ch), BF),
        MG=vm((2, TOKENS, ch), BF),
        S=vm((2 * KEYS, 2 * TOKENS), F32),
        D=vm((2 * KEYS, 2 * TOKENS), F32),
        PR=vm((2 * KEYS, 2 * TOKENS), BF),
        DS=vm((2 * KEYS, 2 * TOKENS), BF),
        PG=vm((KEYS, 3 * ch), BF),
        MX=vm((KEYS, ch), BF),
        att=vm((cfg.tokens, ch), BF),
        fg=vm((cfg.tokens, ch), F32),
        own=[vm((2, size, 128), BF) for size in cfg.groups],
        result=[vm((2, size, 128), BF) for size in cfg.groups],
        sums=[total_scratch(*plan, cfg.far) for plan in zip(cfg.groups, cfg.plans)],
        load_sem=pltpu.SemaphoreType.DMA((len(args),)),
        store_sem=pltpu.SemaphoreType.DMA((len(out_shapes),)),
        x_send=pltpu.SemaphoreType.DMA((13,)),
        x_recv=pltpu.SemaphoreType.DMA((13,)),
        pk_send=pltpu.SemaphoreType.DMA((len(cfg.bits),)),
        pk_recv=pltpu.SemaphoreType.DMA((len(cfg.bits),)),
    )
    made = pl.pallas_call(
        functools.partial(level_kernel, cfg),
        out_shape=list(out_shapes.values()),
        in_specs=[SMEM] + [ANY] * (len(args) - 1),
        out_specs=[ANY] * len(out_shapes),
        scratch_shapes=[scratch],
        compiler_params=pltpu.CompilerParams(
            collective_id=0, has_side_effects=True, vmem_limit_bytes=62 * 2**20
        ),
        name="level",
    )(*args.values())
    made = dict(zip(cfg.outputs, made))

    small = dict(
        packet=made["packet"].reshape(dp * 16, 128),
        norm2_gain=args["norm2_gain"],
        norm2_bias=args["norm2_bias"],
    )
    big = {name: value for name, value in made.items() if name not in small}
    cfg.finish_in = tuple(small) + tuple(big)
    finals = dict(
        block_out=out_shapes["block_out"],
        attended=out_shapes["attended"],
        image_grad=out_shapes["image_grad"],
        features_grad=out_shapes["features_grad"],
        conv1=shape((9 * chi, ch), F32),
        conv2=shape((9 * ch, ch), F32),
        skip=shape((chi, ch), F32),
        down=shape((9 * ch, ch), F32),
        qkv=shape((ch, 3 * ch), F32),
        proj=shape((ch, ch), F32),
    )
    finals.update(
        gain1=shape((1, chi), F32),
        bias1=shape((1, chi), F32),
        film_w=shape((2 * ch, 2 * ch), F32),
        film_b=shape((1, 2 * ch), F32),
        gain2=shape((1, ch), F32),
        bias2=shape((1, ch), F32),
    )
    cfg.finish_out = tuple(finals)
    finish_scratch = dict(
        low=[vm((2, size, 128), BF) for size in cfg.groups],
        wide=[vm((ch, 3 * ch), F32)] + [vm((size, ch), F32) for size in cfg.groups[1:]],
        wide_p=vm((ch, ch), F32),
        image_grad=vm((rows, cols, chi), F32),
        features_grad=vm((cfg.tokens, ch), F32),
        block_out=vm((2, half, ch), BF),
        attended=vm((cfg.tokens, ch), BF),
        packet=vm((dp * 16, 128), F32),
        norm2_gain=vm((1, ch), F32),
        norm2_bias=vm((1, ch), F32),
        gain1=vm((1, chi), F32),
        bias1=vm((1, chi), F32),
        film_w=vm((2 * ch, 2 * ch), F32),
        film_b=vm((1, 2 * ch), F32),
        gain2=vm((1, ch), F32),
        bias2=vm((1, ch), F32),
        sem=pltpu.SemaphoreType.DMA((48,)),
    )
    done = pl.pallas_call(
        functools.partial(finish_kernel, cfg),
        out_shape=list(finals.values()),
        in_specs=[ANY] * len(cfg.finish_in),
        out_specs=[ANY] * len(finals),
        scratch_shapes=[finish_scratch],
        compiler_params=pltpu.CompilerParams(vmem_limit_bytes=56 * 2**20),
        name="finish",
    )(*small.values(), *big.values())
    done = Names(zip(cfg.finish_out, done))
    return (
        done.block_out[None],
        done.attended[None],
        done.image_grad[None],
        done.features_grad[None],
        done.gain1.reshape(chi),
        done.bias1.reshape(chi),
        done.conv1.reshape(conv1_w.shape),
        done.film_w,
        done.film_b.reshape(2 * ch),
        done.gain2.reshape(ch),
        done.bias2.reshape(ch),
        done.conv2.reshape(conv2_w.shape),
        done.skip,
        done.down.reshape(down_w.shape),
        done.qkv,
        done.proj,
    )


def solution(mesh):
    placed = (
        P("dp", "rows", None, None),
        P("dp", "rows", None, None),
        P("dp"),
        P("dp", None),
        P("dp", "rows", None),
        P(),
        P(),
        P(),
        P(),
        P(),
        P(),
        P(),
        P(),
        P(),
        P(),
        P(),
        P(),
        P("dp", "rows", None, None),
        P("dp", "rows", None),
    )
    return jax.shard_map(
        body,
        mesh=mesh,
        in_specs=placed,
        out_specs=(
            P("dp", "rows", None, None),
            P("dp", "rows", None),
            P("dp", "rows", None, None),
            P("dp", "rows", None),
            P(),
            P(),
            P(),
            P(),
            P(),
            P(),
            P(),
            P(),
            P(),
            P(),
            P(),
            P(),
        ),
        check_vma=False,
    )
```

```python
import functools

import jax
import jax.numpy as jnp
from jax import lax
from jax.experimental import pallas as pl
from jax.experimental.pallas import tpu as pltpu
from jax.sharding import PartitionSpec as P

G = 32
EPSILON = 1e-05
SIGMA_DATA = 0.5
MESH = pl.DeviceIdType.MESH
ANY = pl.BlockSpec(memory_space=pl.ANY)
SMEM = pl.BlockSpec(memory_space=pltpu.SMEM)
BF = jnp.bfloat16
F32 = jnp.float32
TOKENS = 448
KEYS = 400


def flip(index, bit):
    return index + bit * (1 - 2 * ((index // bit) % 2))


class Side:
    def __init__(self, names):
        d = lax.axis_index("dp")
        r = lax.axis_index("rows")
        self.mine = []
        for name in names:
            self.mine.append(r if name == "rows" else (d // name) % 2)
        self.parts = 2 ** len(names)
        self.names = names
        self.position = (d, r)

    def partners(self):
        found = []
        for flips in range(1, self.parts):
            d, r = self.position
            index = 0
            for k, name in enumerate(self.names):
                other = (flips >> k) % 2
                side = self.mine[k]
                if other:
                    side = 1 - side
                    if name == "rows":
                        r = 1 - r
                    else:
                        d = flip(d, name)
                index = index * 2 + side
            found.append(((d, r), index))
        return found

    @property
    def index(self):
        index = 0
        for side in self.mine:
            index = index * 2 + side
        return index


def part(start, size):
    return pl.ds(pl.multiple_of(start, size), size)


class Total:
    def __init__(self, rows, stages, whole, own, kept, inbox, extra, result, send, recv):
        self.rows = rows
        self.stages = [Side(names) for names in stages]
        self.whole = [Side([name]) for name in whole]
        self.own = own
        self.kept = kept
        self.inbox = inbox
        self.extra = extra
        self.result = result
        self.send = send
        self.recv = recv
        self.sizes = sizes_of(rows, stages)
        self.steps = len(stages)
        self.copies = None
        self.count = 0

    def begin(self, src, dst, where):
        k = self.count
        self.count += 1
        copy = pltpu.make_async_remote_copy(
            src_ref=src,
            dst_ref=dst,
            send_sem=self.send.at[k],
            recv_sem=self.recv.at[k],
            device_id=where,
            device_id_type=MESH,
        )
        copy.start()
        self.copies.append(copy)

    def scatter(self, step):
        side = self.stages[step]
        size = self.sizes[step]
        for slot, (where, index) in enumerate(side.partners()):
            if step == 0:
                src = self.own.at[index]
            else:
                src = self.kept[step - 1].at[part(index * size, size)]
            self.begin(src, self.inbox[step].at[slot], where)

    def start(self):
        self.copies = []
        self.scatter(0)
        self.stage = 0

    def region(self, step):
        lead = self.stages[0].index
        if step == 0:
            return self.result.at[lead]
        offset = 0
        for t in range(1, step + 1):
            offset = offset + self.stages[t].index * self.sizes[t]
        return self.result.at[lead, part(offset, self.sizes[step])]

    def gather(self, step):
        mine = self.region(step)
        for where, _ in self.stages[step].partners():
            self.begin(mine, mine, where)

    def swap_whole(self, k):
        (where, _), = self.whole[k].partners()
        self.begin(self.kept[self.steps - 1 + k], self.extra.at[k], where)

    def advance(self):
        stage = self.stage
        last = self.steps - 1
        for copy in self.copies:
            copy.wait()
        self.copies = []
        if stage < self.steps:
            side = self.stages[stage]
            size = self.sizes[stage]
            if stage == 0:
                have = self.own.at[side.index]
            else:
                have = self.kept[stage - 1].at[part(side.index * size, size)]
            if stage == last and not self.whole:
                dest = self.region(last)
            else:
                dest = self.kept[stage]
            add_rows(dest, have, self.inbox[stage], side.parts - 1, size)
            if stage < last:
                self.scatter(stage + 1)
            elif self.whole:
                self.swap_whole(0)
            else:
                self.gather(last)
        elif stage < self.steps + len(self.whole):
            k = stage - self.steps
            final = k == len(self.whole) - 1
            dest = self.region(last) if final else self.kept[last + k + 1]
            add_rows(dest, self.kept[last + k], self.extra.at[pl.ds(k, 1)], 1, self.sizes[last])
            if final:
                self.gather(last)
            else:
                self.swap_whole(k + 1)
        else:
            k = stage - self.steps - len(self.whole)
            if k < last:
                self.gather(last - 1 - k)
            else:
                self.copies = None
        self.stage = stage + 1

    @property
    def busy(self):
        return self.copies is not None


def add_rows(dest, have, got, count, size):
    block = size
    while block > 400:
        block //= 2 if (block // 2) % 16 == 0 else 3

    def add(here):
        value = have[here].astype(jnp.float32)
        for slot in range(count):
            value = value + got[slot, here].astype(jnp.float32)
        dest[here] = value.astype(jnp.bfloat16)

    if block == size:
        add(pl.ds(0, size))
    else:

        @pl.loop(0, size // block)
        def _(i):
            add(part(i * block, block))


def sizes_of(rows, stages):
    sizes = [rows]
    for names in stages[1:]:
        sizes.append(sizes[-1] // 2 ** len(names))
    return sizes


def copies_of(stages, whole):
    return 2 * sum(2 ** len(names) - 1 for names in stages) + len(whole)


def total_scratch(rows, stages, whole):
    sizes = sizes_of(rows, stages)
    kept = [pltpu.VMEM((size, 128), jnp.bfloat16) for size in sizes + [sizes[-1]] * len(whole)]
    inbox = [
        pltpu.VMEM((2 ** len(names) - 1, size, 128), jnp.bfloat16)
        for names, size in zip(stages, sizes)
    ]
    extra = pltpu.VMEM((max(len(whole), 1), sizes[-1], 128), jnp.bfloat16)
    count = copies_of(stages, whole)
    return [
        kept,
        inbox,
        extra,
        pltpu.SemaphoreType.DMA((count,)),
        pltpu.SemaphoreType.DMA((count,)),
    ]


class Names:
    def __init__(self, pairs=()):
        vars(self).update(pairs)


class Once:
    def __init__(self, copy):
        self.copy = copy
        self.waited = False
        copy.start()

    def wait(self):
        if not self.waited:
            self.waited = True
            self.copy.wait()


def nn(left, right):
    return lax.dot_general(left, right, (((1,), (0,)), ((), ())), preferred_element_type=F32)


def nt(left, right):
    return lax.dot_general(left, right, (((1,), (1,)), ((), ())), preferred_element_type=F32)


def tn(left, right):
    return lax.dot_general(left, right, (((0,), (0,)), ((), ())), preferred_element_type=F32)


def fold(value):
    rows, lanes = value.shape
    return jnp.sum(value.reshape(rows // 8, 8, lanes), axis=0)


def one_row(value):
    return jnp.sum(value, axis=0, keepdims=True)


def group_sum(value, width):
    lanes = value.shape[1]
    lane = lax.broadcasted_iota(jnp.int32, value.shape, 1)
    step = 1
    while step < width:
        up = pltpu.roll(value, lanes - step, 1)
        down = pltpu.roll(value, step, 1)
        value = value + jnp.where((lane // step) % 2 == 0, up, down)
        step *= 2
    return value


def sigmoid(value):
    return 0.5 + 0.5 * jnp.tanh(0.5 * value)


def spread(row, staged, lanes):
    cells = row.shape[0]
    for b in range(3):
        for k in range(lanes // 128):
            at = b * lanes + k * 128
            row[:, at : at + 128] = staged[k, 7 + b : 7 + b + cells, :].astype(BF)


def put(staged, start, value):
    cells, lanes = value.shape
    for k in range(lanes // 128):
        staged[k, pl.ds(start, cells), :] = value[:, k * 128 : (k + 1) * 128]


def level_kernel(cfg, *refs):
    n_in = len(cfg.inputs)
    ins = Names(zip(cfg.inputs, refs[:n_in]))
    outs = Names(zip(cfg.outputs, refs[n_in : n_in + len(cfg.outputs)]))
    sc = Names(refs[n_in + len(cfg.outputs)])
    st = Names()
    rows, cols, chi, ch = cfg.rows, cfg.cols, cfg.chi, cfg.ch
    half = cols // 2
    r = lax.axis_index("rows")
    d = lax.axis_index("dp")
    across = (d, 1 - r)

    loads = Names()
    loading = []

    def load(name, dst):
        copy = Once(pltpu.make_async_copy(vars(ins)[name], dst, sc.load_sem.at[len(loading)]))
        loading.append(copy)
        setattr(loads, name, copy)

    stores = []

    def store(src, dst):
        copy = pltpu.make_async_copy(src, dst, sc.store_sem.at[len(stores)])
        copy.start()
        stores.append(copy)

    def swap_copy(k, src, dst):
        return pltpu.make_async_remote_copy(
            src_ref=src,
            dst_ref=dst,
            send_sem=sc.x_send.at[k],
            recv_sem=sc.x_recv.at[k],
            device_id=across,
            device_id_type=MESH,
        )

    swaps = []

    def swap(k, src, dst):
        copy = Once(swap_copy(k, src, dst))
        swaps.append(copy)
        return copy

    barrier = pltpu.get_barrier_semaphore()
    greeted = {}
    for stages in cfg.plans:
        for names in stages + [[name] for name in cfg.far]:
            side = Side(names)
            for flips, (where, _) in enumerate(side.partners(), 1):
                met = frozenset(n for k, n in enumerate(names) if (flips >> k) % 2)
                greeted[met] = where
    for where in greeted.values():
        pl.semaphore_signal(barrier, inc=1, device_id=where, device_id_type=MESH)

    sc.down_cot = sc.dc.at[1:3]
    names = cfg.inputs[1:]
    for name in names[:4]:
        load(name, vars(sc)[name])

    sigma = jnp.full((1, chi), ins.sigma_in[0], F32)
    scale_in = lax.rsqrt(SIGMA_DATA * SIGMA_DATA + sigma * sigma)
    loads.image_in.wait()
    loads.noise_in.wait()
    for name in names[4:]:
        load(name, vars(sc)[name])
    piece = cols // 2

    def stats_one(i, carry):
        row, col = i // 2, i % 2
        here = part(col * half, half)
        value = scale_in * (
            sc.image_in[row, here].astype(F32) + sigma * sc.noise_in[row, here].astype(F32)
        )
        sc.xs[row, here] = value
        sc.image_in[row, here] = value.astype(BF)
        return carry[0] + fold(value), carry[1] + fold(value * value)

    zero8 = jnp.zeros((8, chi), F32)
    sum_a, sum_b = lax.fori_loop(0, rows * 2, stats_one, (zero8, zero8))
    low_in = sc.image_in

    def send_stats(k, top, bottom):
        lanes = top.shape[1]
        sc.st_out[k, 0:1, 0:lanes] = top
        sc.st_out[k, 1:2, 0:lanes] = bottom
        copy = swap(1 + k, sc.st_out.at[k], sc.st_in.at[k])
        return copy

    def both_stats(k, copy, lanes):
        copy.wait()
        total = sc.st_out[k, :, 0:lanes] + sc.st_in[k, :, 0:lanes]
        return total[0:1], total[1:2]

    pl.semaphore_wait(barrier, len(greeted))
    swap_one = send_stats(0, one_row(sum_a), one_row(sum_b))

    edge = 4 - 3 * r
    rows_one = [swap(6, low_in.at[edge - 1], sc.xh.at[0])]

    def send_next_row():
        rows_one.append(swap(8, low_in.at[2 - r], sc.xh.at[1]))

    dc_swap = swap(0, ins.down_cot.at[1 - r], sc.dc.at[3 * r])
    dc_more = swap_copy(5, ins.down_cot.at[1], sc.dc.at[4])

    def down_cot_more():
        @pl.when(r == 1)
        def _():
            dc_more.start()

    for ref in (sc.stage_i, sc.stage_o, sc.stage_c, sc.stage_h):
        zeros = jnp.zeros((ref.shape[0], 8, 128), F32)
        ref[:, 0:8, :] = zeros
        ref[:, ref.shape[1] - 8 :, :] = zeros
    outer = 5 * r
    inner = 5 * (1 - r)
    sc.h1c[outer + 1] = jnp.zeros((cols, 3 * chi), BF)
    sc.h2c[outer] = jnp.zeros((cols, 3 * ch), BF)
    sc.cg[outer] = jnp.zeros((cols, ch), BF)
    sc.sg3[outer + 1] = jnp.zeros((cols, 3 * ch), BF)
    sc.dc[3 * r] = jnp.zeros((half, ch), BF)
    for ref in (sc.F, sc.GA):
        ref[1, 400:, :] = jnp.zeros((TOKENS - 400, ch), BF)

    @pl.when(r == 0)
    def _():
        sc.s3[0] = jnp.zeros((half, 3 * ch), BF)

    dw = sc.down_w
    loads.down_cot.wait()
    loads.down_w.wait()

    def shifted_cot(m):
        staged = sc.stage_h
        put(staged, 8, sc.dc[m].astype(F32))
        right = [staged[k, 9 : 9 + half, :].astype(BF) for k in range(ch // 128)]
        return sc.dc[m], jnp.concatenate(right, axis=1)

    def dw_tap(a, b):
        return dw[a, b * ch : (b + 1) * ch, :]

    def even_row(m):
        here, right = shifted_cot(m)
        return nt(here, dw_tap(1, 1)), nt(here, dw_tap(1, 2)) + nt(right, dw_tap(1, 0))

    def odd_row(m):
        here, right = shifted_cot(m)
        even = nt(here, dw_tap(2, 1))
        odd = nt(here, dw_tap(2, 2)) + nt(right, dw_tap(2, 0))
        here, right = shifted_cot(m + 1)
        even += nt(here, dw_tap(0, 1))
        odd += nt(here, dw_tap(0, 2)) + nt(right, dw_tap(0, 0))
        return even, odd

    def put_row(l, pair):
        staged = sc.stage_c
        for k in range(ch // 128):
            for odd in range(2):
                value = pair[odd][:, k * 128 : (k + 1) * 128]
                staged[k, pl.ds(8 + odd, half, stride=2), :] = value
        spread(sc.sg3.at[l + 1], staged, ch)

    def summed_grad_own():
        @pl.loop(0, 2)
        def _(k):
            put_row(1 + 2 * k, even_row(1 + k))

        put_row(2, odd_row(1))

        @pl.when(r == 1)
        def _():
            put_row(4, odd_row(2))

    def summed_grad_edge():
        dc_swap.wait()

        @pl.when(r == 0)
        def _():
            put_row(4, odd_row(2))
            put_row(5, even_row(3))

        @pl.when(r == 1)
        def _():
            put_row(0, odd_row(0))

    def summed_grad_more():
        @pl.when(r == 0)
        def _():
            dc_more.wait_recv()
            put_row(6, odd_row(3))

        @pl.when(r == 1)
        def _():
            dc_more.wait_send()
            put_row(-1, even_row(0))

    gain1 = lambda: sc.norm1_gain[...]
    bias1 = lambda: sc.norm1_bias[...]
    count1 = float(2 * rows * cols * (chi // G))
    count2 = float(2 * rows * cols * (ch // G))

    def moments(first, second, width, count):
        mean = group_sum(first, width) / count
        return mean, lax.rsqrt(group_sum(second, width) / count - mean * mean + EPSILON)

    st.sums2 = (0.0, 0.0)
    st.tok = []
    st.sums4 = (zero8, zero8)

    def row_one(place, values):
        mean, inverse = st.mean1, st.inv1

        @pl.loop(0, 2)
        def _(c):
            here = part(c * piece, piece)
            pre = (values[here].astype(F32) - mean) * inverse * gain1() + bias1()
            put(sc.stage_i, pl.multiple_of(8 + c * piece, 8), pre * sigmoid(pre))

        spread(sc.h1c.at[place], sc.stage_i, chi)

    def hidden_one():
        loads.norm1_gain.wait()
        loads.norm1_bias.wait()
        first, second = both_stats(0, swap_one, chi)
        st.mean1, st.inv1 = moments(first, second, chi // G, count1)

        @pl.loop(0, rows)
        def _(i):
            row_one(2 + i, sc.xs.at[i])

    def hidden_one_halo(k):
        rows_one[k].wait()
        row_one(inner + 1 if k == 0 else 7 * (1 - r), sc.xh.at[k])

    near_pair = 1 + 2 * r
    edge_pair = 3 - 2 * r

    def conv_rows(source, weight, base, count, lanes):
        left = [
            source[pl.ds(base - 1 + a, count)].reshape(count * cols, 3 * lanes) for a in range(3)
        ]
        return nn(jnp.concatenate(left, axis=1), weight[...].reshape(9 * lanes, ch))

    def conv_one(base):
        loads.conv1_w.wait()
        acc = conv_rows(sc.h1c, sc.conv1_w, base + 1, 2, chi)
        sc.c1[pl.ds(base - 1, 2)] = acc.reshape(2, cols, ch)
        sums = fold(acc), fold(acc * acc)
        st.sums2 = tuple(x + y for x, y in zip(st.sums2, sums))

    def conv_one_halo():
        sc.c1[rows] = conv_rows(sc.h1c, sc.conv1_w, inner + 1, 1, chi)

    def stats_two():
        first, second = st.sums2
        st.swap2 = send_stats(1, one_row(first), one_row(second))

    def back_pair(source, weight, base, lanes):
        return back_rows(source, weight, base, 2, lanes)

    def back_rows(source, weight, base, count, lanes):
        acc = None
        for a in range(3):
            for b in range(3):
                left = source[pl.ds(base - 1 + a, count), :, b * ch : (b + 1) * ch]
                term = nt(
                    left.reshape(count * cols, ch), weight[2 - a, (2 - b) * lanes : (3 - b) * lanes, :]
                )
                acc = term if acc is None else acc + term
        return acc

    def hidden_two_grad(base):
        loads.conv2_w.wait()
        acc = back_pair(sc.sg3, sc.conv2_w, base + 1, ch)
        sc.g2[pl.ds(base - 1, 2)] = acc.reshape(2, cols, ch)

    def hidden_two_grad_halo():
        sc.g2[rows] = back_rows(sc.sg3, sc.conv2_w, inner + 1, 1, ch)

    def grad_rows():
        return sc.sg3[2:6, :, ch : 2 * ch].reshape(rows * cols, ch)

    down_at = [(4, 0), (5, 0), (6, 0)]
    conv1_at = [(7, 0), (7, 3 * chi), (8, 0)]
    skip_at = (8, 3 * chi)

    def put_grad(place, value):
        group, start = place
        low = value.astype(BF)
        size = low.shape[0]
        sc.own[group][0, start : start + size, :] = low[:, :128]
        sc.own[group][1, start : start + size, :] = low[:, 128:]

    def skip_back():
        loads.skip_w.wait()
        sc.skb[...] = nt(grad_rows(), sc.skip_w[...]).reshape(rows, cols, chi)

    def skip_grad():
        put_grad(skip_at, tn(low_in[...].reshape(rows * cols, chi), grad_rows()))

    def film():
        for copy in (
            loads.embedding,
            loads.film_w,
            loads.film_b,
            loads.norm2_gain,
            loads.norm2_bias,
        ):
            copy.wait()
        row = nn(sc.embedding[...], sc.film_w[...]) + sc.film_b[...]
        scale = 1.0 + row[:, :ch]
        shift = row[:, ch:]
        gain, bias = sc.norm2_gain[...], sc.norm2_bias[...]
        st.scale = scale
        st.pre_gain = gain * scale
        st.pre_bias = bias * scale + shift

    def hidden_two():
        first, second = both_stats(1, st.swap2, ch)
        mean, inverse = moments(first, second, ch // G, count2)
        st.mean2, st.inv2 = mean, inverse
        step = cols // 8

        def row_of(l, carry):
            staged = sc.stage_c

            def cells(c, carry):
                here = part(c * step, step)
                hat = (sc.c1[l - 1, here] - mean) * inverse
                sc.c1[l - 1, here] = hat
                pre = hat * st.pre_gain + st.pre_bias
                gate = sigmoid(pre)
                value = pre * gate
                put(staged, pl.multiple_of(8 + c * step, 8), value)
                grad = sc.g2[l - 1, here] * (gate + value * (1.0 - gate))
                sc.g2[l - 1, here] = grad
                return carry[0] + fold(grad), carry[1] + fold(grad * hat)

            carry = lax.fori_loop(0, 8, cells, carry)
            spread(sc.h2c.at[l], staged, ch)
            return carry

        zero = jnp.zeros((8, ch), F32)
        carry = lax.fori_loop(0, rows, lambda i, carry: row_of(1 + i, carry), (zero, zero))
        st.swap3 = send_stats(2, one_row(carry[0]), one_row(carry[1]))

    def hidden_two_halo():
        step = cols // 8

        @pl.loop(0, 8)
        def _(c):
            here = part(c * step, step)
            hat = (sc.c1[rows, here] - st.mean2) * st.inv2
            sc.c1[rows, here] = hat
            pre = hat * st.pre_gain + st.pre_bias
            put(sc.stage_c, pl.multiple_of(8 + c * step, 8), pre * sigmoid(pre))

        spread(sc.h2c.at[inner], sc.stage_c, ch)

    def conv2_grad(b):
        left = sc.h2c[1:5, :, b * ch : (b + 1) * ch].reshape(rows * cols, ch)
        right = [
            sc.sg3[3 - a : 7 - a, :, ch : 2 * ch].reshape(rows * cols, ch) for a in range(3)
        ]
        grad = tn(left, jnp.concatenate(right, axis=1))
        for a in range(3):
            put_grad((1 + b, a * ch), grad[:, a * ch : (a + 1) * ch])

    def odd_shift(row):
        staged = sc.stage_h
        put(staged, 8, row[:, 2 * ch :].astype(F32))
        for k in range(ch // 128):
            row[:, k * 128 : (k + 1) * 128] = staged[k, 7 : 7 + half, :].astype(BF)

    def summed(base):
        loads.skip_w.wait()
        loads.conv2_w.wait()
        acc = conv_rows(sc.h2c, sc.conv2_w, base, 2, ch)
        low = low_in[pl.ds(base - 1, 2)].reshape(2 * cols, chi)
        acc = (acc + nn(low, sc.skip_w[...])).reshape(2, cols, ch)
        for k in range(2):
            staged = sc.stage_c
            put(staged, 8, acc[k])
            row = sc.s3.at[base + k]
            for i in range(ch // 128):
                for odd in range(2):
                    at = (1 + odd) * ch + i * 128
                    value = staged[i, pl.ds(8 + odd, half, stride=2), :]
                    row[:, at : at + 128] = value.astype(BF)
            odd_shift(row)

    def summed_swap():
        copy = swap_copy(7, sc.s3.at[4, :, ch:], sc.s3.at[0, :, ch:])
        st.s3 = copy

        @pl.when(r == 0)
        def _():
            copy.start()

    def halo_summed():
        copy = st.s3

        @pl.when(r == 0)
        def _():
            copy.wait_send()

        @pl.when(r == 1)
        def _():
            copy.wait_recv()
            odd_shift(sc.s3.at[0])

    def down(k):
        acc = None
        for a in range(3):
            term = nn(sc.s3[2 * k + a], dw[a])
            acc = term if acc is None else acc + term
        sc.block[k] = acc.astype(BF)

    def down_grad(a):
        first, cot = ((2, 2), (1, 1), (2, 1))[a]
        value = tn(sc.s3[first], sc.dc[cot]) + tn(sc.s3[first + 2], sc.dc[cot + 1])
        put_grad(down_at[a], value)

    def back_two(grad, hat):
        return (grad * st.pre_gain - st.m1 - hat * st.m2) * st.inv2

    def conv_one_grad():
        first, second = both_stats(2, st.swap3, ch)
        st.A, st.B = first, second
        st.m1 = group_sum(first * st.pre_gain, ch // G) / count2
        st.m2 = group_sum(second * st.pre_gain, ch // G) / count2
        step = cols // 4

        @pl.loop(0, rows * 4)
        def _(i):
            row, here = i // 4, part(i % 4 * step, step)
            sc.cg[1 + row, here] = back_two(sc.g2[row, here], sc.c1[row, here]).astype(BF)

    def conv_one_grad_halo():
        step = cols // 4

        @pl.loop(0, 4)
        def _(c):
            here = part(c * step, step)
            hat = sc.c1[rows, here]
            pre = hat * st.pre_gain + st.pre_bias
            gate = sigmoid(pre)
            grad = sc.g2[rows, here] * (gate + pre * gate * (1.0 - gate))
            sc.cg[inner, here] = back_two(grad, hat).astype(BF)

    def conv1_grad():
        left = sc.h1c[2:6].reshape(rows * cols, 3 * chi)
        right = [sc.cg[2 - a : 6 - a].reshape(rows * cols, ch) for a in range(3)]
        grad = tn(left, jnp.concatenate(right, axis=1))
        for a in range(3):
            put_grad(conv1_at[a], grad[:, a * ch : (a + 1) * ch])

    def hidden_one_grad(base):
        acc = None
        for a in range(3):
            left = sc.cg[pl.ds(base - 1 + a, 2)].reshape(2 * cols, ch)
            term = nt(left, sc.conv1_w[2 - a])
            acc = term if acc is None else acc + term
        acc = acc.reshape(2, cols, 3 * chi)
        for i in range(2):
            put(sc.stage_i, 8, acc[i, :, 0:chi])
            put(sc.stage_o, 8, acc[i, :, 2 * chi :])
            right = sc.stage_i[0, 9 : 9 + cols, :]
            left = sc.stage_o[0, 7 : 7 + cols, :]
            sc.h1g[base - 1 + i] = acc[i, :, chi : 2 * chi] + right + left

    def pre_one_grad(base):
        mean, inverse = st.mean1, st.inv1

        def cells(i, carry):
            row, col = base - 1 + i // 2, i % 2
            here = part(col * piece, piece)
            hat = (sc.xs[row, here] - mean) * inverse
            sc.xs[row, here] = hat
            pre = hat * gain1() + bias1()
            gate = sigmoid(pre)
            grad = sc.h1g[row, here] * (gate + pre * gate * (1.0 - gate))
            sc.h1g[row, here] = grad
            return carry[0] + fold(grad), carry[1] + fold(grad * hat)

        st.sums4 = lax.fori_loop(0, 4, cells, st.sums4)

    def stats_four():
        first, second = st.sums4
        st.swap4 = send_stats(3, one_row(first), one_row(second))

    def packet_begin():
        first, second = both_stats(3, st.swap4, chi)
        st.C, st.D = first, second
        pk = sc.packet.at[d]
        values = (
            sc.embedding[...].astype(F32),
            st.A,
            st.B,
            st.scale * st.A,
            st.scale * st.B,
            first,
            second,
            jnp.zeros((1, 256), F32),
        )
        at = 0
        for value in values:
            for k in range(value.shape[1] // 128):
                pk[at : at + 1, :] = value[:, k * 128 : (k + 1) * 128]
                at += 1
        packet_start()

    def image_grad():
        first, second = st.C, st.D
        m1 = group_sum(first * gain1(), chi // G) / count1
        m2 = group_sum(second * gain1(), chi // G) / count1

        @pl.loop(0, rows * 2)
        def _(i):
            row, col = i // 2, i % 2
            here = part(col * piece, piece)
            value = (
                sc.h1g[row, here] * gain1() - m1 - sc.xs[row, here] * m2
            ) * st.inv1 + sc.skb[row, here]
            sc.h1g[row, here] = scale_in * value

        store(sc.h1g, outs.image_grad)

    bits = [Side([bit]).partners()[0][0] for bit in cfg.bits]

    def packet_copy(k):
        size = cfg.bits[k]
        mine = sc.packet.at[pl.ds((d // size) * size, size)]
        return pltpu.make_async_remote_copy(
            src_ref=mine,
            dst_ref=mine,
            send_sem=sc.pk_send.at[k],
            recv_sem=sc.pk_recv.at[k],
            device_id=bits[k],
            device_id_type=MESH,
        )

    pk_state = [0]

    def packet_start():
        packet_copy(0).start()

    def packet_step():
        k = pk_state[0]
        packet_copy(k).wait()
        pk_state[0] = k + 1
        if k + 1 < len(cfg.bits):
            packet_copy(k + 1).start()

    tokens = cfg.tokens

    def tokens_in():
        loads.features.wait()
        loads.attn_cot.wait()
        for src, dst in ((sc.features, sc.F), (sc.attn_cot, sc.GA)):
            pad = jnp.zeros((TOKENS - tokens, ch), F32)
            dst[0] = jnp.concatenate([src[...].astype(F32), pad], axis=0).astype(BF)

    def send_tokens(ref, k):
        where = pl.ds(0, 208) if k % 2 == 0 else pl.ds(208, 192)
        return swap(9 + k, ref.at[0, where], ref.at[1, where])

    att_scale = ch ** (-0.5)

    def project(k):
        loads.qkv_w.wait()
        loads.proj_w.wait()
        value = nn(sc.F[k], sc.qkv_w[...])
        scaled = value[:, :ch] * att_scale
        sc.Q[k] = scaled.astype(BF)
        sc.K[k] = value[:KEYS, ch : 2 * ch].astype(BF)
        sc.V[k] = value[:KEYS, 2 * ch :].astype(BF)
        sc.MG[k] = nt(sc.GA[k], sc.proj_w[...]).astype(BF)


    def flat(ref):
        return ref[...].reshape(2 * ref.shape[1], ch)

    def scores():
        sc.S[...] = nt(flat(sc.K), flat(sc.Q))

    def prob_grads():
        sc.D[...] = nt(flat(sc.V), flat(sc.MG))

    def softmax(first, last):
        row = lax.broadcasted_iota(jnp.int32, (KEYS, 128), 0)
        real = row < tokens

        @pl.loop(first, last)
        def _(c):
            here = part(c * 128, 128)
            both = [pl.ds(0, KEYS), pl.ds(KEYS, KEYS)]
            value = [jnp.where(real, sc.S[keys, here], -1e30) for keys in both]
            most = jnp.max(jnp.maximum(value[0], value[1]), axis=0, keepdims=True)
            value = [jnp.exp(v - most) for v in value]
            scale = 1.0 / jnp.sum(value[0] + value[1], axis=0, keepdims=True)
            prob = [v * scale for v in value]
            for keys, v in zip(both, prob):
                sc.PR[keys, here] = v.astype(BF)
            back = [sc.D[keys, here] for keys in both]
            total = jnp.sum(prob[0] * back[0] + prob[1] * back[1], axis=0, keepdims=True)
            for keys, v, b in zip(both, prob, back):
                sc.DS[keys, here] = (v * (b - total)).astype(BF)

    def attend():
        mixed = tn(sc.PR[:, 0:512], flat(sc.V))[:KEYS].astype(BF)
        sc.MX[...] = mixed
        put_grad((0, 3 * ch), tn(mixed, sc.GA[0, :KEYS]))

    def attended():
        out = sc.F[0, :KEYS].astype(F32) + nn(sc.MX[...], sc.proj_w[...])
        sc.att[...] = out[:tokens].astype(BF)
        store(sc.att, outs.attended)

    def attention_back():
        pg = sc.PG
        pg[:, 0:ch] = (tn(sc.DS[:, 0:512], flat(sc.K))[:KEYS] * att_scale).astype(BF)
        pg[:, ch : 2 * ch] = nn(sc.DS[0:KEYS], flat(sc.Q)).astype(BF)
        pg[:, 2 * ch :] = nn(sc.PR[0:KEYS], flat(sc.MG)).astype(BF)

    def attention_grads():
        pg = sc.PG
        grad = tn(sc.F[0, :KEYS], pg[...])
        for i in range(3):
            put_grad((0, i * ch), grad[:, i * ch : (i + 1) * ch])

    def features_grad():
        pg = sc.PG
        out = sc.GA[0, :KEYS].astype(F32) + nt(pg[...], sc.qkv_w[...])
        sc.fg[...] = out[:tokens]
        store(sc.fg, outs.features_grad)

    groups = []
    for k, size in enumerate(cfg.groups):
        kept, inbox, extra, send, recv = sc.sums[k]
        groups.append(
            Total(
                size,
                cfg.plans[k],
                cfg.far,
                sc.own[k],
                kept,
                inbox,
                extra,
                sc.result[k],
                send,
                recv,
            )
        )

    def adv(*which):
        for k in which:
            if groups[k].count == 0:
                groups[k].start()
            elif groups[k].busy:
                groups[k].advance()
                if not groups[k].busy:
                    store(sc.result[k], vars(outs)["sum%d" % k])

    summed_grad_own()
    tokens_in()
    hidden_two_grad(near_pair)
    hidden_one()
    down_cot_more()
    hidden_one_halo(0)
    conv_one(near_pair)
    st.tok.append(send_tokens(sc.F, 1))
    film()
    project(0)
    conv_one(edge_pair)
    stats_two()
    send_next_row()
    st.tok.append(send_tokens(sc.GA, 3))
    st.tok.append(send_tokens(sc.F, 0))
    st.tok.append(send_tokens(sc.GA, 2))
    summed_grad_edge()
    skip_grad()
    hidden_two_grad(edge_pair)
    summed_grad_more()
    hidden_two_grad_halo()
    hidden_two()
    conv2_grad(0)
    adv(1)
    conv2_grad(2)
    adv(3)
    hidden_one_halo(1)
    adv(1)
    conv_one_halo()
    adv(3)
    hidden_two_halo()
    summed(near_pair)
    summed(edge_pair)
    adv(1)
    summed_swap()
    down_grad(0)
    adv(4)
    for copy in st.tok:
        copy.wait()
    project(1)
    down_grad(1)
    adv(5)
    scores()
    adv(4)
    adv(3)
    conv_one_grad()
    adv(5)
    adv(1)
    hidden_one_grad(near_pair)
    down_grad(2)
    adv(6)
    conv_one_grad_halo()
    conv1_grad()
    adv(7)
    adv(8)
    adv(4)
    adv(6)
    adv(3)
    hidden_one_grad(edge_pair)
    adv(7)
    adv(8)
    adv(5)
    prob_grads()
    softmax(0, 2)
    adv(4)
    adv(1)
    softmax(2, 4)
    adv(6)
    softmax(4, 6)
    softmax(6, 7)
    adv(3)
    attend()
    adv(8)
    adv(7)
    attention_back()
    adv(5)
    adv(4)
    attention_grads()
    adv(0)
    attended()
    adv(1)
    conv2_grad(1)
    adv(2)
    adv(6)
    adv(0)
    features_grad()
    adv(8)
    down(1)
    adv(2)
    adv(3)
    pre_one_grad(near_pair)
    adv(5)
    adv(7)
    pre_one_grad(edge_pair)
    stats_four()
    adv(3)
    skip_back()
    adv(1)
    adv(4)
    halo_summed()
    down(0)
    store(sc.block, outs.block_out)
    adv(6)
    adv(8)
    adv(0)
    adv(5)
    adv(7)
    adv(4)
    packet_begin()
    image_grad()
    adv(2)
    adv(6)
    packet_step()
    adv(1)
    adv(0)
    adv(7)
    adv(1)
    adv(8)
    adv(5)
    adv(8)
    adv(2)
    adv(6)
    adv(4)
    packet_step()
    adv(0)
    adv(4)
    adv(7)
    adv(2)
    packet_step()
    adv(5)
    adv(6)
    adv(5)
    adv(6)
    adv(7)
    adv(0)
    adv(7)
    adv(0)
    adv(2)
    packet_step()
    adv(2)

    while any(group.busy for group in groups):
        adv(*range(len(groups)))
    while pk_state[0] < len(cfg.bits):
        packet_step()
    store(sc.packet, outs.packet)
    for copy in stores + swaps:
        copy.wait()
    for copy in loading:
        copy.wait()


class Config:
    pass


def finish_kernel(cfg, *refs):
    n_in = len(cfg.finish_in)
    ins = Names(zip(cfg.finish_in, refs[:n_in]))
    n_out = len(cfg.finish_out)
    outs = Names(zip(cfg.finish_out, refs[n_in : n_in + n_out]))
    sc = Names(refs[n_in + n_out])
    ch, chi = cfg.ch, cfg.chi
    copies = []

    def begin(src, dst):
        copy = pltpu.make_async_copy(src, dst, sc.sem.at[len(copies)])
        copy.start()
        copies.append(copy)
        return copy

    small = [
        begin(ins.packet, sc.packet),
        begin(ins.norm2_gain, sc.norm2_gain),
        begin(ins.norm2_bias, sc.norm2_bias),
    ]
    order = cfg.done_order
    got = [begin(vars(ins)["sum%d" % k], sc.low[k]) for k in order]
    through = [
        begin(ins.image_grad, sc.image_grad),
        begin(ins.features_grad, sc.features_grad),
        begin(ins.block_out, sc.block_out),
        begin(ins.attended, sc.attended),
    ]
    passed = (
        (sc.image_grad, outs.image_grad),
        (sc.features_grad, outs.features_grad),
        (sc.block_out, outs.block_out),
        (sc.attended, outs.attended),
    )
    waits = []

    def packet_rows(k):
        return sc.packet[pl.ds(k, cfg.dp, stride=16), :]

    def wide_rows(k):
        return jnp.concatenate([packet_rows(k), packet_rows(k + 1)], axis=1)

    def total(value):
        return jnp.sum(value, axis=0, keepdims=True)

    def widen(low, wide, size):
        step = 256

        @pl.loop(0, size // step)
        def _(i):
            here = part(i * step, step)
            wide[here, 0:128] = low[0, here, :].astype(F32)
            wide[here, 128:256] = low[1, here, :].astype(F32)

    def places(k):
        if 1 <= k <= 3:
            for a in range(3):
                yield a * ch, ch, outs.conv2.at[pl.ds((3 * a + k - 1) * ch, ch)]
        elif k <= 6:
            yield 0, 3 * ch, outs.down.at[pl.ds((k - 4) * 3 * ch, 3 * ch)]
        elif k == 7:
            yield 0, 6 * chi, outs.conv1.at[pl.ds(0, 6 * chi)]
        else:
            yield 0, 3 * chi, outs.conv1.at[pl.ds(6 * chi, 3 * chi)]
            yield 3 * chi, chi, outs.skip

    def film():
        for copy in small:
            copy.wait()
        first, second = wide_rows(4), wide_rows(6)
        scale_grad = sc.norm2_gain[...] * second + sc.norm2_bias[...] * first
        rows = jnp.concatenate([scale_grad, first], axis=1)
        embed = jnp.concatenate([wide_rows(0), wide_rows(2)], axis=1)
        sc.film_w[...] = lax.dot_general(
            embed,
            rows,
            (((0,), (0,)), ((), ())),
            precision=lax.Precision.HIGHEST,
            preferred_element_type=F32,
        )
        sc.film_b[...] = total(rows)
        sc.gain2[...] = total(wide_rows(10))
        sc.bias2[...] = total(wide_rows(8))
        sc.gain1[...] = total(packet_rows(13))
        sc.bias1[...] = total(packet_rows(12))
        for src, dst in (
            (sc.film_w, outs.film_w),
            (sc.film_b, outs.film_b),
            (sc.gain2, outs.gain2),
            (sc.bias2, outs.bias2),
            (sc.gain1, outs.gain1),
            (sc.bias1, outs.bias1),
        ):
            waits.append(begin(src, dst))

    for turn, (k, copy) in enumerate(zip(order, got)):
        if turn == 6:
            film()
        copy.wait()
        if k == 0:
            for i in range(4):
                wide = sc.wide[0] if i < 3 else sc.wide_p
                at = i * ch if i < 3 else 0
                for j in range(2):
                    value = sc.low[0][j, i * ch : (i + 1) * ch, :].astype(F32)
                    wide[:, at + j * 128 : at + (j + 1) * 128] = value
            waits.append(begin(sc.wide[0], outs.qkv))
            waits.append(begin(sc.wide_p, outs.proj))
        else:
            widen(sc.low[k], sc.wide[k], cfg.groups[k])
            for start, size, dst in places(k):
                waits.append(begin(sc.wide[k].at[pl.ds(start, size)], dst))
    for (src, dst), copy in zip(passed, through):
        copy.wait()
        waits.append(begin(src, dst))
    for copy in waits:
        copy.wait()


def body(
    image_in,
    noise_in,
    sigma_in,
    embedding,
    features,
    norm1_gain,
    norm1_bias,
    conv1_w,
    film_w,
    film_b,
    norm2_gain,
    norm2_bias,
    conv2_w,
    skip_w,
    down_w,
    qkv_w,
    proj_w,
    down_cot,
    attn_cot,
):
    cfg = Config()
    cfg.rows, cfg.cols, cfg.chi = image_in.shape[1:]
    cfg.ch = conv1_w.shape[3]
    cfg.tokens = features.shape[1]
    cfg.dp = lax.axis_size("dp")
    cfg.bits = [2**k for k in range(cfg.dp.bit_length() - 1)]
    cfg.far = cfg.bits[4:]
    rows, cols, chi, ch, dp = cfg.rows, cfg.cols, cfg.chi, cfg.ch, cfg.dp
    half = cols // 2
    cfg.groups = [4 * ch] + [3 * ch] * 6 + [6 * chi, 4 * chi]
    cfg.plans = [
        [[1], ["rows", 2], [4, 8]],
        [[1], [2], [4], ["rows", 8]],
        [[1], ["rows", 2], [4, 8]],
        [[1], ["rows", 2], [4, 8]],
        [[1], [2], [4], [8, "rows"]],
        [[1], ["rows"], [2], [4, 8]],
        [[1], [2], ["rows", 4], [8]],
        [[1], [4], ["rows", 2], [8]],
        [[1], ["rows", 2], [4, 8]],
    ]
    cfg.done_order = (3, 1, 8, 4, 5, 6, 7, 0, 2)
    args = dict(
        sigma_in=sigma_in,
        image_in=image_in[0],
        noise_in=noise_in[0],
        norm1_gain=norm1_gain.reshape(1, chi),
        norm1_bias=norm1_bias.reshape(1, chi),
        down_cot=down_cot[0],
        down_w=down_w.reshape(3, 3 * ch, ch),
        conv1_w=conv1_w.reshape(3, 3 * chi, ch),
        conv2_w=conv2_w.reshape(3, 3 * ch, ch),
        skip_w=skip_w,
        features=features[0],
        attn_cot=attn_cot[0],
        embedding=embedding,
        film_w=film_w,
        film_b=film_b.reshape(1, 2 * ch),
        norm2_gain=norm2_gain.reshape(1, ch),
        norm2_bias=norm2_bias.reshape(1, ch),
        qkv_w=qkv_w,
        proj_w=proj_w,
    )
    cfg.inputs = tuple(args)
    shape = jax.ShapeDtypeStruct
    out_shapes = dict(
        block_out=shape((2, half, ch), BF),
        attended=shape((cfg.tokens, ch), BF),
        image_grad=shape((rows, cols, chi), F32),
        features_grad=shape((cfg.tokens, ch), F32),
        packet=shape((dp, 16, 128), F32),
    )
    for k, size in enumerate(cfg.groups):
        out_shapes["sum%d" % k] = shape((2, size, 128), BF)
    cfg.outputs = tuple(out_shapes)
    vm = pltpu.VMEM
    scratch = {
        name: vm(value.shape, value.dtype)
        for name, value in args.items()
        if value is not sigma_in and value is not args["down_cot"]
    }
    scratch.update(
        dc=vm((5, half, ch), BF),
        xh=vm((2, cols, chi), BF),
        xs=vm((rows, cols, chi), F32),
        stage_i=vm((chi // 128, cols + 16, 128), F32),
        stage_o=vm((chi // 128, cols + 16, 128), F32),
        stage_c=vm((ch // 128, cols + 16, 128), F32),
        stage_h=vm((ch // 128, half + 16, 128), F32),
        h1c=vm((rows + 4, cols, 3 * chi), BF),
        h2c=vm((rows + 2, cols, 3 * ch), BF),
        sg3=vm((rows + 4, cols, 3 * ch), BF),
        cg=vm((rows + 2, cols, ch), BF),
        s3=vm((rows + 1, half, 3 * ch), BF),
        c1=vm((rows + 1, cols, ch), F32),
        g2=vm((rows + 1, cols, ch), F32),
        h1g=vm((rows, cols, chi), F32),
        skb=vm((rows, cols, chi), F32),
        block=vm((2, half, ch), BF),
        st_out=vm((4, 8, ch), F32),
        st_in=vm((4, 8, ch), F32),
        packet=vm((dp, 16, 128), F32),
        F=vm((2, TOKENS, ch), BF),
        GA=vm((2, TOKENS, ch), BF),
        Q=vm((2, TOKENS, ch), BF),
        K=vm((2, KEYS, ch), BF),
        V=vm((2, KEYS, ch), BF),
        MG=vm((2, TOKENS, ch), BF),
        S=vm((2 * KEYS, 2 * TOKENS), F32),
        D=vm((2 * KEYS, 2 * TOKENS), F32),
        PR=vm((2 * KEYS, 2 * TOKENS), BF),
        DS=vm((2 * KEYS, 2 * TOKENS), BF),
        PG=vm((KEYS, 3 * ch), BF),
        MX=vm((KEYS, ch), BF),
        att=vm((cfg.tokens, ch), BF),
        fg=vm((cfg.tokens, ch), F32),
        own=[vm((2, size, 128), BF) for size in cfg.groups],
        result=[vm((2, size, 128), BF) for size in cfg.groups],
        sums=[total_scratch(*plan, cfg.far) for plan in zip(cfg.groups, cfg.plans)],
        load_sem=pltpu.SemaphoreType.DMA((len(args),)),
        store_sem=pltpu.SemaphoreType.DMA((len(out_shapes),)),
        x_send=pltpu.SemaphoreType.DMA((13,)),
        x_recv=pltpu.SemaphoreType.DMA((13,)),
        pk_send=pltpu.SemaphoreType.DMA((len(cfg.bits),)),
        pk_recv=pltpu.SemaphoreType.DMA((len(cfg.bits),)),
    )
    made = pl.pallas_call(
        functools.partial(level_kernel, cfg),
        out_shape=list(out_shapes.values()),
        in_specs=[SMEM] + [ANY] * (len(args) - 1),
        out_specs=[ANY] * len(out_shapes),
        scratch_shapes=[scratch],
        compiler_params=pltpu.CompilerParams(
            collective_id=0, has_side_effects=True, vmem_limit_bytes=62 * 2**20
        ),
        name="level",
    )(*args.values())
    made = dict(zip(cfg.outputs, made))

    small = dict(
        packet=made["packet"].reshape(dp * 16, 128),
        norm2_gain=args["norm2_gain"],
        norm2_bias=args["norm2_bias"],
    )
    big = {name: value for name, value in made.items() if name not in small}
    cfg.finish_in = tuple(small) + tuple(big)
    finals = dict(
        block_out=out_shapes["block_out"],
        attended=out_shapes["attended"],
        image_grad=out_shapes["image_grad"],
        features_grad=out_shapes["features_grad"],
        conv1=shape((9 * chi, ch), F32),
        conv2=shape((9 * ch, ch), F32),
        skip=shape((chi, ch), F32),
        down=shape((9 * ch, ch), F32),
        qkv=shape((ch, 3 * ch), F32),
        proj=shape((ch, ch), F32),
    )
    finals.update(
        gain1=shape((1, chi), F32),
        bias1=shape((1, chi), F32),
        film_w=shape((2 * ch, 2 * ch), F32),
        film_b=shape((1, 2 * ch), F32),
        gain2=shape((1, ch), F32),
        bias2=shape((1, ch), F32),
    )
    cfg.finish_out = tuple(finals)
    finish_scratch = dict(
        low=[vm((2, size, 128), BF) for size in cfg.groups],
        wide=[vm((ch, 3 * ch), F32)] + [vm((size, ch), F32) for size in cfg.groups[1:]],
        wide_p=vm((ch, ch), F32),
        image_grad=vm((rows, cols, chi), F32),
        features_grad=vm((cfg.tokens, ch), F32),
        block_out=vm((2, half, ch), BF),
        attended=vm((cfg.tokens, ch), BF),
        packet=vm((dp * 16, 128), F32),
        norm2_gain=vm((1, ch), F32),
        norm2_bias=vm((1, ch), F32),
        gain1=vm((1, chi), F32),
        bias1=vm((1, chi), F32),
        film_w=vm((2 * ch, 2 * ch), F32),
        film_b=vm((1, 2 * ch), F32),
        gain2=vm((1, ch), F32),
        bias2=vm((1, ch), F32),
        sem=pltpu.SemaphoreType.DMA((48,)),
    )
    done = pl.pallas_call(
        functools.partial(finish_kernel, cfg),
        out_shape=list(finals.values()),
        in_specs=[ANY] * len(cfg.finish_in),
        out_specs=[ANY] * len(finals),
        scratch_shapes=[finish_scratch],
        compiler_params=pltpu.CompilerParams(vmem_limit_bytes=56 * 2**20),
        name="finish",
    )(*small.values(), *big.values())
    done = Names(zip(cfg.finish_out, done))
    return (
        done.block_out[None],
        done.attended[None],
        done.image_grad[None],
        done.features_grad[None],
        done.gain1.reshape(chi),
        done.bias1.reshape(chi),
        done.conv1.reshape(conv1_w.shape),
        done.film_w,
        done.film_b.reshape(2 * ch),
        done.gain2.reshape(ch),
        done.bias2.reshape(ch),
        done.conv2.reshape(conv2_w.shape),
        done.skip,
        done.down.reshape(down_w.shape),
        done.qkv,
        done.proj,
    )


def solution(mesh):
    placed = (
        P("dp", "rows", None, None),
        P("dp", "rows", None, None),
        P("dp"),
        P("dp", None),
        P("dp", "rows", None),
        P(),
        P(),
        P(),
        P(),
        P(),
        P(),
        P(),
        P(),
        P(),
        P(),
        P(),
        P(),
        P("dp", "rows", None, None),
        P("dp", "rows", None),
    )
    return jax.shard_map(
        body,
        mesh=mesh,
        in_specs=placed,
        out_specs=(
            P("dp", "rows", None, None),
            P("dp", "rows", None),
            P("dp", "rows", None, None),
            P("dp", "rows", None),
            P(),
            P(),
            P(),
            P(),
            P(),
            P(),
            P(),
            P(),
            P(),
            P(),
            P(),
            P(),
        ),
        check_vma=False,
    )
```
